32 devices in a mesh: dp: 32 (over z, y, x, core).
Axes of the slice: x: 2, y: 2, z: 4, core: 2. Of those that a mesh axis runs over, the one named last changes fastest.
Arguments:
- tokens: bfloat16 [32768, 512], P('dp'), may hold values from -6 to 6
- cotangent: bfloat16 [32768, 512], P('dp'), may hold values from -6 to 6
- patches: bfloat16 [256, 256, 1664], P('dp'), may hold values from -6 to 6
- lengths: int32 [256], P('dp'), may hold values from 8 to 128
- group_member: int32 [32], replicated, may hold values from 0 to 1, as said below
- mix: float32 [2], replicated, may hold values from 0.3 to 3
- gain_one: float32 [512], replicated, may hold values from 0.5 to 1.5
- w_query: bfloat16 [512, 384], replicated, may hold values from -0.25 to 0.25
- w_key: bfloat16 [512, 384], replicated, may hold values from -0.25 to 0.25
- w_value: bfloat16 [512, 384], replicated, may hold values from -0.25 to 0.25
- w_out: bfloat16 [384, 512], replicated, may hold values from -1.25 to 1.25
- gain_two: float32 [512], replicated, may hold values from 0.5 to 1.5
- w_patch: bfloat16 [1664, 512], replicated, may hold values from -0.15625 to 0.15625
- bias_patch: float32 [512], replicated, may hold values from -3 to 3
- w_cross_query: bfloat16 [512, 384], replicated, may hold values from -0.25 to 0.25
- w_cross_key: bfloat16 [512, 384], replicated, may hold values from -0.25 to 0.25
- w_cross_value: bfloat16 [512, 384], replicated, may hold values from -0.25 to 0.25
- w_cross_out: bfloat16 [384, 512], replicated, may hold values from -2.5 to 2.5
- gain_three: float32 [512], replicated, may hold values from 0.5 to 1.5
- w_gate: bfloat16 [512, 1024], replicated, may hold values from -0.25 to 0.25
- w_up: bfloat16 [512, 1024], replicated, may hold values from -0.25 to 0.25
- w_down: bfloat16 [1024, 512], replicated, may hold values from -0.1875 to 0.1875
Outputs:
- mixed_out: bfloat16 [32768, 512], P('dp')
- grad_tokens: float32 [32768, 512], P('dp')
- grad_patches: float32 [256, 256, 1664], P('dp')
- grad_gain_one: float32 [512], replicated
- grad_w_query: float32 [512, 384], replicated
- grad_w_key: float32 [512, 384], replicated
- grad_w_value: float32 [512, 384], replicated
- grad_w_out: float32 [384, 512], replicated
- grad_gain_two: float32 [512], replicated
- grad_w_patch: float32 [1664, 512], replicated
- grad_bias_patch: float32 [512], replicated
- grad_w_cross_query: float32 [512, 384], replicated
- grad_w_cross_key: float32 [512, 384], replicated
- grad_w_cross_value: float32 [512, 384], replicated
- grad_w_cross_out: float32 [384, 512], replicated
- grad_gain_three: float32 [512], replicated
- grad_w_gate: float32 [512, 1024], replicated
- grad_w_up: float32 [512, 1024], replicated
- grad_w_down: float32 [1024, 512], replicated
The draws below stay inside these ranges and needn't reach their ends.
Inputs may be any that keep to these rules, and one draw needn't show every extreme that they name: `group_member`: between 4 and 16 devices, anywhere on the axis, hold 1 and form the robot trajectory group; the others form the web question answering group.
All inputs are finite; a program needn't handle non-finite values.
Results may differ from the reference program's by a relative error of at most 0.02.
The reference program's roundings to bfloat16 on the way count: a program that leaves them out, or rounds other values in their place, can miss the bound.
Values sent between devices are 32-bit elements; how exact they have to be, the bound alone decides.
No kernel may reach another device: no remote copies, remote signals or barrier semaphores. Data moves between devices by JAX's collectives and lax.ppermute only.
A program may use at most 192 MiB of HBM per device.

```python
import math
import jax
import jax.numpy as jnp
from jax import lax

D = 512
FF = 1024
HEADS = 6
HEAD_DIM = 64
INNER = 384
PATCHES = 256
PATCH_DIM = 1664
MAXLEN = 128
MINLEN = 8
SEQS_DEV = 8
SEQS = 256
TOK_DEV = 1024
TOKENS = 32768
N_DP = 32


def draw_group_member(key, part):
    key = jax.random.fold_in(key, 11)
    size_key, order_key = jax.random.split(key)
    member_count = jax.random.randint(size_key, (), N_DP // 8, N_DP // 2 + 1)
    order = jax.random.permutation(order_key, N_DP)
    return (order < member_count).astype(jnp.int32)


def place_ends(entries, own_key, least, top_value):
    shape = entries.shape
    place = [jax.random.randint(jax.random.fold_in(own_key, axis), (), 0, shape[axis]) for axis in range(len(shape))]
    entries = entries.at[tuple(place)].set(least)
    longest = shape.index(max(shape))
    place[longest] = (place[longest] + 1) % shape[longest]
    return entries.at[tuple(place)].set(top_value)


def shard_levels(rng, extent, pieces, low, high):
    level, own = 1.0, jax.random.fold_in(rng, 6)
    for dim, parts in pieces:
        steps = jnp.exp(jax.random.uniform(jax.random.fold_in(own, dim), (parts,), jnp.float32, low / len(pieces), high / len(pieces)))
        level = level * jnp.repeat(steps, extent[dim] // parts).reshape([-1 if axis == dim else 1 for axis in range(len(extent))])
    return level


def noise(stream_key, shape, spread, limit, pieces=(), kind=jnp.bfloat16):
    level = shard_levels(stream_key, shape, pieces, -0.22, 0.18) if pieces else 1.0
    entries = jax.random.normal(stream_key, shape, jnp.float32) * spread * level
    return jnp.minimum(jnp.maximum(entries, -limit), limit).astype(kind)


def setup_inputs(seed: int = 0) -> dict:
    keys = jax.random.split(jax.random.key(seed), 23)
    return {
        "tokens": noise(keys[0], (TOKENS, D), 1.0, 6.0, ((0, 32),)),
        "cotangent": noise(keys[1], (TOKENS, D), 1.0, 6.0, ((0, 32),)),
        "patches": noise(keys[2], (SEQS, PATCHES, PATCH_DIM), 1.0, 6.0, ((0, 32),)),
        "lengths": place_ends(jax.random.randint(keys[3], (SEQS,), MINLEN, MAXLEN + 1), jax.random.fold_in(keys[3], 1), MINLEN, MAXLEN).astype(jnp.int32),
        "group_member": draw_group_member(jax.random.fold_in(keys[22], 71), 0),
        "mix": jnp.clip(jnp.exp(jax.random.uniform(keys[5], (2,), jnp.float32, math.log(0.3), math.log(3.0))), 0.3, 3.0),
        "gain_one": jnp.clip(1.0 + 0.1 * jax.random.normal(keys[6], (D,), jnp.float32), 0.5, 1.5),
        "w_query": noise(keys[7], (D, INNER), D ** -0.5, 0.25),
        "w_key": noise(keys[8], (D, INNER), D ** -0.5, 0.25),
        "w_value": noise(keys[9], (D, INNER), D ** -0.5, 0.25),
        "w_out": noise(keys[10], (INNER, D), (max(INNER // 16, 1)) ** -0.5, 1.25),
        "gain_two": jnp.clip(1.0 + 0.1 * jax.random.normal(keys[11], (D,), jnp.float32), 0.5, 1.5),
        "w_patch": noise(keys[12], (PATCH_DIM, D), PATCH_DIM ** -0.5, 0.15625),
        "bias_patch": noise(keys[13], (D,), 0.5, 3.0, (), jnp.float32),
        "w_cross_query": noise(keys[14], (D, INNER), D ** -0.5, 0.25),
        "w_cross_key": noise(keys[15], (D, INNER), D ** -0.5, 0.25),
        "w_cross_value": noise(keys[16], (D, INNER), D ** -0.5, 0.25),
        "w_cross_out": noise(keys[17], (INNER, D), (max(INNER // 64, 1)) ** -0.5, 2.5),
        "gain_three": jnp.clip(1.0 + 0.1 * jax.random.normal(keys[18], (D,), jnp.float32), 0.5, 1.5),
        "w_gate": noise(keys[19], (D, FF), D ** -0.5, 0.25),
        "w_up": noise(keys[20], (D, FF), D ** -0.5, 0.25),
        "w_down": noise(keys[21], (FF, D), FF ** -0.5, 0.1875),
    }


@jax.custom_vjp
def low(v):
    return lax.optimization_barrier(v.astype(jnp.bfloat16)).astype(jnp.float32)

@jax.custom_vjp
def low_back(v):
    return v

def low_keep(v):
    return (low(v), None)

def low_pass(kept, grad):
    return (grad,)

def back_keep(v):
    return (v, None)

def back_low(kept, grad):
    return (low(grad),)
low.defvjp(low_keep, low_pass)
low_back.defvjp(back_keep, back_low)
epsilon = 1e-06

def matmul(left_op, right_op):
    return jnp.dot(left_op, right_op, precision=lax.Precision.HIGHEST)

def contract(einsum_form, left_op, right_op):
    return jnp.einsum(einsum_form, left_op, right_op, precision=lax.Precision.HIGHEST)

def norm_scale(values, gain):
    return values * lax.rsqrt(lax.optimization_barrier(jnp.mean(values * values, axis=-1, keepdims=True)) + epsilon) * gain

def split_heads(values, seq_count, length):
    return values.reshape(seq_count, length, HEADS, HEAD_DIM)

def attend(queries, key_rows, value_rows, allowed):
    scores = low_back(contract('sqhe,skhe->shqk', queries, key_rows) * (1.0 / math.sqrt(HEAD_DIM)))
    scores = jnp.where(allowed, scores, -1000000000.0)
    chances = low(jax.nn.softmax(scores, axis=-1))
    return contract('shqk,skhe->sqhe', chances, value_rows)

def forward(params, row_data, pictures, seq_lengths):
    gain_one, w_query, w_key, w_value, w_out, gain_two, w_patch, bias_patch, w_cross_query, w_cross_key, w_cross_value, w_cross_out, gain_three, w_gate, w_up, w_down = params
    seq_count = seq_lengths.shape[0]
    position = jnp.arange(MAXLEN, dtype=jnp.int32)
    causal = position[None, :] <= position[:, None]
    allowed = causal[None, None] & (position[None, None, None, :] < seq_lengths[:, None, None, None])
    normed_one = low(norm_scale(row_data, gain_one))
    queries = split_heads(low(low_back(matmul(normed_one, w_query))), seq_count, MAXLEN)
    key_rows = split_heads(low(low_back(matmul(normed_one, w_key))), seq_count, MAXLEN)
    value_rows = split_heads(low(low_back(matmul(normed_one, w_value))), seq_count, MAXLEN)
    attended = low(low_back(attend(queries, key_rows, value_rows, allowed).reshape(seq_count * MAXLEN, INNER)))
    stream_one = row_data + low_back(matmul(attended, w_out))
    normed_two = low(norm_scale(stream_one, gain_two))
    cross_queries = split_heads(low(low_back(matmul(normed_two, w_cross_query))), seq_count, MAXLEN)
    features = low(low_back(matmul(pictures.reshape(seq_count * PATCHES, PATCH_DIM), w_patch) + bias_patch))
    cross_keys = split_heads(low(low_back(matmul(features, w_cross_key))), seq_count, PATCHES)
    cross_values = split_heads(low(low_back(matmul(features, w_cross_value))), seq_count, PATCHES)
    everywhere = jnp.ones((1, 1, 1, 1), dtype=jnp.bool_)
    cross_attended = low(low_back(attend(cross_queries, cross_keys, cross_values, everywhere).reshape(seq_count * MAXLEN, INNER)))
    stream_two = stream_one + low_back(matmul(cross_attended, w_cross_out))
    normed_three = low(norm_scale(stream_two, gain_three))
    gate_pre = low_back(matmul(normed_three, w_gate))
    up_proj = low_back(matmul(normed_three, w_up))
    hidden = low(jax.nn.gelu(gate_pre, approximate=True) * up_proj)
    return stream_two + low_back(matmul(hidden, w_down))

def reference(tokens, cotangent, patches, lengths, group_member, mix, gain_one, w_query, w_key, w_value, w_out, gain_two, w_patch, bias_patch, w_cross_query, w_cross_key, w_cross_value, w_cross_out, gain_three, w_gate, w_up, w_down):
    params = tuple((entry.astype(jnp.float32) for entry in (gain_one, w_query, w_key, w_value, w_out, gain_two, w_patch, bias_patch, w_cross_query, w_cross_key, w_cross_value, w_cross_out, gain_three, w_gate, w_up, w_down)))
    dev_first = group_member == 1
    seq_first = jnp.repeat(dev_first, SEQS_DEV)
    seq_len = lengths.astype(jnp.float32)
    count_first = jnp.sum(jnp.where(seq_first, seq_len, 0.0))
    count_second = jnp.sum(jnp.where(seq_first, 0.0, seq_len))
    summed = count_first + count_second
    weight_first = mix[0] * summed / count_first
    weight_second = mix[1] * summed / count_second
    dev_weight = jnp.where(dev_first, weight_first, weight_second)

    def scan_step(carried, block_data):
        row_data, cot_rows, pictures, seq_lengths, weight = block_data

        def local_forward(param_all, rows_all, pics_all):
            return forward(param_all, rows_all, pics_all, seq_lengths)
        out_rows, pullback = jax.vjp(local_forward, params, row_data.astype(jnp.float32), pictures.astype(jnp.float32))
        position = jnp.arange(MAXLEN, dtype=jnp.int32)
        is_valid = (position[None, :] < seq_lengths[:, None]).reshape(-1).astype(jnp.float32)
        grad_params, grad_rows, grad_pics = pullback(cot_rows.astype(jnp.float32) * is_valid[:, None])
        carried = tuple((acc + weight * grad for acc, grad in zip(carried, grad_params)))
        return (carried, (out_rows.astype(jnp.bfloat16), weight * grad_rows, weight * grad_pics))
    start = tuple((jnp.zeros(entry.shape, jnp.float32) for entry in params))
    blocks = (tokens.reshape(N_DP, TOK_DEV, D), cotangent.reshape(N_DP, TOK_DEV, D), patches.reshape(N_DP, SEQS_DEV, PATCHES, PATCH_DIM), lengths.reshape(N_DP, SEQS_DEV), dev_weight)
    merged, (outputs, grad_tok, grad_pic) = lax.scan(scan_step, start, blocks)
    return (outputs.reshape(TOKENS, D), grad_tok.reshape(TOKENS, D), grad_pic.reshape(SEQS, PATCHES, PATCH_DIM), merged[0], merged[1], merged[2], merged[3], merged[4], merged[5], merged[6], merged[7], merged[8], merged[9], merged[10], merged[11], merged[12], merged[13], merged[14], merged[15])
```

```python
import functools
import math

import jax
import jax.numpy as jnp
from jax import lax
from jax.experimental import pallas as pl
from jax.experimental.pallas import tpu as pltpu
from jax.sharding import PartitionSpec as P

HEADS = 6
HEAD_DIM = 64


epsilon = 1e-06


def norm_scale(values, gain):
    return values * lax.rsqrt(jnp.mean(values * values, axis=-1, keepdims=True) + epsilon) * gain


def dot_plain(left_op, right_op):
    return jnp.dot(left_op, right_op, preferred_element_type=jnp.float32)


def dot_rows(left_op, right_op):
    return lax.dot_general(
        left_op, right_op, (((0,), (0,)), ((), ())), preferred_element_type=jnp.float32
    )


def dot_back(left_op, right_op):
    return lax.dot_general(
        left_op, right_op, (((1,), (1,)), ((), ())), preferred_element_type=jnp.float32
    )


def split_heads(values, seq_count, length):
    return values.reshape(seq_count, length, HEADS, HEAD_DIM)


def scores_of(queries, key_rows, allowed):
    raw_scores = jnp.einsum(
        "sqhe,skhe->shqk", queries, key_rows, preferred_element_type=jnp.float32
    )
    return jnp.where(allowed, raw_scores * (1.0 / math.sqrt(HEAD_DIM)), -1000000000.0)


def attend_forward(queries, key_rows, value_rows, allowed):
    scores = scores_of(queries, key_rows, allowed)
    highest = jnp.max(scores, axis=-1, keepdims=True)
    expo_rows = jnp.exp(scores - highest)
    summed = jnp.sum(expo_rows, axis=-1, keepdims=True)
    chances = (expo_rows / summed).astype(jnp.bfloat16)
    attended = jnp.einsum(
        "shqk,skhe->sqhe", chances, value_rows, preferred_element_type=jnp.float32
    )
    return (attended.astype(jnp.bfloat16), highest + jnp.log(summed))


def attend_backward(queries, key_rows, value_rows, allowed, logsum, grad_mixed):
    scaling = 1.0 / math.sqrt(HEAD_DIM)
    chances = jnp.exp(scores_of(queries, key_rows, allowed) - logsum)
    grad_chances = jnp.einsum(
        "sqhe,skhe->shqk", grad_mixed, value_rows, preferred_element_type=jnp.float32
    )
    grad_values = jnp.einsum(
        "shqk,sqhe->skhe",
        chances.astype(jnp.bfloat16),
        grad_mixed,
        preferred_element_type=jnp.float32,
    )
    inner_sum = jnp.sum(chances * grad_chances, axis=-1, keepdims=True)
    grad_scores = (chances * (grad_chances - inner_sum)).astype(jnp.bfloat16)
    grad_queries = (
        jnp.einsum("shqk,skhe->sqhe", grad_scores, key_rows, preferred_element_type=jnp.float32)
        * scaling
    )
    grad_keys = (
        jnp.einsum("shqk,sqhe->skhe", grad_scores, queries, preferred_element_type=jnp.float32)
        * scaling
    )
    return (
        grad_queries.astype(jnp.bfloat16),
        grad_keys.astype(jnp.bfloat16),
        grad_values.astype(jnp.bfloat16),
    )


def gated_unit(gate_pre, up_proj):
    return jax.nn.gelu(gate_pre, approximate=True) * up_proj


BLOCKS = 32
HALF = 16


def flips(count, first, second):
    return [(i, i ^ (first if i % 2 == 0 else second)) for i in range(count)]


def code_pair(me):
    core, ex, why = me & 1, (me >> 1) & 1, (me >> 2) & 1
    low = (me >> 3) & 3
    low = ((low & 1) << 1) | (low >> 1)
    first = jnp.where(core == 0, ex, why)
    second = jnp.where(core == 0, why, ex)
    own = core * 16 + first * 8 + second * 4 + low
    other = (1 - core) * 16 + second * 8 + first * 4 + low
    return own, other


def exchange(values, first, second=None):
    count = lax.axis_size("dp")
    return lax.ppermute(values, "dp", flips(count, first, first if second is None else second))


def block_rows(shape):
    return shape[0] * shape[1] // (BLOCKS * 128)


def block_parts(shape, index):
    rows, lanes = shape
    tiles = lanes // 128
    if BLOCKS % tiles:
        height = rows // BLOCKS
        return [
            (pl.ds(pl.multiple_of(index * height, 8), height), pl.ds(t * 128, 128))
            for t in range(tiles)
        ]
    height = rows * tiles // BLOCKS
    row, lane = index // tiles, index % tiles
    return [
        (
            pl.ds(pl.multiple_of(row * height, 8), height),
            pl.ds(pl.multiple_of(lane * 128, 128), 128),
        )
    ]


def pack_block(shapes, refs, index, scale, out_ref, slot):
    start = 0
    for shape, ref in zip(shapes, refs):
        for rows, lanes in block_parts(shape, index):
            out_ref[slot, pl.ds(start, rows.size), :] = ref[rows, lanes] * scale
            start += rows.size


def pack_kernel(shapes, code_ref, weight_ref, *refs):
    ins, (keep_ref, send_ref) = refs[: len(shapes)], refs[len(shapes) :]
    scale = weight_ref[0]

    def step(p, carry):
        pack_block(shapes, ins, p ^ code_ref[0], scale, keep_ref, p)
        pack_block(shapes, ins, p ^ code_ref[1], scale, send_ref, p)
        return carry

    lax.fori_loop(0, HALF, step, 0)


def unpack_kernel(shapes, code_ref, *refs):
    ins, outs = refs[:4], refs[4:]
    for k, piece in enumerate(ins):

        def step(p, carry):
            index = (p + 8 * (k % 2)) ^ code_ref[k // 2]
            start = 0
            for shape, out_ref in zip(shapes, outs):
                for rows, lanes in block_parts(shape, index):
                    out_ref[rows, lanes] = piece[p, pl.ds(start, rows.size), :]
                    start += rows.size
            return carry

        lax.fori_loop(0, 8, step, 0)


VMEM = pltpu.VMEM
SMEM = pltpu.SMEM


def pack(grads, codes, weight):
    shapes = [g.shape for g in grads]
    rows = sum(block_rows(s) for s in shapes)
    out = jax.ShapeDtypeStruct((HALF, rows, 128), jnp.float32)
    return pl.pallas_call(
        functools.partial(pack_kernel, shapes),
        out_shape=(out, out),
        in_specs=[pl.BlockSpec(memory_space=SMEM)] * 2
        + [pl.BlockSpec(memory_space=VMEM)] * len(grads),
        out_specs=[pl.BlockSpec(memory_space=VMEM)] * 2,
        compiler_params=pltpu.CompilerParams(vmem_limit_bytes=40 * 2**20),
        name="pack",
    )(codes, weight, *grads)


def unpack(pieces, shapes, codes):
    return pl.pallas_call(
        functools.partial(unpack_kernel, shapes),
        out_shape=[jax.ShapeDtypeStruct(s, jnp.float32) for s in shapes],
        in_specs=[pl.BlockSpec(memory_space=SMEM)] + [pl.BlockSpec(memory_space=VMEM)] * 4,
        out_specs=[pl.BlockSpec(memory_space=VMEM)] * len(shapes),
        compiler_params=pltpu.CompilerParams(vmem_limit_bytes=40 * 2**20),
        name="unpack",
    )(codes, *pieces)


def sum_blocks(keep, send):
    got = exchange(send, 1)
    for first, second in ((2, 4), (4, 2), (8, 8), (16, 16)):
        half = keep.shape[0] // 2
        send, keep = keep[half:] + got[half:], keep[:half] + got[:half]
        got = exchange(send, first, second)
    keep = keep + got
    extra = BLOCKS
    while extra < lax.axis_size("dp"):
        keep = keep + exchange(keep, extra)
        extra *= 2
    return keep


def spread_blocks(held):
    held = jnp.concatenate([held, exchange(held, 16)])
    held = jnp.concatenate([held, exchange(held, 8)])
    held = jnp.concatenate([held, exchange(held, 4, 2)])
    near = exchange(held, 1)
    rest = exchange(held, 2, 4)
    far = exchange(rest, 1)
    return held, rest, near, far


def merge(grads, codes, weight):
    keep, send = pack(grads, codes, weight)
    return unpack(spread_blocks(sum_blocks(keep, send)), [g.shape for g in grads], codes)


def local(
    tokens,
    cotangent,
    patches,
    lengths,
    group_member,
    mix,
    gain_one,
    w_query,
    w_key,
    w_value,
    w_out,
    gain_two,
    w_patch,
    bias_patch,
    w_cross_query,
    w_cross_key,
    w_cross_value,
    w_cross_out,
    gain_three,
    w_gate,
    w_up,
    w_down,
):
    seq_count = lengths.shape[0]
    maxlen = tokens.shape[0] // seq_count
    patch_rows = patches.shape[1]
    row_count = seq_count * maxlen
    stream = tokens.astype(jnp.float32)
    own_member = lax.dynamic_index_in_dim(group_member, lax.axis_index("dp"), 0, keepdims=False)
    in_first = own_member == 1
    group_slots = jnp.where(
        in_first, jnp.array([1.0, 0.0], jnp.float32), jnp.array([0.0, 1.0], jnp.float32)
    )
    own_count = jnp.sum(lengths).astype(jnp.float32)
    counts = own_count * group_slots
    bit = 1
    while bit < lax.axis_size("dp"):
        counts = counts + exchange(counts, bit)
        bit *= 2
    group_weights = mix * jnp.sum(counts) / counts
    weight_own = jnp.sum(group_slots * group_weights)
    weight_ref = weight_own[None]
    codes = jnp.stack(code_pair(lax.axis_index("dp")))
    position = jnp.arange(maxlen, dtype=jnp.int32)
    is_valid = position[None, :] < lengths[:, None]
    causal = position[None, :] <= position[:, None]
    allowed = causal[None, None] & is_valid[:, None, None, :]
    everywhere = jnp.ones((1, 1, 1, 1), dtype=jnp.bool_)
    normed_one = norm_scale(stream, gain_one).astype(jnp.bfloat16)
    queries = split_heads(dot_plain(normed_one, w_query).astype(jnp.bfloat16), seq_count, maxlen)
    key_rows = split_heads(dot_plain(normed_one, w_key).astype(jnp.bfloat16), seq_count, maxlen)
    value_rows = split_heads(dot_plain(normed_one, w_value).astype(jnp.bfloat16), seq_count, maxlen)
    attended, logsum = attend_forward(queries, key_rows, value_rows, allowed)
    attn_rows = attended.reshape(row_count, -1)
    stream_one = stream + dot_plain(attn_rows, w_out)
    normed_two = norm_scale(stream_one, gain_two).astype(jnp.bfloat16)
    cross_queries = split_heads(
        dot_plain(normed_two, w_cross_query).astype(jnp.bfloat16), seq_count, maxlen
    )
    flat_patches = patches.reshape(seq_count * patch_rows, -1)
    features = (dot_plain(flat_patches, w_patch) + bias_patch).astype(jnp.bfloat16)
    cross_keys = split_heads(
        dot_plain(features, w_cross_key).astype(jnp.bfloat16), seq_count, patch_rows
    )
    cross_values = split_heads(
        dot_plain(features, w_cross_value).astype(jnp.bfloat16), seq_count, patch_rows
    )
    cross_attended, cross_logsum = attend_forward(
        cross_queries, cross_keys, cross_values, everywhere
    )
    cross_rows = cross_attended.reshape(row_count, -1)
    stream_two = stream_one + dot_plain(cross_rows, w_cross_out)
    normed_three = norm_scale(stream_two, gain_three).astype(jnp.bfloat16)
    gate_pre = dot_plain(normed_three, w_gate)
    up_proj = dot_plain(normed_three, w_up)
    hidden = gated_unit(gate_pre, up_proj).astype(jnp.bfloat16)
    result = (stream_two + dot_plain(hidden, w_down)).astype(jnp.bfloat16)
    keep_rows = is_valid.reshape(-1).astype(jnp.float32)[:, None]
    grad_stream = cotangent.astype(jnp.float32) * keep_rows
    grad_down_in = grad_stream.astype(jnp.bfloat16)
    grad_w_down = dot_rows(hidden, grad_down_in)
    grad_hidden = dot_back(grad_down_in, w_down)
    unused_gated, gated_pull = jax.vjp(gated_unit, gate_pre, up_proj)
    grad_gate_raw, grad_up_raw = gated_pull(grad_hidden)
    grad_gate = grad_gate_raw.astype(jnp.bfloat16)
    grad_up = grad_up_raw.astype(jnp.bfloat16)
    grad_w_gate = dot_rows(normed_three, grad_gate)
    grad_w_up = dot_rows(normed_three, grad_up)
    grad_normed_three = dot_back(grad_gate, w_gate) + dot_back(grad_up, w_up)
    unused_three, norm_pull_three = jax.vjp(norm_scale, stream_two, gain_three)
    grad_from_three, grad_gain_three = norm_pull_three(grad_normed_three)
    grad_two = grad_stream + grad_from_three
    grad_cross_in = grad_two.astype(jnp.bfloat16)
    grad_w_cross_out = dot_rows(cross_rows, grad_cross_in)
    grad_cross_mixed = split_heads(
        dot_back(grad_cross_in, w_cross_out).astype(jnp.bfloat16), seq_count, maxlen
    )
    grad_cq, grad_ck, grad_cv = attend_backward(
        cross_queries, cross_keys, cross_values, everywhere, cross_logsum, grad_cross_mixed
    )
    grad_cq = grad_cq.reshape(row_count, -1)
    grad_ck = grad_ck.reshape(seq_count * patch_rows, -1)
    grad_cv = grad_cv.reshape(seq_count * patch_rows, -1)
    grad_w_cross_query = dot_rows(normed_two, grad_cq)
    grad_normed_two = dot_back(grad_cq, w_cross_query)
    grad_w_cross_key = dot_rows(features, grad_ck)
    grad_w_cross_value = dot_rows(features, grad_cv)
    grad_features = (dot_back(grad_ck, w_cross_key) + dot_back(grad_cv, w_cross_value)).astype(
        jnp.bfloat16
    )
    grad_bias_patch = jnp.sum(grad_features.astype(jnp.float32), axis=0)
    grad_w_patch = dot_rows(flat_patches, grad_features)
    grad_patch_raw = dot_back(grad_features, w_patch)
    unused_two, norm_pull_two = jax.vjp(norm_scale, stream_one, gain_two)
    grad_from_two, grad_gain_two = norm_pull_two(grad_normed_two)
    grad_one = grad_two + grad_from_two
    grad_attn_in = grad_one.astype(jnp.bfloat16)
    grad_w_out = dot_rows(attn_rows, grad_attn_in)
    grad_mixed = split_heads(dot_back(grad_attn_in, w_out).astype(jnp.bfloat16), seq_count, maxlen)
    grad_q, grad_k, grad_v = attend_backward(
        queries, key_rows, value_rows, allowed, logsum, grad_mixed
    )
    grad_q = grad_q.reshape(row_count, -1)
    grad_k = grad_k.reshape(row_count, -1)
    grad_v = grad_v.reshape(row_count, -1)
    grad_w_query = dot_rows(normed_one, grad_q)
    grad_w_key = dot_rows(normed_one, grad_k)
    grad_w_value = dot_rows(normed_one, grad_v)
    grad_normed_one = (
        dot_back(grad_q, w_query) + dot_back(grad_k, w_key) + dot_back(grad_v, w_value)
    )
    unused_one, norm_pull_one = jax.vjp(norm_scale, stream, gain_one)
    grad_from_one, grad_gain_one = norm_pull_one(grad_normed_one)
    grad_tokens_raw = grad_one + grad_from_one
    gains = jnp.concatenate([grad_gain_one, grad_gain_two, grad_gain_three, grad_bias_patch])
    gain_block = jnp.zeros((BLOCKS, 8, 128), jnp.float32).at[:16, 0, :].set(gains.reshape(16, 128))
    gain_block = gain_block.reshape(BLOCKS * 8, 128)
    late = merge((grad_w_down, grad_w_gate, grad_w_up), codes, weight_ref)
    cross = merge(
        (grad_w_cross_out, grad_w_cross_query, grad_w_cross_key, grad_w_cross_value),
        codes,
        weight_ref,
    )
    patch = merge((grad_w_patch,), codes, weight_ref)
    own = merge((grad_w_out, grad_w_query, grad_w_key, grad_w_value, gain_block), codes, weight_ref)
    gains = own[4].reshape(BLOCKS, 8, 128)[:16, 0, :].reshape(4, 512)
    grad_tokens = weight_own * grad_tokens_raw
    grad_patches = (weight_own * grad_patch_raw).reshape(seq_count, patch_rows, -1)
    return (
        result,
        grad_tokens,
        grad_patches,
        gains[0],
        own[1],
        own[2],
        own[3],
        own[0],
        gains[1],
        patch[0],
        gains[3],
        cross[1],
        cross[2],
        cross[3],
        cross[0],
        gains[2],
        late[1],
        late[2],
        late[0],
    )


def solution(mesh):
    placed = (
        P("dp", None),
        P("dp", None),
        P("dp", None, None),
        P("dp"),
        P(),
        P(),
        P(),
        P(),
        P(),
        P(),
        P(),
        P(),
        P(),
        P(),
        P(),
        P(),
        P(),
        P(),
        P(),
        P(),
        P(),
        P(),
    )
    return jax.shard_map(
        local,
        mesh=mesh,
        in_specs=placed,
        out_specs=(
            P("dp", None),
            P("dp", None),
            P("dp", None, None),
            P(),
            P(),
            P(),
            P(),
            P(),
            P(),
            P(),
            P(),
            P(),
            P(),
            P(),
            P(),
            P(),
            P(),
            P(),
            P(),
        ),
        check_vma=False,
    )
```

```python
import functools

import jax
import jax.numpy as jnp
from jax import lax
from jax.experimental import pallas as pl
from jax.experimental.pallas import tpu as pltpu
from jax.sharding import PartitionSpec as P

HEADS = 6
HEAD_DIM = 64
PAIRS = HEADS // 2
PAIR = 2 * HEAD_DIM
INNER = HEADS * HEAD_DIM
BLOCKS = 32
HALF = 16
EPSILON = 1e-06
F32 = jnp.float32
BF16 = jnp.bfloat16
VMEM = pltpu.VMEM
SMEM = pltpu.SMEM


def dot_plain(left_op, right_op):
    return jnp.dot(left_op, right_op, preferred_element_type=F32)


def dot_rows(left_op, right_op):
    return lax.dot_general(left_op, right_op, (((0,), (0,)), ((), ())), preferred_element_type=F32)


def dot_back(left_op, right_op):
    return lax.dot_general(left_op, right_op, (((1,), (1,)), ((), ())), preferred_element_type=F32)


def inverse_rms(values):
    return lax.rsqrt(jnp.mean(values * values, axis=-1, keepdims=True) + EPSILON)


def norm_backward(values, gain, grad):
    inverse = inverse_rms(values)
    unit = values * inverse
    scaled = grad * gain
    along = jnp.mean(scaled * unit, axis=-1, keepdims=True)
    return inverse * (scaled - unit * along), jnp.sum(grad * unit, axis=0, keepdims=True)


def lane_masks():
    lane = lax.broadcasted_iota(jnp.int32, (1, PAIR), 1)
    first = jnp.where(lane < HEAD_DIM, 1.0, 0.0)
    return first.astype(BF16), (1.0 - first).astype(BF16)


def stack_heads(values):
    first, second = lane_masks()
    return jnp.concatenate([values * first, values * second], axis=0)


def fold_heads(values):
    half = values.shape[0] // 2
    lane = lax.broadcasted_iota(jnp.int32, (half, PAIR), 1)
    return jnp.where(lane < HEAD_DIM, values[:half], values[half:])


def pair_forward(queries, key_rows, value_rows, allowed):
    keys = key_rows.shape[0]
    scores = dot_back(stack_heads(key_rows), queries).reshape(2, keys, queries.shape[0])
    if allowed is not None:
        scores = jnp.where(allowed, scores, -1000000000.0)
    expo = jnp.exp(scores - jnp.max(scores, axis=1, keepdims=True))
    chances = expo * (1.0 / jnp.sum(expo, axis=1, keepdims=True))
    chances = chances.reshape(2 * keys, queries.shape[0]).astype(BF16)
    return chances, dot_rows(chances, stack_heads(value_rows)).astype(BF16)


def pair_backward(queries, key_rows, value_rows, chances, grad_mixed):
    keys, count = key_rows.shape[0], queries.shape[0]
    wide = chances.astype(F32)
    grad_chances = dot_back(stack_heads(value_rows), grad_mixed)
    product = wide * grad_chances
    inner = jnp.sum(product.reshape(2, keys, count), axis=1, keepdims=True)
    spread = (wide.reshape(2, keys, count) * inner).reshape(2 * keys, count)
    grad_scores = (product - spread).astype(BF16)
    grad_values = fold_heads(dot_plain(chances, grad_mixed))
    grad_keys = fold_heads(dot_plain(grad_scores, queries))
    grad_queries = dot_rows(grad_scores, stack_heads(key_rows)) * 0.125
    return grad_queries.astype(BF16), grad_keys.astype(BF16), grad_values.astype(BF16)


def pair_lanes(index, offset=0):
    return pl.ds(offset + index * PAIR, PAIR)


def features_kernel(patch_ref, weight_ref, bias_ref, wk_ref, wv_ref, feat_ref, kv_ref, joined):
    @pl.when(pl.program_id(0) == 0)
    def join():
        joined[:, :INNER] = wk_ref[...]
        joined[:, INNER:] = wv_ref[...]

    feat = (dot_plain(patch_ref[...], weight_ref[...]) + bias_ref[...]).astype(BF16)
    feat_ref[...] = feat
    kv_ref[...] = dot_plain(feat, joined[...]).astype(BF16)


def self_forward_kernel(
    len_ref, tok_ref, g1_ref, wq_ref, wk_ref, wv_ref, wo_ref, g2_ref, wcq_ref,
    h1_ref, qkv_ref, pt_ref, o_ref, x1_ref, h2_ref, cq_ref, joined, wcq,
):
    step = pl.program_id(0)

    @pl.when(step == 0)
    def join():
        joined[:, :INNER] = wq_ref[...] * 0.125
        joined[:, INNER : 2 * INNER] = wk_ref[...]
        joined[:, 2 * INNER :] = wv_ref[...]
        wcq[...] = wcq_ref[...] * 0.125

    seqs, _, _, maxlen = pt_ref.shape
    x = tok_ref[...].astype(F32)
    h1 = (x * inverse_rms(x) * g1_ref[...]).astype(BF16)
    h1_ref[...] = h1
    qkv_ref[...] = dot_plain(h1, joined[...]).astype(BF16)
    key_at = lax.broadcasted_iota(jnp.int32, (1, maxlen, maxlen), 1)
    query_at = lax.broadcasted_iota(jnp.int32, (1, maxlen, maxlen), 2)
    for s in range(seqs):
        rows = pl.ds(s * maxlen, maxlen)
        allowed = (key_at <= query_at) & (key_at < len_ref[step * seqs + s])
        for p in range(PAIRS):
            pt_ref[s, p], o_ref[rows, pair_lanes(p)] = pair_forward(
                qkv_ref[rows, pair_lanes(p)],
                qkv_ref[rows, pair_lanes(p, INNER)],
                qkv_ref[rows, pair_lanes(p, 2 * INNER)],
                allowed,
            )
    x1 = x + dot_plain(o_ref[...], wo_ref[...])
    x1_ref[...] = x1
    h2 = (x1 * inverse_rms(x1) * g2_ref[...]).astype(BF16)
    h2_ref[...] = h2
    cq_ref[...] = dot_plain(h2, wcq[...]).astype(BF16)


def cross_forward_kernel(cq_ref, kv_ref, x1_ref, wco_ref, pt_ref, oc_ref, x2_ref):
    seqs, _, both, maxlen = pt_ref.shape
    patches = both // 2
    for s in range(seqs):
        rows, wide = pl.ds(s * maxlen, maxlen), pl.ds(s * patches, patches)
        for p in range(PAIRS):
            pt_ref[s, p], oc_ref[rows, pair_lanes(p)] = pair_forward(
                cq_ref[rows, pair_lanes(p)],
                kv_ref[wide, pair_lanes(p)],
                kv_ref[wide, pair_lanes(p, INNER)],
                None,
            )
    x2_ref[...] = x1_ref[...] + dot_plain(oc_ref[...], wco_ref[...])


def add_to(ref, first, value):
    @pl.when(first)
    def fresh():
        ref[...] = value

    @pl.when(jnp.logical_not(first))
    def more():
        ref[...] += value


def feed_forward_kernel(
    len_ref, code_ref, x2_ref, cot_ref, g3_ref, wg_ref, wu_ref, wd_ref,
    out_ref, dx2_ref, gain_ref, keep_ref, send_ref,
    hid, dgate, dup, acc_down, acc_gate, acc_up, *, maxlen,
):
    step, steps = pl.program_id(0), pl.num_programs(0)
    x2 = x2_ref[...]
    h3 = (x2 * inverse_rms(x2) * g3_ref[...]).astype(BF16)
    rows = x2.shape[0]
    seqs = rows // maxlen
    at = lax.broadcasted_iota(jnp.int32, (maxlen, 1), 0)
    keep = jnp.concatenate(
        [jnp.where(at < len_ref[step * seqs + s], 1.0, 0.0) for s in range(seqs)], axis=0
    )
    e = cot_ref[...].astype(F32) * keep
    de = e.astype(BF16)
    wide = wg_ref.shape[1]
    chunk = 256
    for c in range(wide // chunk):
        cols = pl.ds(c * chunk, chunk)
        gate = dot_plain(h3, wg_ref[:, cols])
        up = dot_plain(h3, wu_ref[:, cols])
        grad = dot_back(de, wd_ref[cols, :])
        square = gate * gate
        tanh = jnp.tanh(gate * (0.7978845608028654 + (0.7978845608028654 * 0.044715) * square))
        half = 0.5 * (1.0 + tanh)
        gelu = gate * half
        slope = half + (0.5 * gate) * (1.0 - tanh * tanh) * (
            0.7978845608028654 + (3.0 * 0.7978845608028654 * 0.044715) * square
        )
        hid[:, cols] = (gelu * up).astype(BF16)
        dgate[:, cols] = (grad * up * slope).astype(BF16)
        dup[:, cols] = (grad * gelu).astype(BF16)
    out_ref[...] = (x2 + dot_plain(hid[...], wd_ref[...])).astype(BF16)
    dh3 = dot_back(dgate[...], wg_ref[...]) + dot_back(dup[...], wu_ref[...])
    dx, gain = norm_backward(x2, g3_ref[...], dh3)
    dx2_ref[...] = e + dx
    add_to(gain_ref, step == 0, gain)
    add_to(acc_down, step == 0, dot_rows(hid[...], de))
    add_to(acc_gate, step == 0, dot_rows(h3, dgate[...]))
    add_to(acc_up, step == 0, dot_rows(h3, dup[...]))

    @pl.when(step == steps - 1)
    def finish():
        items = [(acc_down, acc_down.shape, 0), (acc_gate, acc_gate.shape, 0), (acc_up, acc_up.shape, 0)]
        pack(items, code_ref, keep_ref, send_ref)


def cross_backward_kernel(
    code_ref, dx2_ref, oc_ref, cq_ref, pt_ref, kv_ref, h2_ref, feat_ref, x1_ref, g2_ref,
    wco_ref, wcq_ref, wck_ref, wcv_ref,
    dfeat_ref, dx1_ref, gain_ref, bias_ref, keep_ref, send_ref,
    joined, dcq, dkv, acc_out, acc_query, acc_kv,
):
    step, steps = pl.program_id(0), pl.num_programs(0)

    @pl.when(step == 0)
    def join():
        joined[:, :INNER] = wck_ref[...]
        joined[:, INNER:] = wcv_ref[...]

    seqs, _, both, maxlen = pt_ref.shape
    patches = both // 2
    dx2 = dx2_ref[...]
    dc = dx2.astype(BF16)
    doc = dot_back(dc, wco_ref[...]).astype(BF16)
    for s in range(seqs):
        rows, wide = pl.ds(s * maxlen, maxlen), pl.ds(s * patches, patches)
        for p in range(PAIRS):
            dcq[rows, pair_lanes(p)], dkv[wide, pair_lanes(p)], dkv[wide, pair_lanes(p, INNER)] = (
                pair_backward(
                    cq_ref[rows, pair_lanes(p)],
                    kv_ref[wide, pair_lanes(p)],
                    kv_ref[wide, pair_lanes(p, INNER)],
                    pt_ref[s, p],
                    doc[s * maxlen : (s + 1) * maxlen, p * PAIR : (p + 1) * PAIR],
                )
            )
    dh2 = dot_back(dcq[...], wcq_ref[...])
    dfeat = dot_back(dkv[...], joined[...]).astype(BF16)
    dfeat_ref[...] = dfeat
    dx, gain = norm_backward(x1_ref[...], g2_ref[...], dh2)
    dx1_ref[...] = dx2 + dx
    add_to(gain_ref, step == 0, gain)
    add_to(bias_ref, step == 0, jnp.sum(dfeat.astype(F32), axis=0, keepdims=True))
    add_to(acc_out, step == 0, dot_rows(oc_ref[...], dc))
    add_to(acc_query, step == 0, dot_rows(h2_ref[...], dcq[...]))
    add_to(acc_kv, step == 0, dot_rows(feat_ref[...], dkv[...]))

    @pl.when(step == steps - 1)
    def finish():
        small = acc_query.shape
        items = [(acc_out, acc_out.shape, 0), (acc_query, small, 0), (acc_kv, small, 0), (acc_kv, small, INNER)]
        pack(items, code_ref, keep_ref, send_ref)


def patch_weight_kernel(code_ref, patch_ref, dfeat_ref, keep_ref, send_ref, acc, turned):
    step, steps = pl.program_id(0), pl.num_programs(0)
    add_to(acc, step == 0, dot_rows(dfeat_ref[...], patch_ref[...]))

    @pl.when(step == steps - 1)
    def finish():
        turned[...] = acc[...].T
        pack([(turned, turned.shape, 0)], code_ref, keep_ref, send_ref)


def patch_input_kernel(weight_ref, dfeat_ref, w_ref, out_ref):
    out_ref[...] = dot_back(dfeat_ref[...], w_ref[...]) * weight_ref[0]


def self_backward_kernel(
    code_ref, weight_ref, dx1_ref, o_ref, qkv_ref, pt_ref, h1_ref, tok_ref, g1_ref,
    wo_ref, wq_ref, wk_ref, wv_ref, gain_two_ref, gain_three_ref, bias_ref,
    dtok_ref, keep_ref, send_ref,
    joined, dqkv, acc_out, acc_qkv, gain, gain_block,
):
    step, steps = pl.program_id(0), pl.num_programs(0)

    @pl.when(step == 0)
    def join():
        joined[:, :INNER] = wq_ref[...]
        joined[:, INNER : 2 * INNER] = wk_ref[...]
        joined[:, 2 * INNER :] = wv_ref[...]

    seqs, _, _, maxlen = pt_ref.shape
    dx1 = dx1_ref[...]
    da = dx1.astype(BF16)
    do = dot_back(da, wo_ref[...]).astype(BF16)
    for s in range(seqs):
        rows = pl.ds(s * maxlen, maxlen)
        for p in range(PAIRS):
            lanes = [pair_lanes(p, k * INNER) for k in range(3)]
            dqkv[rows, lanes[0]], dqkv[rows, lanes[1]], dqkv[rows, lanes[2]] = pair_backward(
                qkv_ref[rows, lanes[0]],
                qkv_ref[rows, lanes[1]],
                qkv_ref[rows, lanes[2]],
                pt_ref[s, p],
                do[s * maxlen : (s + 1) * maxlen, p * PAIR : (p + 1) * PAIR],
            )
    dh1 = dot_back(dqkv[...], joined[...])
    dx, grad_gain = norm_backward(tok_ref[...].astype(F32), g1_ref[...], dh1)
    dtok_ref[...] = (dx1 + dx) * weight_ref[0]
    add_to(gain, step == 0, grad_gain)
    add_to(acc_out, step == 0, dot_rows(o_ref[...], da))
    add_to(acc_qkv, step == 0, dot_rows(h1_ref[...], dqkv[...]))

    @pl.when(step == steps - 1)
    def finish():
        gain_block[...] = jnp.zeros_like(gain_block)
        for k, ref in enumerate((gain, gain_two_ref, gain_three_ref, bias_ref)):
            for t in range(4):
                gain_block[pl.ds((4 * k + t) * 8, 1), :] = ref[:, pl.ds(t * 128, 128)]
        small = (acc_qkv.shape[0], INNER)
        items = [(acc_out, acc_out.shape, 0)]
        items += [(acc_qkv, small, k * INNER) for k in range(3)]
        items += [(gain_block, gain_block.shape, 0)]
        pack(items, code_ref, keep_ref, send_ref)


def flips(count, first, second):
    return [(i, i ^ (first if i % 2 == 0 else second)) for i in range(count)]


def code_pair(me):
    core, ex, why = me & 1, (me >> 1) & 1, (me >> 2) & 1
    low = (me >> 3) & 3
    low = ((low & 1) << 1) | (low >> 1)
    first = jnp.where(core == 0, ex, why)
    second = jnp.where(core == 0, why, ex)
    own = core * 16 + first * 8 + second * 4 + low
    other = (1 - core) * 16 + second * 8 + first * 4 + low
    return own, other


def exchange(values, first, second=None):
    count = lax.axis_size("dp")
    return lax.ppermute(values, "dp", flips(count, first, first if second is None else second))


def block_rows(shape):
    return shape[0] * shape[1] // (BLOCKS * 128)


def block_parts(shape, index, offset):
    rows, lanes = shape
    tiles = lanes // 128
    if BLOCKS % tiles:
        height = rows // BLOCKS
        return [
            (pl.ds(pl.multiple_of(index * height, 8), height), pl.ds(offset + t * 128, 128))
            for t in range(tiles)
        ]
    height = rows * tiles // BLOCKS
    row, lane = index // tiles, index % tiles
    return [
        (
            pl.ds(pl.multiple_of(row * height, 8), height),
            pl.ds(pl.multiple_of(offset + lane * 128, 128), 128),
        )
    ]


def pack(items, code_ref, keep_ref, send_ref):
    def step(p, carry):
        for code, out_ref in ((code_ref[0], keep_ref), (code_ref[1], send_ref)):
            start = 0
            for ref, shape, offset in items:
                for rows, lanes in block_parts(shape, p ^ code, offset):
                    out_ref[p, pl.ds(start, rows.size), :] = ref[rows, lanes]
                    start += rows.size
        return carry

    lax.fori_loop(0, HALF, step, 0)


def unpack_kernel(shapes, with_gains, code_ref, *refs):
    ins, outs = refs[:4], refs[4:]
    for k, piece in enumerate(ins):

        def step(p, carry, piece=piece, k=k):
            index = (p + 8 * (k % 2)) ^ code_ref[k // 2]
            start = 0
            for shape, out_ref in zip(shapes, outs):
                for rows, lanes in block_parts(shape, index, 0):
                    out_ref[rows, lanes] = piece[p, pl.ds(start, rows.size), :]
                    start += rows.size
            return carry

        lax.fori_loop(0, 8, step, 0)
    if with_gains:
        count = len(shapes)
        block = outs[count - 1]
        for k, out_ref in enumerate(outs[count:]):
            for t in range(4):
                out_ref[:, pl.ds(t * 128, 128)] = block[pl.ds((4 * k + t) * 8, 1), :]


def vmem(count):
    return [pl.BlockSpec(memory_space=VMEM)] * count


def unpack(pieces, shapes, codes, with_gains=False):
    outs = [jax.ShapeDtypeStruct(s, F32) for s in shapes]
    if with_gains:
        outs += [jax.ShapeDtypeStruct((1, 512), F32)] * 4
    return pl.pallas_call(
        functools.partial(unpack_kernel, shapes, with_gains),
        out_shape=outs,
        in_specs=[pl.BlockSpec(memory_space=SMEM)] + vmem(4),
        out_specs=vmem(len(outs)),
        compiler_params=pltpu.CompilerParams(vmem_limit_bytes=40 * 2**20),
        name="unpack",
    )(codes, *pieces)


def sum_blocks(packed, own, other):
    keep, send = packed
    got = exchange(send, 1)
    keep, got = keep * own, got * other
    for first, second in ((2, 4), (4, 2), (8, 8), (16, 16)):
        half = keep.shape[0] // 2
        send, keep = keep[half:] + got[half:], keep[:half] + got[:half]
        got = exchange(send, first, second)
    keep = keep + got
    extra = BLOCKS
    while extra < lax.axis_size("dp"):
        keep = keep + exchange(keep, extra)
        extra *= 2
    return keep


def spread_blocks(held):
    held = jnp.concatenate([held, exchange(held, 16)])
    held = jnp.concatenate([held, exchange(held, 8)])
    held = jnp.concatenate([held, exchange(held, 4, 2)])
    near = exchange(held, 1)
    rest = exchange(held, 2, 4)
    far = exchange(rest, 1)
    return held, rest, near, far


def by_step(array_shape, steps):
    block = (array_shape[0] // steps,) + tuple(array_shape[1:])
    return pl.BlockSpec(block, lambda i: (i,) + (0,) * (len(block) - 1))


def whole(array_shape):
    return pl.BlockSpec(tuple(array_shape), lambda i: (0,) * len(array_shape))


SCALARS = pl.BlockSpec(memory_space=SMEM)


def run(kernel, name, steps, scalars, stepped, fixed, order, outs, scratch, cost):
    lists = {"s": iter(scalars), "r": iter(stepped), "f": iter(fixed)}
    operands = [next(lists[c]) for c in order]
    in_specs = [
        SCALARS if c == "s" else by_step(v.shape, steps) if c == "r" else whole(v.shape)
        for c, v in zip(order, operands)
    ]
    return pl.pallas_call(
        kernel,
        grid=(steps,),
        out_shape=[jax.ShapeDtypeStruct(s, d) for s, d, _ in outs],
        in_specs=in_specs,
        out_specs=[by_step(s, steps) if moves else whole(s) for s, _, moves in outs],
        scratch_shapes=[VMEM(s, d) for s, d in scratch],
        compiler_params=pltpu.CompilerParams(vmem_limit_bytes=56 * 2**20),
        cost_estimate=pl.CostEstimate(flops=int(cost * 1e9), bytes_accessed=2**20, transcendentals=0),
        name=name,
    )(*operands)


def local(
    tokens,
    cotangent,
    patches,
    lengths,
    group_member,
    mix,
    gain_one,
    w_query,
    w_key,
    w_value,
    w_out,
    gain_two,
    w_patch,
    bias_patch,
    w_cross_query,
    w_cross_key,
    w_cross_value,
    w_cross_out,
    gain_three,
    w_gate,
    w_up,
    w_down,
):
    seqs = lengths.shape[0]
    rows, width = tokens.shape
    maxlen = rows // seqs
    images, patch_dim = patches.shape[1], patches.shape[2]
    image_rows = seqs * images
    wide = w_gate.shape[1]
    steps = seqs // 2
    part = rows // steps
    flat = patches.reshape(image_rows, patch_dim)
    gain_one, gain_two, gain_three, bias_patch = (
        g.reshape(1, width) for g in (gain_one, gain_two, gain_three, bias_patch)
    )

    me = lax.axis_index("dp")
    codes = jnp.stack(code_pair(me))
    members = lax.dynamic_slice_in_dim(group_member, me & ~1, 2)
    in_first = lax.dynamic_index_in_dim(members, me & 1, keepdims=False) == 1
    other_first = lax.dynamic_index_in_dim(members, 1 - (me & 1), keepdims=False) == 1
    own_count = jnp.sum(lengths).astype(F32)
    counts = own_count * jnp.where(in_first, jnp.array([1.0, 0.0], F32), jnp.array([0.0, 1.0], F32))
    bit = 1
    while bit < lax.axis_size("dp"):
        counts = counts + exchange(counts, bit)
        bit *= 2
    group_weights = mix * jnp.sum(counts) / counts
    weight_own = jnp.where(in_first, group_weights[0], group_weights[1])
    weight_other = jnp.where(other_first, group_weights[0], group_weights[1])
    weight_ref = weight_own[None]

    feat, cross_kv = run(
        features_kernel, "features", steps, [], [flat],
        [w_patch, bias_patch, w_cross_key, w_cross_value], "rffff",
        [((image_rows, width), BF16, True), ((image_rows, 2 * INNER), BF16, True)],
        [((width, 2 * INNER), BF16)], 5.1,
    )
    h1, qkv, chances, mixed, x1, h2, cross_q = run(
        self_forward_kernel, "self_forward", steps, [lengths], [tokens],
        [gain_one, w_query, w_key, w_value, w_out, gain_two, w_cross_query], "srfffffff",
        [
            ((rows, width), BF16, True),
            ((rows, 3 * INNER), BF16, True),
            ((seqs, PAIRS, 2 * maxlen, maxlen), BF16, True),
            ((rows, INNER), BF16, True),
            ((rows, width), F32, True),
            ((rows, width), BF16, True),
            ((rows, INNER), BF16, True),
        ],
        [((width, 3 * INNER), BF16), ((width, INNER), BF16)], 6.0,
    )
    cross_chances, cross_mixed, x2 = run(
        cross_forward_kernel, "cross_forward", steps, [], [cross_q, cross_kv, x1], [w_cross_out], "rrrf",
        [
            ((seqs, PAIRS, 2 * images, maxlen), BF16, True),
            ((rows, INNER), BF16, True),
            ((rows, width), F32, True),
        ],
        [], 6.0,
    )
    late_shapes = [w_down.shape, w_gate.shape, w_up.shape]
    late_rows = sum(block_rows(s) for s in late_shapes)
    result, dx2, gain3, *late = run(
        functools.partial(feed_forward_kernel, maxlen=maxlen), "feed_forward", steps,
        [lengths, codes], [x2, cotangent], [gain_three, w_gate, w_up, w_down], "ssrrffff",
        [
            ((rows, width), BF16, True),
            ((rows, width), F32, True),
            ((1, width), F32, False),
            ((HALF, late_rows, 128), F32, False),
            ((HALF, late_rows, 128), F32, False),
        ],
        [
            ((part, wide), BF16),
            ((part, wide), BF16),
            ((part, wide), BF16),
            (w_down.shape, F32),
            (w_gate.shape, F32),
            (w_up.shape, F32),
        ],
        14.0,
    )
    cross_shapes = [w_cross_out.shape, w_cross_query.shape, w_cross_key.shape, w_cross_value.shape]
    cross_rows = sum(block_rows(s) for s in cross_shapes)
    dfeat, dx1, gain2, dbias, *cross = run(
        cross_backward_kernel, "cross_backward", steps, [codes],
        [dx2, cross_mixed, cross_q, cross_chances, cross_kv, h2, feat, x1],
        [gain_two, w_cross_out, w_cross_query, w_cross_key, w_cross_value], "srrrrrrrrfffff",
        [
            ((image_rows, width), BF16, True),
            ((rows, width), F32, True),
            ((1, width), F32, False),
            ((1, width), F32, False),
            ((HALF, cross_rows, 128), F32, False),
            ((HALF, cross_rows, 128), F32, False),
        ],
        [
            ((width, 2 * INNER), BF16),
            ((part, INNER), BF16),
            ((image_rows // steps, 2 * INNER), BF16),
            (w_cross_out.shape, F32),
            (w_cross_query.shape, F32),
            ((width, 2 * INNER), F32),
        ],
        10.0,
    )
    patch_shapes = [w_patch.shape]
    patch_rows = block_rows(w_patch.shape)
    patch = run(
        patch_weight_kernel, "patch_weight", steps, [codes], [flat, dfeat], [], "srr",
        [((HALF, patch_rows, 128), F32, False), ((HALF, patch_rows, 128), F32, False)],
        [((width, patch_dim), F32), ((patch_dim, width), F32)], 5.0,
    )
    own_shapes = [w_out.shape, w_query.shape, w_key.shape, w_value.shape, (BLOCKS * 8, 128)]
    own_rows = sum(block_rows(s) for s in own_shapes)
    grad_tokens, *own = run(
        self_backward_kernel, "self_backward", steps, [codes, weight_ref],
        [dx1, mixed, qkv, chances, h1, tokens],
        [gain_one, w_out, w_query, w_key, w_value, gain2, gain3, dbias], "ssrrrrrrffffffff",
        [
            ((rows, width), F32, True),
            ((HALF, own_rows, 128), F32, False),
            ((HALF, own_rows, 128), F32, False),
        ],
        [
            ((width, 3 * INNER), BF16),
            ((part, 3 * INNER), BF16),
            (w_out.shape, F32),
            ((width, 3 * INNER), F32),
            ((1, width), F32),
            ((BLOCKS * 8, 128), F32),
        ],
        8.0,
    )
    (grad_patches,) = run(
        patch_input_kernel, "patch_input", 2 * steps, [weight_ref], [dfeat], [w_patch], "srf",
        [((image_rows, patch_dim), F32, True)], [], 4.0,
    )

    pieces = [spread_blocks(sum_blocks(v, weight_own, weight_other)) for v in (late, cross, patch, own)]
    late = unpack(pieces[0], late_shapes, codes)
    cross = unpack(pieces[1], cross_shapes, codes)
    patch = unpack(pieces[2], patch_shapes, codes)
    own = unpack(pieces[3], own_shapes, codes, True)
    gains = [g.reshape(width) for g in own[5:]]
    return (
        result,
        grad_tokens,
        grad_patches.reshape(seqs, images, patch_dim),
        gains[0],
        own[1],
        own[2],
        own[3],
        own[0],
        gains[1],
        patch[0],
        gains[3],
        cross[1],
        cross[2],
        cross[3],
        cross[0],
        gains[2],
        late[1],
        late[2],
        late[0],
    )


def solution(mesh):
    split = P("dp", None)
    images = P("dp", None, None)
    return jax.shard_map(
        local,
        mesh=mesh,
        in_specs=(split, split, images, P("dp")) + (P(),) * 18,
        out_specs=(split, split, images) + (P(),) * 16,
        check_vma=False,
    )
```

```python
import functools

import jax
import jax.numpy as jnp
from jax import lax
from jax.experimental import pallas as pl
from jax.experimental.pallas import tpu as pltpu
from jax.sharding import PartitionSpec as P

HEADS = 6
HEAD_DIM = 64
PAIRS = HEADS // 2
PAIR = 2 * HEAD_DIM
INNER = HEADS * HEAD_DIM
BLOCKS = 32
HALF = 16
EPSILON = 1e-06
F32 = jnp.float32
BF16 = jnp.bfloat16
VMEM = pltpu.VMEM
SMEM = pltpu.SMEM


def dot_plain(left_op, right_op):
    return jnp.dot(left_op, right_op, preferred_element_type=F32)


def dot_rows(left_op, right_op):
    return lax.dot_general(left_op, right_op, (((0,), (0,)), ((), ())), preferred_element_type=F32)


def dot_back(left_op, right_op):
    return lax.dot_general(left_op, right_op, (((1,), (1,)), ((), ())), preferred_element_type=F32)


def inverse_rms(values):
    return lax.rsqrt(jnp.mean(values * values, axis=-1, keepdims=True) + EPSILON)


def norm_backward(values, gain, grad):
    inverse = inverse_rms(values)
    unit = values * inverse
    scaled = grad * gain
    along = jnp.mean(scaled * unit, axis=-1, keepdims=True)
    return inverse * (scaled - unit * along), jnp.sum(grad * unit, axis=0, keepdims=True)


def lane_masks():
    lane = lax.broadcasted_iota(jnp.int32, (1, PAIR), 1)
    first = jnp.where(lane < HEAD_DIM, 1.0, 0.0)
    return first.astype(BF16), (1.0 - first).astype(BF16)


def stack_heads(values):
    first, second = lane_masks()
    return jnp.concatenate([values * first, values * second], axis=0)


def fold_heads(values):
    half = values.shape[0] // 2
    lane = lax.broadcasted_iota(jnp.int32, (half, PAIR), 1)
    return jnp.where(lane < HEAD_DIM, values[:half], values[half:])


def pair_forward(queries, key_rows, value_rows, allowed):
    keys = key_rows.shape[0]
    scores = dot_back(stack_heads(key_rows), queries).reshape(2, keys, queries.shape[0])
    if allowed is not None:
        scores = jnp.where(allowed, scores, -1000000000.0)
    expo = jnp.exp(scores - jnp.max(scores, axis=1, keepdims=True))
    chances = expo * (1.0 / jnp.sum(expo, axis=1, keepdims=True))
    chances = chances.reshape(2 * keys, queries.shape[0]).astype(BF16)
    return chances, dot_rows(chances, stack_heads(value_rows)).astype(BF16)


def pair_backward(queries, key_rows, value_rows, chances, grad_mixed):
    keys, count = key_rows.shape[0], queries.shape[0]
    wide = chances.astype(F32)
    grad_chances = dot_back(stack_heads(value_rows), grad_mixed)
    product = wide * grad_chances
    inner = jnp.sum(product.reshape(2, keys, count), axis=1, keepdims=True)
    spread = (wide.reshape(2, keys, count) * inner).reshape(2 * keys, count)
    grad_scores = (product - spread).astype(BF16)
    grad_values = fold_heads(dot_plain(chances, grad_mixed))
    grad_keys = fold_heads(dot_plain(grad_scores, queries))
    grad_queries = dot_rows(grad_scores, stack_heads(key_rows)) * 0.125
    return grad_queries.astype(BF16), grad_keys.astype(BF16), grad_values.astype(BF16)


def pair_lanes(index, offset=0):
    return pl.ds(offset + index * PAIR, PAIR)


def features_kernel(patch_ref, weight_ref, bias_ref, wk_ref, wv_ref, feat_ref, kv_ref, joined):
    @pl.when(pl.program_id(0) == 0)
    def join():
        joined[:, :INNER] = wk_ref[...]
        joined[:, INNER:] = wv_ref[...]

    feat = (dot_plain(patch_ref[...], weight_ref[...]) + bias_ref[...]).astype(BF16)
    feat_ref[...] = feat
    kv_ref[...] = dot_plain(feat, joined[...]).astype(BF16)


def self_forward_kernel(
    len_ref, tok_ref, g1_ref, wq_ref, wk_ref, wv_ref, wo_ref, g2_ref, wcq_ref,
    h1_ref, qkv_ref, pt_ref, o_ref, x1_ref, h2_ref, cq_ref, joined, wcq,
):
    step = pl.program_id(0)

    @pl.when(step == 0)
    def join():
        joined[:, :INNER] = wq_ref[...] * 0.125
        joined[:, INNER : 2 * INNER] = wk_ref[...]
        joined[:, 2 * INNER :] = wv_ref[...]
        wcq[...] = wcq_ref[...] * 0.125

    seqs, _, _, maxlen = pt_ref.shape
    x = tok_ref[...].astype(F32)
    h1 = (x * inverse_rms(x) * g1_ref[...]).astype(BF16)
    h1_ref[...] = h1
    qkv_ref[...] = dot_plain(h1, joined[...]).astype(BF16)
    key_at = lax.broadcasted_iota(jnp.int32, (1, maxlen, maxlen), 1)
    query_at = lax.broadcasted_iota(jnp.int32, (1, maxlen, maxlen), 2)
    for s in range(seqs):
        rows = pl.ds(s * maxlen, maxlen)
        allowed = (key_at <= query_at) & (key_at < len_ref[step * seqs + s])
        for p in range(PAIRS):
            pt_ref[s, p], o_ref[rows, pair_lanes(p)] = pair_forward(
                qkv_ref[rows, pair_lanes(p)],
                qkv_ref[rows, pair_lanes(p, INNER)],
                qkv_ref[rows, pair_lanes(p, 2 * INNER)],
                allowed,
            )
    x1 = x + dot_plain(o_ref[...], wo_ref[...])
    x1_ref[...] = x1
    h2 = (x1 * inverse_rms(x1) * g2_ref[...]).astype(BF16)
    h2_ref[...] = h2
    cq_ref[...] = dot_plain(h2, wcq[...]).astype(BF16)


def cross_forward_kernel(cq_ref, kv_ref, x1_ref, wco_ref, pt_ref, oc_ref, x2_ref):
    seqs, _, both, maxlen = pt_ref.shape
    patches = both // 2
    for s in range(seqs):
        rows, wide = pl.ds(s * maxlen, maxlen), pl.ds(s * patches, patches)
        for p in range(PAIRS):
            pt_ref[s, p], oc_ref[rows, pair_lanes(p)] = pair_forward(
                cq_ref[rows, pair_lanes(p)],
                kv_ref[wide, pair_lanes(p)],
                kv_ref[wide, pair_lanes(p, INNER)],
                None,
            )
    x2_ref[...] = x1_ref[...] + dot_plain(oc_ref[...], wco_ref[...])


def add_to(ref, first, value):
    @pl.when(first)
    def fresh():
        ref[...] = value

    @pl.when(jnp.logical_not(first))
    def more():
        ref[...] += value


def feed_forward_kernel(
    len_ref, code_ref, x2_ref, cot_ref, g3_ref, wg_ref, wu_ref, wd_ref,
    out_ref, dx2_ref, gain_ref, keep_low, keep_high, send_low, send_high,
    hid, dgate, dup, acc_down, acc_gate, acc_up, *, maxlen,
):
    step, steps = pl.program_id(0), pl.num_programs(0)
    x2 = x2_ref[...]
    h3 = (x2 * inverse_rms(x2) * g3_ref[...]).astype(BF16)
    rows = x2.shape[0]
    seqs = rows // maxlen
    at = lax.broadcasted_iota(jnp.int32, (maxlen, 1), 0)
    keep = jnp.concatenate(
        [jnp.where(at < len_ref[step * seqs + s], 1.0, 0.0) for s in range(seqs)], axis=0
    )
    e = cot_ref[...].astype(F32) * keep
    de = e.astype(BF16)
    wide = wg_ref.shape[1]
    chunk = 256
    for c in range(wide // chunk):
        cols = pl.ds(c * chunk, chunk)
        gate = dot_plain(h3, wg_ref[:, cols])
        up = dot_plain(h3, wu_ref[:, cols])
        grad = dot_back(de, wd_ref[cols, :])
        square = gate * gate
        tanh = jnp.tanh(gate * (0.7978845608028654 + (0.7978845608028654 * 0.044715) * square))
        half = 0.5 * (1.0 + tanh)
        gelu = gate * half
        slope = half + (0.5 * gate) * (1.0 - tanh * tanh) * (
            0.7978845608028654 + (3.0 * 0.7978845608028654 * 0.044715) * square
        )
        hid[:, cols] = (gelu * up).astype(BF16)
        dgate[:, cols] = (grad * up * slope).astype(BF16)
        dup[:, cols] = (grad * gelu).astype(BF16)
    out_ref[...] = (x2 + dot_plain(hid[...], wd_ref[...])).astype(BF16)
    dh3 = dot_back(dgate[...], wg_ref[...]) + dot_back(dup[...], wu_ref[...])
    dx, gain = norm_backward(x2, g3_ref[...], dh3)
    dx2_ref[...] = e + dx
    add_to(gain_ref, step == 0, gain)
    add_to(acc_down, step == 0, dot_rows(hid[...], de))
    add_to(acc_gate, step == 0, dot_rows(h3, dgate[...]))
    add_to(acc_up, step == 0, dot_rows(h3, dup[...]))

    @pl.when(step == steps - 1)
    def finish():
        items = [(acc_down, acc_down.shape, 0), (acc_gate, acc_gate.shape, 0), (acc_up, acc_up.shape, 0)]
        pack(items, code_ref, keep_low, keep_high, send_low, send_high)


def cross_attention_kernel(dx2_ref, cq_ref, pt_ref, kv_ref, wco_ref, dcq_ref, dkv_ref):
    seqs, _, both, maxlen = pt_ref.shape
    patches = both // 2
    doc = dot_back(dx2_ref[...].astype(BF16), wco_ref[...]).astype(BF16)
    for s in range(seqs):
        rows, wide = pl.ds(s * maxlen, maxlen), pl.ds(s * patches, patches)
        for p in range(PAIRS):
            keys, values = pair_lanes(p), pair_lanes(p, INNER)
            dcq_ref[rows, keys], dkv_ref[wide, keys], dkv_ref[wide, values] = pair_backward(
                cq_ref[rows, keys],
                kv_ref[wide, keys],
                kv_ref[wide, values],
                pt_ref[s, p],
                doc[s * maxlen : (s + 1) * maxlen, p * PAIR : (p + 1) * PAIR],
            )


def cross_weights_kernel(
    code_ref, dx2_ref, oc_ref, dcq_ref, dkv_ref, h2_ref, feat_ref, x1_ref, g2_ref,
    wcq_ref, wck_ref, wcv_ref,
    dfeat_ref, dx1_ref, gain_ref, bias_ref, keep_low, keep_high, send_low, send_high,
    joined, acc_out, acc_query, acc_kv,
):
    step, steps = pl.program_id(0), pl.num_programs(0)

    @pl.when(step == 0)
    def join():
        joined[:, :INNER] = wck_ref[...]
        joined[:, INNER:] = wcv_ref[...]

    dx2 = dx2_ref[...]
    dfeat = dot_back(dkv_ref[...], joined[...]).astype(BF16)
    dfeat_ref[...] = dfeat
    dh2 = dot_back(dcq_ref[...], wcq_ref[...])
    dx, gain = norm_backward(x1_ref[...], g2_ref[...], dh2)
    dx1_ref[...] = dx2 + dx
    add_to(gain_ref, step == 0, gain)
    add_to(bias_ref, step == 0, jnp.sum(dfeat.astype(F32), axis=0, keepdims=True))
    add_to(acc_out, step == 0, dot_rows(oc_ref[...], dx2.astype(BF16)))
    add_to(acc_query, step == 0, dot_rows(h2_ref[...], dcq_ref[...]))
    add_to(acc_kv, step == 0, dot_rows(feat_ref[...], dkv_ref[...]))

    @pl.when(step == steps - 1)
    def finish():
        small = acc_query.shape
        items = [(acc_out, acc_out.shape, 0), (acc_query, small, 0), (acc_kv, small, 0), (acc_kv, small, INNER)]
        pack(items, code_ref, keep_low, keep_high, send_low, send_high)


def patch_weight_kernel(code_ref, patch_ref, dfeat_ref, keep_low, keep_high, send_low, send_high, acc, turned):
    step, steps = pl.program_id(0), pl.num_programs(0)
    add_to(acc, step == 0, dot_rows(dfeat_ref[...], patch_ref[...]))

    @pl.when(step == steps - 1)
    def finish():
        turned[...] = acc[...].T
        pack([(turned, turned.shape, 0)], code_ref, keep_low, keep_high, send_low, send_high)


def patch_input_kernel(weight_ref, dfeat_ref, w_ref, *refs):
    refs[-1][...] = dot_back(dfeat_ref[...], w_ref[...]) * weight_ref[0]


def self_attention_kernel(dx1_ref, qkv_ref, pt_ref, wo_ref, dqkv_ref):
    seqs, _, _, maxlen = pt_ref.shape
    do = dot_back(dx1_ref[...].astype(BF16), wo_ref[...]).astype(BF16)
    for s in range(seqs):
        rows = pl.ds(s * maxlen, maxlen)
        for p in range(PAIRS):
            lanes = [pair_lanes(p, k * INNER) for k in range(3)]
            dqkv_ref[rows, lanes[0]], dqkv_ref[rows, lanes[1]], dqkv_ref[rows, lanes[2]] = pair_backward(
                qkv_ref[rows, lanes[0]],
                qkv_ref[rows, lanes[1]],
                qkv_ref[rows, lanes[2]],
                pt_ref[s, p],
                do[s * maxlen : (s + 1) * maxlen, p * PAIR : (p + 1) * PAIR],
            )


def self_weights_kernel(
    code_ref, weight_ref, dx1_ref, o_ref, dqkv_ref, h1_ref, tok_ref, g1_ref,
    wq_ref, wk_ref, wv_ref, gain_two_ref, gain_three_ref, bias_ref,
    dtok_ref, keep_low, keep_high, send_low, send_high,
    joined, acc_out, acc_qkv, gain, gain_block,
):
    step, steps = pl.program_id(0), pl.num_programs(0)

    @pl.when(step == 0)
    def join():
        joined[:, :INNER] = wq_ref[...]
        joined[:, INNER : 2 * INNER] = wk_ref[...]
        joined[:, 2 * INNER :] = wv_ref[...]

    dx1 = dx1_ref[...]
    dh1 = dot_back(dqkv_ref[...], joined[...])
    dx, grad_gain = norm_backward(tok_ref[...].astype(F32), g1_ref[...], dh1)
    dtok_ref[...] = (dx1 + dx) * weight_ref[0]
    add_to(gain, step == 0, grad_gain)
    add_to(acc_out, step == 0, dot_rows(o_ref[...], dx1.astype(BF16)))
    add_to(acc_qkv, step == 0, dot_rows(h1_ref[...], dqkv_ref[...]))

    @pl.when(step == steps - 1)
    def finish():
        gain_block[...] = jnp.zeros_like(gain_block)
        for k, ref in enumerate((gain, gain_two_ref, gain_three_ref, bias_ref)):
            for t in range(4):
                gain_block[pl.ds((4 * k + t) * 8, 1), :] = ref[:, pl.ds(t * 128, 128)]
        small = (acc_qkv.shape[0], INNER)
        items = [(acc_out, acc_out.shape, 0)]
        items += [(acc_qkv, small, k * INNER) for k in range(3)]
        items += [(gain_block, gain_block.shape, 0)]
        pack(items, code_ref, keep_low, keep_high, send_low, send_high)


def flips(count, first, second):
    return [(i, i ^ (first if i % 2 == 0 else second)) for i in range(count)]


def code_pair(me):
    core, ex, why = me & 1, (me >> 1) & 1, (me >> 2) & 1
    low = (me >> 3) & 3
    low = ((low & 1) << 1) | (low >> 1)
    first = jnp.where(core == 0, ex, why)
    second = jnp.where(core == 0, why, ex)
    own = core * 16 + first * 8 + second * 4 + low
    other = (1 - core) * 16 + second * 8 + first * 4 + low
    return own, other


def exchange(values, first, second=None):
    count = lax.axis_size("dp")
    return lax.ppermute(values, "dp", flips(count, first, first if second is None else second))


def block_rows(shape):
    return shape[0] * shape[1] // (BLOCKS * 128)


def block_parts(shape, index, offset):
    rows, lanes = shape
    tiles = lanes // 128
    if BLOCKS % tiles:
        height = rows // BLOCKS
        return [
            (pl.ds(pl.multiple_of(index * height, 8), height), pl.ds(offset + t * 128, 128))
            for t in range(tiles)
        ]
    height = rows * tiles // BLOCKS
    row, lane = index // tiles, index % tiles
    return [
        (
            pl.ds(pl.multiple_of(row * height, 8), height),
            pl.ds(pl.multiple_of(offset + lane * 128, 128), 128),
        )
    ]


def pack(items, code_ref, *out_refs):
    def step(p, carry):
        for k, out_ref in enumerate(out_refs):
            start = 0
            index = (p + 8 * (k % 2)) ^ code_ref[k // 2]
            for ref, shape, offset in items:
                for rows, lanes in block_parts(shape, index, offset):
                    out_ref[p, pl.ds(start, rows.size), :] = ref[rows, lanes]
                    start += rows.size
        return carry

    lax.fori_loop(0, 8, step, 0)


def unpack_kernel(shapes, with_gains, code_ref, *refs):
    ins, outs = refs[:4], refs[4:]
    for k, piece in enumerate(ins):

        def step(p, carry, piece=piece, k=k):
            index = (p + 8 * (k % 2)) ^ code_ref[k // 2]
            start = 0
            for shape, out_ref in zip(shapes, outs):
                for rows, lanes in block_parts(shape, index, 0):
                    out_ref[rows, lanes] = piece[p, pl.ds(start, rows.size), :]
                    start += rows.size
            return carry

        lax.fori_loop(0, 8, step, 0)
    if with_gains:
        count = len(shapes)
        block = outs[count - 1]
        for k, out_ref in enumerate(outs[count:]):
            for t in range(4):
                out_ref[:, pl.ds(t * 128, 128)] = block[pl.ds((4 * k + t) * 8, 1), :]


def vmem(count):
    return [pl.BlockSpec(memory_space=VMEM)] * count


def unpack(pieces, shapes, codes, with_gains=False):
    outs = [jax.ShapeDtypeStruct(s, F32) for s in shapes]
    if with_gains:
        outs += [jax.ShapeDtypeStruct((1, 512), F32)] * 4
    return pl.pallas_call(
        functools.partial(unpack_kernel, shapes, with_gains),
        out_shape=outs,
        in_specs=[pl.BlockSpec(memory_space=SMEM)] + vmem(4),
        out_specs=vmem(len(outs)),
        compiler_params=pltpu.CompilerParams(vmem_limit_bytes=40 * 2**20),
        name="unpack",
    )(codes, *pieces)


def after(values, *others):
    return lax.optimization_barrier((values, others))[0]


class Chunk:
    def __init__(self, packed, shapes, weights, codes, with_gains=False):
        self.keep_low, self.keep_high, self.send_low, self.send_high = packed
        self.shapes, self.weights, self.codes, self.with_gains = shapes, weights, codes, with_gains

    def start(self):
        own, other = self.weights
        high = exchange(self.send_high, 1)
        low = exchange(self.send_low, 1)
        self.send = self.keep_high * own + high * other
        self.keep = self.keep_low * own + low * other

    def halve(self, first, second=None, last=False):
        got = exchange(self.send, first, second)
        if last:
            self.send = self.keep + got
            return
        half = got.shape[0] // 2
        self.send, self.keep = self.keep[half:] + got[half:], self.keep[:half] + got[:half]

    def first(self):
        self.halve(2, 4)

    def second(self):
        self.halve(4, 2)

    def third(self):
        self.halve(8)

    def fourth(self):
        self.halve(16, last=True)
        extra = BLOCKS
        while extra < lax.axis_size("dp"):
            self.send = self.send + exchange(self.send, extra)
            extra *= 2

    def double(self, first, second=None):
        self.send = jnp.concatenate([self.send, exchange(self.send, first, second)])

    def back_fourth(self):
        self.double(16)

    def back_third(self):
        self.double(8)

    def back_second(self):
        self.double(4, 2)

    def back_first(self):
        self.near = exchange(self.send, 1)
        self.rest = exchange(self.send, 2, 4)

    def finish(self):
        self.far = exchange(self.rest, 1)

    def unpack(self):
        pieces = (self.send, self.rest, self.near, self.far)
        return unpack(pieces, self.shapes, self.codes, self.with_gains)


def by_step(array_shape, steps):
    block = (array_shape[0] // steps,) + tuple(array_shape[1:])
    return pl.BlockSpec(block, lambda i: (i,) + (0,) * (len(block) - 1))


def whole(array_shape):
    return pl.BlockSpec(tuple(array_shape), lambda i: (0,) * len(array_shape))


SCALARS = pl.BlockSpec(memory_space=SMEM)


def run(kernel, name, steps, scalars, stepped, fixed, order, outs, scratch, cost):
    lists = {"s": iter(scalars), "r": iter(stepped), "f": iter(fixed)}
    operands = [next(lists[c]) for c in order]
    in_specs = [
        SCALARS if c == "s" else by_step(v.shape, steps) if c == "r" else whole(v.shape)
        for c, v in zip(order, operands)
    ]
    return pl.pallas_call(
        kernel,
        grid=(steps,),
        out_shape=[jax.ShapeDtypeStruct(s, d) for s, d, _ in outs],
        in_specs=in_specs,
        out_specs=[by_step(s, steps) if moves else whole(s) for s, _, moves in outs],
        scratch_shapes=[VMEM(s, d) for s, d in scratch],
        compiler_params=pltpu.CompilerParams(vmem_limit_bytes=56 * 2**20),
        cost_estimate=pl.CostEstimate(flops=int(cost * 1e9), bytes_accessed=2**20, transcendentals=0),
        name=name,
    )(*operands)


def local(
    tokens,
    cotangent,
    patches,
    lengths,
    group_member,
    mix,
    gain_one,
    w_query,
    w_key,
    w_value,
    w_out,
    gain_two,
    w_patch,
    bias_patch,
    w_cross_query,
    w_cross_key,
    w_cross_value,
    w_cross_out,
    gain_three,
    w_gate,
    w_up,
    w_down,
):
    seqs = lengths.shape[0]
    rows, width = tokens.shape
    maxlen = rows // seqs
    images, patch_dim = patches.shape[1], patches.shape[2]
    image_rows = seqs * images
    wide = w_gate.shape[1]
    steps = seqs // 2
    part = rows // steps
    flat = patches.reshape(image_rows, patch_dim)
    gain_one, gain_two, gain_three, bias_patch = (
        g.reshape(1, width) for g in (gain_one, gain_two, gain_three, bias_patch)
    )

    me = lax.axis_index("dp")
    codes = jnp.stack(code_pair(me))
    members = lax.dynamic_slice_in_dim(group_member, me & ~1, 2)
    in_first = lax.dynamic_index_in_dim(members, me & 1, keepdims=False) == 1
    other_first = lax.dynamic_index_in_dim(members, 1 - (me & 1), keepdims=False) == 1
    own_count = jnp.sum(lengths).astype(F32)
    counts = own_count * jnp.where(in_first, jnp.array([1.0, 0.0], F32), jnp.array([0.0, 1.0], F32))
    bits = [1]
    while 2 * bits[-1] < lax.axis_size("dp"):
        bits.append(2 * bits[-1])
    counts = counts + exchange(counts, bits.pop(0))

    feat, cross_kv = run(
        features_kernel, "features", steps, [], [after(flat, counts)],
        [w_patch, bias_patch, w_cross_key, w_cross_value], "rffff",
        [((image_rows, width), BF16, True), ((image_rows, 2 * INNER), BF16, True)],
        [((width, 2 * INNER), BF16)], 5.1,
    )
    counts = counts + exchange(counts, bits.pop(0))
    h1, qkv, chances, mixed, x1, h2, cross_q = run(
        self_forward_kernel, "self_forward", steps, [lengths], [after(tokens, counts, feat)],
        [gain_one, w_query, w_key, w_value, w_out, gain_two, w_cross_query], "srfffffff",
        [
            ((rows, width), BF16, True),
            ((rows, 3 * INNER), BF16, True),
            ((seqs, PAIRS, 2 * maxlen, maxlen), BF16, True),
            ((rows, INNER), BF16, True),
            ((rows, width), F32, True),
            ((rows, width), BF16, True),
            ((rows, INNER), BF16, True),
        ],
        [((width, 3 * INNER), BF16), ((width, INNER), BF16)], 6.0,
    )
    counts = counts + exchange(counts, bits.pop(0))
    cross_chances, cross_mixed, x2 = run(
        cross_forward_kernel, "cross_forward", steps, [], [after(cross_q, counts), cross_kv, x1],
        [w_cross_out], "rrrf",
        [
            ((seqs, PAIRS, 2 * images, maxlen), BF16, True),
            ((rows, INNER), BF16, True),
            ((rows, width), F32, True),
        ],
        [], 6.0,
    )
    while len(bits) > 1:
        counts = counts + exchange(counts, bits.pop(0))
    late_shapes = [w_down.shape, w_gate.shape, w_up.shape]
    late_rows = sum(block_rows(s) for s in late_shapes)
    result, dx2, gain3, *late = run(
        functools.partial(feed_forward_kernel, maxlen=maxlen), "feed_forward", steps,
        [lengths, codes], [after(x2, counts), cotangent], [gain_three, w_gate, w_up, w_down], "ssrrffff",
        [
            ((rows, width), BF16, True),
            ((rows, width), F32, True),
            ((1, width), F32, False),
        ] + [((8, late_rows, 128), F32, False)] * 4,
        [
            ((part, wide), BF16),
            ((part, wide), BF16),
            ((part, wide), BF16),
            (w_down.shape, F32),
            (w_gate.shape, F32),
            (w_up.shape, F32),
        ],
        14.0,
    )
    counts = counts + exchange(counts, bits.pop(0))
    group_weights = mix * jnp.sum(counts) / counts
    weight_own = jnp.where(in_first, group_weights[0], group_weights[1])
    weight_other = jnp.where(other_first, group_weights[0], group_weights[1])
    weight_ref = weight_own[None]
    weights = (weight_own, weight_other)

    late = Chunk(late, late_shapes, weights, codes)
    late.start()
    dcq, dkv = run(
        cross_attention_kernel, "cross_attention", steps, [],
        [after(dx2, late.send), cross_q, cross_chances, cross_kv], [w_cross_out], "rrrrf",
        [((rows, INNER), BF16, True), ((image_rows, 2 * INNER), BF16, True)], [], 8.0,
    )
    late.first()
    cross_shapes = [w_cross_out.shape, w_cross_query.shape, w_cross_key.shape, w_cross_value.shape]
    cross_rows = sum(block_rows(s) for s in cross_shapes)
    dfeat, dx1, gain2, dbias, *cross = run(
        cross_weights_kernel, "cross_weights", steps, [codes],
        [after(dx2, late.send), cross_mixed, dcq, dkv, h2, feat, x1],
        [gain_two, w_cross_query, w_cross_key, w_cross_value], "srrrrrrrffff",
        [
            ((image_rows, width), BF16, True),
            ((rows, width), F32, True),
            ((1, width), F32, False),
            ((1, width), F32, False),
        ] + [((8, cross_rows, 128), F32, False)] * 4,
        [
            ((width, 2 * INNER), BF16),
            (w_cross_out.shape, F32),
            (w_cross_query.shape, F32),
            ((width, 2 * INNER), F32),
        ],
        8.0,
    )
    late.second()
    cross = Chunk(cross, cross_shapes, weights, codes)
    cross.start()
    (dqkv,) = run(
        self_attention_kernel, "self_attention", steps, [],
        [after(dx1, late.send, cross.send), qkv, chances], [w_out], "rrrf",
        [((rows, 3 * INNER), BF16, True)], [], 8.0,
    )
    late.third()
    cross.first()
    own_shapes = [w_out.shape, w_query.shape, w_key.shape, w_value.shape, (BLOCKS * 8, 128)]
    own_rows = sum(block_rows(s) for s in own_shapes)
    grad_tokens, *own = run(
        self_weights_kernel, "self_weights", steps, [codes, weight_ref],
        [after(dx1, late.send, cross.send), mixed, dqkv, h1, tokens],
        [gain_one, w_query, w_key, w_value, gain2, gain3, dbias], "ssrrrrrfffffff",
        [((rows, width), F32, True)] + [((8, own_rows, 128), F32, False)] * 4,
        [
            ((width, 3 * INNER), BF16),
            (w_out.shape, F32),
            ((width, 3 * INNER), F32),
            ((1, width), F32),
            ((BLOCKS * 8, 128), F32),
        ],
        8.0,
    )
    late.fourth()
    cross.second()
    own = Chunk(own, own_shapes, weights, codes, True)
    own.start()
    patch_shapes = [w_patch.shape]
    patch_rows = block_rows(w_patch.shape)
    patch = run(
        patch_weight_kernel, "patch_weight", steps, [codes],
        [flat, after(dfeat, late.send, cross.send, own.send)], [], "srr",
        [((8, patch_rows, 128), F32, False)] * 4,
        [((width, patch_dim), F32), ((patch_dim, width), F32)], 8.0,
    )
    late.back_fourth()
    own.first()
    patch = Chunk(patch, patch_shapes, weights, codes)
    patch.start()
    half = image_rows // 2
    (grad_patches,) = run(
        patch_input_kernel, "patch_input", 2 * steps, [weight_ref],
        [after(dfeat, late.send, own.send, patch.send)], [w_patch], "srf",
        [((image_rows, patch_dim), F32, True)], [], 8.0,
    )
    late.back_third()
    own.second()
    cross.third()
    grad_patches, late.send, own.send, cross.send = lax.optimization_barrier(
        (grad_patches, late.send, own.send, cross.send)
    )
    late.back_second()
    cross.fourth()
    cross.back_fourth()
    late.send, cross.send = lax.optimization_barrier((late.send, cross.send))
    late.back_first()
    cross.back_third()
    own.third()
    own.fourth()
    late.rest, cross.send, own.send, patch.send = lax.optimization_barrier(
        (late.rest, cross.send, own.send, patch.send)
    )
    late.finish()
    patch.first()
    own.back_fourth()
    own.back_third()
    patch.send, own.send, cross.send = lax.optimization_barrier((patch.send, own.send, cross.send))
    patch.second()
    patch.send, cross.send = lax.optimization_barrier((patch.send, cross.send))
    cross.back_second()
    patch.third()
    patch.send, cross.send = lax.optimization_barrier((patch.send, cross.send))
    cross.back_first()
    patch.fourth()
    patch.back_fourth()
    patch.send, cross.rest, own.send = lax.optimization_barrier((patch.send, cross.rest, own.send))
    cross.finish()
    own.back_second()
    patch.back_third()
    patch.send, own.send = lax.optimization_barrier((patch.send, own.send))
    own.back_first()
    own.rest, patch.send = lax.optimization_barrier((own.rest, patch.send))
    own.finish()
    patch.back_second()
    patch.back_first()
    patch.finish()
    late = late.unpack()
    cross = cross.unpack()
    own = own.unpack()
    patch = patch.unpack()
    gains = [g.reshape(width) for g in own[5:]]
    return (
        result,
        grad_tokens,
        grad_patches.reshape(seqs, images, patch_dim),
        gains[0],
        own[1],
        own[2],
        own[3],
        own[0],
        gains[1],
        patch[0],
        gains[3],
        cross[1],
        cross[2],
        cross[3],
        cross[0],
        gains[2],
        late[1],
        late[2],
        late[0],
    )


def solution(mesh):
    split = P("dp", None)
    images = P("dp", None, None)
    return jax.shard_map(
        local,
        mesh=mesh,
        in_specs=(split, split, images, P("dp")) + (P(),) * 18,
        out_specs=(split, split, images) + (P(),) * 16,
        check_vma=False,
    )
```

```python
import functools

import jax
import jax.numpy as jnp
from jax import lax
from jax.experimental import pallas as pl
from jax.experimental.pallas import tpu as pltpu
from jax.sharding import PartitionSpec as P

HEADS = 6
HEAD_DIM = 64
PAIRS = HEADS // 2
PAIR = 2 * HEAD_DIM
INNER = HEADS * HEAD_DIM
BLOCKS = 32
HALF = 16
EPSILON = 1e-06
F32 = jnp.float32
BF16 = jnp.bfloat16
VMEM = pltpu.VMEM
SMEM = pltpu.SMEM


def dot_plain(left_op, right_op):
    return jnp.dot(left_op, right_op, preferred_element_type=F32)


def dot_rows(left_op, right_op):
    return lax.dot_general(left_op, right_op, (((0,), (0,)), ((), ())), preferred_element_type=F32)


def dot_back(left_op, right_op):
    return lax.dot_general(left_op, right_op, (((1,), (1,)), ((), ())), preferred_element_type=F32)


def inverse_rms(values):
    return lax.rsqrt(jnp.mean(values * values, axis=-1, keepdims=True) + EPSILON)


def norm_backward(values, gain, grad):
    inverse = inverse_rms(values)
    unit = values * inverse
    scaled = grad * gain
    along = jnp.mean(scaled * unit, axis=-1, keepdims=True)
    return inverse * (scaled - unit * along), jnp.sum(grad * unit, axis=0, keepdims=True)


def lane_masks():
    lane = lax.broadcasted_iota(jnp.int32, (1, PAIR), 1)
    first = jnp.where(lane < HEAD_DIM, 1.0, 0.0)
    return first.astype(BF16), (1.0 - first).astype(BF16)


def stack_heads(values):
    first, second = lane_masks()
    return jnp.concatenate([values * first, values * second], axis=0)


def fold_heads(values):
    half = values.shape[0] // 2
    lane = lax.broadcasted_iota(jnp.int32, (half, PAIR), 1)
    return jnp.where(lane < HEAD_DIM, values[:half], values[half:])


def pair_forward(queries, key_rows, value_rows, allowed):
    keys = key_rows.shape[0]
    scores = dot_back(stack_heads(key_rows), queries).reshape(2, keys, queries.shape[0])
    if allowed is not None:
        scores = jnp.where(allowed, scores, -1000000000.0)
    expo = jnp.exp(scores - jnp.max(scores, axis=1, keepdims=True))
    chances = expo * (1.0 / jnp.sum(expo, axis=1, keepdims=True))
    chances = chances.reshape(2 * keys, queries.shape[0]).astype(BF16)
    return chances, dot_rows(chances, stack_heads(value_rows)).astype(BF16)


def pair_backward(queries, key_rows, value_rows, chances, grad_mixed):
    keys, count = key_rows.shape[0], queries.shape[0]
    wide = chances.astype(F32)
    grad_chances = dot_back(stack_heads(value_rows), grad_mixed)
    product = wide * grad_chances
    inner = jnp.sum(product.reshape(2, keys, count), axis=1, keepdims=True)
    spread = (wide.reshape(2, keys, count) * inner).reshape(2 * keys, count)
    grad_scores = (product - spread).astype(BF16)
    grad_values = fold_heads(dot_plain(chances, grad_mixed))
    grad_keys = fold_heads(dot_plain(grad_scores, queries))
    grad_queries = dot_rows(grad_scores, stack_heads(key_rows)) * 0.125
    return grad_queries.astype(BF16), grad_keys.astype(BF16), grad_values.astype(BF16)


def pair_lanes(index, offset=0):
    return pl.ds(offset + index * PAIR, PAIR)


def features_kernel(
    me_ref, len_ref, member_ref, patch_ref, weight_ref, bias_ref, wk_ref, wv_ref,
    feat_ref, kv_ref, count_ref, joined,
):
    @pl.when(pl.program_id(0) == 0)
    def join():
        count = sum(len_ref[s] for s in range(len_ref.shape[0])).astype(F32)
        in_first = member_ref[me_ref[0]] == 1
        count_ref[0] = jnp.where(in_first, count, 0.0)
        count_ref[1] = jnp.where(in_first, 0.0, count)
        joined[:, :INNER] = wk_ref[...]
        joined[:, INNER:] = wv_ref[...]

    feat = (dot_plain(patch_ref[...], weight_ref[...]) + bias_ref[...]).astype(BF16)
    feat_ref[...] = feat
    kv_ref[...] = dot_plain(feat, joined[...]).astype(BF16)


def self_forward_kernel(
    len_ref, tok_ref, g1_ref, wq_ref, wk_ref, wv_ref, wo_ref, g2_ref, wcq_ref,
    h1_ref, qkv_ref, pt_ref, o_ref, x1_ref, h2_ref, cq_ref, joined, wcq,
):
    step = pl.program_id(0)

    @pl.when(step == 0)
    def join():
        joined[:, :INNER] = wq_ref[...] * 0.125
        joined[:, INNER : 2 * INNER] = wk_ref[...]
        joined[:, 2 * INNER :] = wv_ref[...]
        wcq[...] = wcq_ref[...] * 0.125

    seqs, _, _, maxlen = pt_ref.shape
    x = tok_ref[...].astype(F32)
    h1 = (x * inverse_rms(x) * g1_ref[...]).astype(BF16)
    h1_ref[...] = h1
    qkv_ref[...] = dot_plain(h1, joined[...]).astype(BF16)
    key_at = lax.broadcasted_iota(jnp.int32, (1, maxlen, maxlen), 1)
    query_at = lax.broadcasted_iota(jnp.int32, (1, maxlen, maxlen), 2)
    for s in range(seqs):
        rows = pl.ds(s * maxlen, maxlen)
        allowed = (key_at <= query_at) & (key_at < len_ref[step * seqs + s])
        for p in range(PAIRS):
            pt_ref[s, p], o_ref[rows, pair_lanes(p)] = pair_forward(
                qkv_ref[rows, pair_lanes(p)],
                qkv_ref[rows, pair_lanes(p, INNER)],
                qkv_ref[rows, pair_lanes(p, 2 * INNER)],
                allowed,
            )
    x1 = x + dot_plain(o_ref[...], wo_ref[...])
    x1_ref[...] = x1
    h2 = (x1 * inverse_rms(x1) * g2_ref[...]).astype(BF16)
    h2_ref[...] = h2
    cq_ref[...] = dot_plain(h2, wcq[...]).astype(BF16)


def cross_forward_kernel(cq_ref, kv_ref, x1_ref, wco_ref, pt_ref, oc_ref, x2_ref):
    seqs, _, both, maxlen = pt_ref.shape
    patches = both // 2
    for s in range(seqs):
        rows, wide = pl.ds(s * maxlen, maxlen), pl.ds(s * patches, patches)
        for p in range(PAIRS):
            pt_ref[s, p], oc_ref[rows, pair_lanes(p)] = pair_forward(
                cq_ref[rows, pair_lanes(p)],
                kv_ref[wide, pair_lanes(p)],
                kv_ref[wide, pair_lanes(p, INNER)],
                None,
            )
    x2_ref[...] = x1_ref[...] + dot_plain(oc_ref[...], wco_ref[...])


def add_to(ref, first, value):
    @pl.when(first)
    def fresh():
        ref[...] = value

    @pl.when(jnp.logical_not(first))
    def more():
        ref[...] += value


def gelu_parts(gate):
    slant = 0.7978845608028654
    square = gate * gate
    tanh = jnp.tanh(gate * (slant + (slant * 0.044715) * square))
    half = 0.5 + 0.5 * tanh
    slope = half + (0.5 * gate) * (1.0 - tanh * tanh) * (slant + (3.0 * slant * 0.044715) * square)
    return gate * half, slope


def feed_forward_kernel(
    len_ref, code_ref, x2_ref, cot_ref, g3_ref, wg_ref, wu_ref, wd_ref,
    hid_ref, dgate_ref, dup_ref, keep_low, keep_high, send_low, send_high,
    h3_all, de_all, hid_all, dgate_all, dup_all, acc_down, acc_gate, acc_up, *, maxlen,
):
    step, steps = pl.program_id(0), pl.num_programs(0)
    x2 = x2_ref[...]
    h3 = (x2 * inverse_rms(x2) * g3_ref[...]).astype(BF16)
    rows = x2.shape[0]
    seqs = rows // maxlen
    at = lax.broadcasted_iota(jnp.int32, (maxlen, 1), 0)
    keep = jnp.concatenate(
        [jnp.where(at < len_ref[step * seqs + s], 1.0, 0.0) for s in range(seqs)], axis=0
    )
    de = (cot_ref[...].astype(F32) * keep).astype(BF16)
    here = pl.ds(pl.multiple_of(step * rows, rows), rows)
    h3_all[here, :] = h3
    de_all[here, :] = de
    wide = wg_ref.shape[1]
    chunk = 256
    for c in range(wide // chunk):
        cols = pl.ds(c * chunk, chunk)
        gate = dot_plain(h3, wg_ref[:, cols])
        up = dot_plain(h3, wu_ref[:, cols])
        grad = dot_back(de, wd_ref[cols, :])
        gelu, slope = gelu_parts(gate)
        hid = (gelu * up).astype(BF16)
        dgate = (grad * up * slope).astype(BF16)
        dup = (grad * gelu).astype(BF16)
        hid_ref[:, cols], hid_all[here, cols] = hid, hid
        dgate_ref[:, cols], dgate_all[here, cols] = dgate, dgate
        dup_ref[:, cols], dup_all[here, cols] = dup, dup

    @pl.when(step == steps - 1)
    def finish():
        for c in range(wide // chunk):
            cols = pl.ds(c * chunk, chunk)
            acc_down[cols, :] = dot_rows(hid_all[:, cols], de_all[...])
            acc_gate[:, cols] = dot_rows(h3_all[...], dgate_all[:, cols])
            acc_up[:, cols] = dot_rows(h3_all[...], dup_all[:, cols])
        items = [(acc_down, acc_down.shape, 0), (acc_gate, acc_gate.shape, 0), (acc_up, acc_up.shape, 0)]
        pack(items, code_ref, keep_low, keep_high, send_low, send_high)


def feed_back_kernel(
    me_ref, len_ref, member_ref, mix_ref, count_ref,
    x2_ref, cot_ref, hid_ref, dgate_ref, dup_ref, g3_ref, wg_ref, wu_ref, wd_ref,
    out_ref, dx2_ref, gain_ref, weight_ref, *, maxlen,
):
    step = pl.program_id(0)

    @pl.when(step == 0)
    def weigh():
        total = count_ref[0] + count_ref[1]
        first = mix_ref[0] * total / count_ref[0]
        second = mix_ref[1] * total / count_ref[1]
        weight_ref[0] = jnp.where(member_ref[me_ref[0]] == 1, first, second)
        weight_ref[1] = jnp.where(member_ref[me_ref[0] ^ 1] == 1, first, second)

    x2 = x2_ref[...]
    seqs = x2.shape[0] // maxlen
    at = lax.broadcasted_iota(jnp.int32, (maxlen, 1), 0)
    keep = jnp.concatenate(
        [jnp.where(at < len_ref[step * seqs + s], 1.0, 0.0) for s in range(seqs)], axis=0
    )
    out_ref[...] = (x2 + dot_plain(hid_ref[...], wd_ref[...])).astype(BF16)
    dh3 = dot_back(dgate_ref[...], wg_ref[...]) + dot_back(dup_ref[...], wu_ref[...])
    dx, gain = norm_backward(x2, g3_ref[...], dh3)
    dx2_ref[...] = cot_ref[...].astype(F32) * keep + dx
    add_to(gain_ref, step == 0, gain)


def cross_backward_kernel(
    dx2_ref, cq_ref, pt_ref, kv_ref, x1_ref, g2_ref, wco_ref, wcq_ref, wck_ref, wcv_ref,
    dcq_ref, dkv_ref, dfeat_ref, dx1_ref, dc_ref, gain_ref, bias_ref, joined,
):
    step = pl.program_id(0)

    @pl.when(step == 0)
    def join():
        joined[:, :INNER] = wck_ref[...]
        joined[:, INNER:] = wcv_ref[...]

    seqs, _, both, maxlen = pt_ref.shape
    patches = both // 2
    dx2 = dx2_ref[...]
    dc = dx2.astype(BF16)
    dc_ref[...] = dc
    doc = dot_back(dc, wco_ref[...]).astype(BF16)
    for s in range(seqs):
        rows, wide = pl.ds(s * maxlen, maxlen), pl.ds(s * patches, patches)
        for p in range(PAIRS):
            keys, values = pair_lanes(p), pair_lanes(p, INNER)
            dcq_ref[rows, keys], dkv_ref[wide, keys], dkv_ref[wide, values] = pair_backward(
                cq_ref[rows, keys],
                kv_ref[wide, keys],
                kv_ref[wide, values],
                pt_ref[s, p],
                doc[s * maxlen : (s + 1) * maxlen, p * PAIR : (p + 1) * PAIR],
            )
    dfeat = dot_back(dkv_ref[...], joined[...]).astype(BF16)
    dfeat_ref[...] = dfeat
    dh2 = dot_back(dcq_ref[...], wcq_ref[...])
    dx, gain = norm_backward(x1_ref[...], g2_ref[...], dh2)
    dx1_ref[...] = dx2 + dx
    add_to(gain_ref, step == 0, gain)
    add_to(bias_ref, step == 0, jnp.sum(dfeat.astype(F32), axis=0, keepdims=True))


def cross_weights_kernel(
    code_ref, oc_ref, dc_ref, h2_ref, dcq_ref, feat_ref, dkv_ref,
    keep_low, keep_high, send_low, send_high, acc_out, acc_query, acc_kv,
):
    acc_out[...] = dot_rows(oc_ref[...], dc_ref[...])
    acc_query[...] = dot_rows(h2_ref[...], dcq_ref[...])
    acc_kv[...] = dot_rows(feat_ref[...], dkv_ref[...])
    small = acc_query.shape
    items = [(acc_out, acc_out.shape, 0), (acc_query, small, 0), (acc_kv, small, 0), (acc_kv, small, INNER)]
    pack(items, code_ref, keep_low, keep_high, send_low, send_high)


def patch_weight_kernel(code_ref, patch_ref, dfeat_ref, keep_low, keep_high, send_low, send_high, acc, turned):
    step, steps = pl.program_id(0), pl.num_programs(0)
    add_to(acc, step == 0, dot_rows(dfeat_ref[...], patch_ref[...]))

    @pl.when(step == steps - 1)
    def finish():
        turned[...] = acc[...].T
        pack([(turned, turned.shape, 0)], code_ref, keep_low, keep_high, send_low, send_high)


def patch_input_kernel(weight_ref, dfeat_ref, w_ref, *refs):
    refs[-1][...] = dot_back(dfeat_ref[...], w_ref[...]) * weight_ref[0]


def self_backward_kernel(
    weight_ref, dx1_ref, qkv_ref, pt_ref, tok_ref, g1_ref, wo_ref, wq_ref, wk_ref, wv_ref,
    dqkv_ref, da_ref, dtok_ref, gain_ref, joined,
):
    step = pl.program_id(0)

    @pl.when(step == 0)
    def join():
        joined[:, :INNER] = wq_ref[...]
        joined[:, INNER : 2 * INNER] = wk_ref[...]
        joined[:, 2 * INNER :] = wv_ref[...]

    seqs, _, _, maxlen = pt_ref.shape
    dx1 = dx1_ref[...]
    da = dx1.astype(BF16)
    da_ref[...] = da
    do = dot_back(da, wo_ref[...]).astype(BF16)
    for s in range(seqs):
        rows = pl.ds(s * maxlen, maxlen)
        for p in range(PAIRS):
            lanes = [pair_lanes(p, k * INNER) for k in range(3)]
            dqkv_ref[rows, lanes[0]], dqkv_ref[rows, lanes[1]], dqkv_ref[rows, lanes[2]] = pair_backward(
                qkv_ref[rows, lanes[0]],
                qkv_ref[rows, lanes[1]],
                qkv_ref[rows, lanes[2]],
                pt_ref[s, p],
                do[s * maxlen : (s + 1) * maxlen, p * PAIR : (p + 1) * PAIR],
            )
    dh1 = dot_back(dqkv_ref[...], joined[...])
    dx, gain = norm_backward(tok_ref[...].astype(F32), g1_ref[...], dh1)
    dtok_ref[...] = (dx1 + dx) * weight_ref[0]
    add_to(gain_ref, step == 0, gain)


def self_weights_kernel(
    code_ref, o_ref, da_ref, h1_ref, dqkv_ref, gain_one_ref, gain_two_ref, gain_three_ref, bias_ref,
    keep_low, keep_high, send_low, send_high, acc_out, acc_qkv, gain_block,
):
    acc_out[...] = dot_rows(o_ref[...], da_ref[...])
    acc_qkv[...] = dot_rows(h1_ref[...], dqkv_ref[...])
    gain_block[...] = jnp.zeros_like(gain_block)
    for k, ref in enumerate((gain_one_ref, gain_two_ref, gain_three_ref, bias_ref)):
        for t in range(4):
            gain_block[pl.ds((4 * k + t) * 8, 1), :] = ref[:, pl.ds(t * 128, 128)]
    small = (acc_qkv.shape[0], INNER)
    items = [(acc_out, acc_out.shape, 0)]
    items += [(acc_qkv, small, k * INNER) for k in range(3)]
    items += [(gain_block, gain_block.shape, 0)]
    pack(items, code_ref, keep_low, keep_high, send_low, send_high)


def flips(count, first, second):
    return [(i, i ^ (first if i % 2 == 0 else second)) for i in range(count)]


def code_pair(me):
    core, ex, why = me & 1, (me >> 1) & 1, (me >> 2) & 1
    low = (me >> 3) & 3
    low = ((low & 1) << 1) | (low >> 1)
    first = jnp.where(core == 0, ex, why)
    second = jnp.where(core == 0, why, ex)
    own = core * 16 + first * 8 + second * 4 + low
    other = (1 - core) * 16 + second * 8 + first * 4 + low
    return own, other


def exchange(values, first, second=None):
    count = lax.axis_size("dp")
    return lax.ppermute(values, "dp", flips(count, first, first if second is None else second))


def block_rows(shape):
    return shape[0] * shape[1] // (BLOCKS * 128)


def block_parts(shape, index, offset):
    rows, lanes = shape
    tiles = lanes // 128
    if BLOCKS % tiles:
        height = rows // BLOCKS
        return [
            (pl.ds(pl.multiple_of(index * height, 8), height), pl.ds(offset + t * 128, 128))
            for t in range(tiles)
        ]
    height = rows * tiles // BLOCKS
    row, lane = index // tiles, index % tiles
    return [
        (
            pl.ds(pl.multiple_of(row * height, 8), height),
            pl.ds(pl.multiple_of(offset + lane * 128, 128), 128),
        )
    ]


def pack(items, code_ref, *out_refs):
    def step(p, carry):
        for k, out_ref in enumerate(out_refs):
            start = 0
            index = (p + 8 * (k % 2)) ^ code_ref[k // 2]
            for ref, shape, offset in items:
                for rows, lanes in block_parts(shape, index, offset):
                    out_ref[p, pl.ds(start, rows.size), :] = ref[rows, lanes]
                    start += rows.size
        return carry

    lax.fori_loop(0, 8, step, 0)


def unpack_kernel(shapes, with_gains, code_ref, *refs):
    ins, outs = refs[:4], refs[4:]
    for k, piece in enumerate(ins):

        def step(p, carry, piece=piece, k=k):
            index = (p + 8 * (k % 2)) ^ code_ref[k // 2]
            start = 0
            for shape, out_ref in zip(shapes, outs):
                for rows, lanes in block_parts(shape, index, 0):
                    out_ref[rows, lanes] = piece[p, pl.ds(start, rows.size), :]
                    start += rows.size
            return carry

        lax.fori_loop(0, 8, step, 0)
    if with_gains:
        count = len(shapes)
        block = outs[count - 1]
        for k, out_ref in enumerate(outs[count:]):
            for t in range(4):
                out_ref[:, pl.ds(t * 128, 128)] = block[pl.ds((4 * k + t) * 8, 1), :]


def vmem(count):
    return [pl.BlockSpec(memory_space=VMEM)] * count


def unpack(pieces, shapes, codes, with_gains=False):
    outs = [jax.ShapeDtypeStruct(s, F32) for s in shapes]
    if with_gains:
        outs += [jax.ShapeDtypeStruct((1, 512), F32)] * 4
    return pl.pallas_call(
        functools.partial(unpack_kernel, shapes, with_gains),
        out_shape=outs,
        in_specs=[pl.BlockSpec(memory_space=SMEM)] + vmem(4),
        out_specs=vmem(len(outs)),
        compiler_params=pltpu.CompilerParams(vmem_limit_bytes=40 * 2**20),
        name="unpack",
    )(codes, *pieces)


def fence(values, *chunks):
    values, state = lax.optimization_barrier((values, [(c.held, c.got) for c in chunks]))
    for c, (held, got) in zip(chunks, state):
        c.held, c.got = held, got
    return values


class Chunk:
    def __init__(self, packed, shapes, codes, with_gains=False):
        self.held, self.got = tuple(packed), ()
        self.shapes, self.codes, self.with_gains = shapes, codes, with_gains

    def send_cores(self):
        _, _, low, high = self.held
        self.got = (exchange(high, 1), exchange(low, 1))

    def take_cores(self, weights):
        keep_low, keep_high, _, _ = self.held
        high, low = self.got
        self.held = (keep_high * weights[0] + high * weights[1], keep_low)
        self.got, self.weights = (low,), weights

    def send_first(self):
        self.got += (exchange(self.held[0], 2, 4),)

    def take_first(self):
        (_, keep), (low, got), weights = self.held, self.got, self.weights
        keep = keep * weights[0] + low * weights[1]
        self.held, self.got = (keep[4:] + got[4:], keep[:4] + got[:4]), ()

    def send(self, first, second=None):
        self.got = (exchange(self.held[0], first, second),)

    def take(self):
        (_, keep), (got,) = self.held, self.got
        half = keep.shape[0] // 2
        self.held, self.got = (keep[half:] + got[half:], keep[:half] + got[:half]), ()

    def send_second(self):
        self.send(4, 2)

    def send_third(self):
        self.send(8)

    def send_fourth(self):
        self.send(16)

    def take_fourth(self):
        total = self.held[1] + self.got[0]
        extra = BLOCKS
        while extra < lax.axis_size("dp"):
            total = total + exchange(total, extra)
            extra *= 2
        self.held, self.got = (total,), ()

    def send_back_fourth(self):
        self.send(16)

    def send_back_third(self):
        self.send(8)

    def send_back_second(self):
        self.send(4, 2)

    def take_back(self):
        self.held, self.got = (jnp.concatenate([*self.held, *self.got]),), ()

    def send_back_first(self):
        self.got = (exchange(self.held[0], 2, 4), exchange(self.held[0], 1))

    def send_back_cores(self):
        self.held = (self.held[0], *self.got)
        self.got = (exchange(self.held[1], 1),)

    def unpack(self):
        return unpack(self.held + self.got, self.shapes, self.codes, self.with_gains)


def by_step(array_shape, steps):
    block = (array_shape[0] // steps,) + tuple(array_shape[1:])
    return pl.BlockSpec(block, lambda i: (i,) + (0,) * (len(block) - 1))


def whole(array_shape):
    return pl.BlockSpec(tuple(array_shape), lambda i: (0,) * len(array_shape))


SCALARS = pl.BlockSpec(memory_space=SMEM)


def run(kernel, name, steps, scalars, stepped, fixed, order, outs, scratch, cost):
    lists = {"s": iter(scalars), "r": iter(stepped), "f": iter(fixed)}
    operands = [next(lists[c]) for c in order]
    in_specs = [
        SCALARS if c == "s" else by_step(v.shape, steps) if c == "r" else whole(v.shape)
        for c, v in zip(order, operands)
    ]
    return pl.pallas_call(
        kernel,
        grid=(steps,),
        out_shape=[jax.ShapeDtypeStruct(s, d) for s, d, _ in outs],
        in_specs=in_specs,
        out_specs=[
            SCALARS if moves is None else by_step(s, steps) if moves else whole(s)
            for s, _, moves in outs
        ],
        scratch_shapes=[VMEM(s, d) for s, d in scratch],
        compiler_params=pltpu.CompilerParams(vmem_limit_bytes=56 * 2**20),
        cost_estimate=pl.CostEstimate(flops=int(cost * 1e9), bytes_accessed=2**20, transcendentals=0),
        name=name,
    )(*operands)


def local(
    tokens,
    cotangent,
    patches,
    lengths,
    group_member,
    mix,
    gain_one,
    w_query,
    w_key,
    w_value,
    w_out,
    gain_two,
    w_patch,
    bias_patch,
    w_cross_query,
    w_cross_key,
    w_cross_value,
    w_cross_out,
    gain_three,
    w_gate,
    w_up,
    w_down,
):
    seqs = lengths.shape[0]
    rows, width = tokens.shape
    maxlen = rows // seqs
    images, patch_dim = patches.shape[1], patches.shape[2]
    image_rows = seqs * images
    wide = w_gate.shape[1]
    steps = seqs // 2
    part = rows // steps
    flat = patches.reshape(image_rows, patch_dim)
    gain_one, gain_two, gain_three, bias_patch = (
        g.reshape(1, width) for g in (gain_one, gain_two, gain_three, bias_patch)
    )

    me = lax.axis_index("dp")
    me_ref = me[None].astype(jnp.int32)
    codes = jnp.stack(code_pair(me))
    feat, cross_kv, counts = run(
        features_kernel, "features", steps, [me_ref, lengths, group_member], [flat],
        [w_patch, bias_patch, w_cross_key, w_cross_value], "sssrffff",
        [((image_rows, width), BF16, True), ((image_rows, 2 * INNER), BF16, True), ((2,), F32, None)],
        [((width, 2 * INNER), BF16)], 5.1,
    )
    counts = counts + exchange(counts, 1)
    tokens_in, counts = lax.optimization_barrier((tokens, counts))
    counts = counts + exchange(counts, 2)
    h1, qkv, chances, mixed, x1, h2, cross_q = run(
        self_forward_kernel, "self_forward", steps, [lengths], [tokens_in],
        [gain_one, w_query, w_key, w_value, w_out, gain_two, w_cross_query], "srfffffff",
        [
            ((rows, width), BF16, True),
            ((rows, 3 * INNER), BF16, True),
            ((seqs, PAIRS, 2 * maxlen, maxlen), BF16, True),
            ((rows, INNER), BF16, True),
            ((rows, width), F32, True),
            ((rows, width), BF16, True),
            ((rows, INNER), BF16, True),
        ],
        [((width, 3 * INNER), BF16), ((width, INNER), BF16)], 6.0,
    )
    cross_q, counts = lax.optimization_barrier((cross_q, counts))
    counts = counts + exchange(counts, 4)
    cross_chances, cross_mixed, x2 = run(
        cross_forward_kernel, "cross_forward", steps, [], [cross_q, cross_kv, x1],
        [w_cross_out], "rrrf",
        [
            ((seqs, PAIRS, 2 * images, maxlen), BF16, True),
            ((rows, INNER), BF16, True),
            ((rows, width), F32, True),
        ],
        [], 6.0,
    )
    x2, counts = lax.optimization_barrier((x2, counts))
    counts = counts + exchange(counts, 8) + exchange(counts, 16) + exchange(counts, 24)
    bit = BLOCKS
    while bit < lax.axis_size("dp"):
        counts = counts + exchange(counts, bit)
        bit *= 2
    late_shapes = [w_down.shape, w_gate.shape, w_up.shape]
    late_rows = sum(block_rows(s) for s in late_shapes)
    hid, dgate, dup, *late = run(
        functools.partial(feed_forward_kernel, maxlen=maxlen), "feed_forward", steps,
        [lengths, codes], [x2, cotangent], [gain_three, w_gate, w_up, w_down], "ssrrffff",
        [((rows, wide), BF16, True)] * 3 + [((8, late_rows, 128), F32, False)] * 4,
        [
            ((rows, width), BF16),
            ((rows, width), BF16),
            ((rows, wide), BF16),
            ((rows, wide), BF16),
            ((rows, wide), BF16),
            (w_down.shape, F32),
            (w_gate.shape, F32),
            (w_up.shape, F32),
        ],
        14.0,
    )
    hid, counts, late = lax.optimization_barrier((hid, counts, late))
    late = Chunk(late, late_shapes, codes)
    late.send_cores()
    result, dx2, gain3, weights = run(
        functools.partial(feed_back_kernel, maxlen=maxlen), "feed_back", steps,
        [me_ref, lengths, group_member, mix, counts], [x2, cotangent, hid, dgate, dup],
        [gain_three, w_gate, w_up, w_down], "sssssrrrrrffff",
        [
            ((rows, width), BF16, True),
            ((rows, width), F32, True),
            ((1, width), F32, False),
            ((2,), F32, None),
        ],
        [], 8.0,
    )
    dx2 = fence(dx2, late)
    late.take_cores(weights)
    dx2 = fence(dx2, late)
    late.send_first()
    dcq, dkv, dfeat, dx1, dc, gain2, dbias = run(
        cross_backward_kernel, "cross_backward", steps, [],
        [dx2, cross_q, cross_chances, cross_kv, x1],
        [gain_two, w_cross_out, w_cross_query, w_cross_key, w_cross_value], "rrrrrfffff",
        [
            ((rows, INNER), BF16, True),
            ((image_rows, 2 * INNER), BF16, True),
            ((image_rows, width), BF16, True),
            ((rows, width), F32, True),
            ((rows, width), BF16, True),
            ((1, width), F32, False),
            ((1, width), F32, False),
        ],
        [((width, 2 * INNER), BF16)], 14.0,
    )
    dcq = fence(dcq, late)
    late.take_first()
    dcq = fence(dcq, late)
    late.send_second()
    cross_shapes = [w_cross_out.shape, w_cross_query.shape, w_cross_key.shape, w_cross_value.shape]
    cross_rows = sum(block_rows(s) for s in cross_shapes)
    cross = run(
        cross_weights_kernel, "cross_weights", 1, [codes], [],
        [cross_mixed, dc, h2, dcq, feat, dkv], "sffffff",
        [((8, cross_rows, 128), F32, False)] * 4,
        [(w_cross_out.shape, F32), (w_cross_query.shape, F32), ((width, 2 * INNER), F32)], 8.0,
    )
    cross = Chunk(fence(cross, late), cross_shapes, codes)
    late.take()
    fence((), cross, late)
    cross.send_cores()
    late.send_third()
    fence((), cross)
    cross.take_cores(weights)
    dx1 = fence(dx1, cross)
    cross.send_first()
    dqkv, da, grad_tokens, gain1 = run(
        self_backward_kernel, "self_backward", steps, [weights], [dx1, qkv, chances, tokens],
        [gain_one, w_out, w_query, w_key, w_value], "srrrrfffff",
        [
            ((rows, 3 * INNER), BF16, True),
            ((rows, width), BF16, True),
            ((rows, width), F32, True),
            ((1, width), F32, False),
        ],
        [((width, 3 * INNER), BF16)], 14.0,
    )
    dqkv = fence(dqkv, cross, late)
    late.take()
    cross.take_first()
    dqkv = fence(dqkv, cross, late)
    late.send_fourth()
    cross.send_second()
    own_shapes = [w_out.shape, w_query.shape, w_key.shape, w_value.shape, (BLOCKS * 8, 128)]
    own_rows = sum(block_rows(s) for s in own_shapes)
    own = run(
        self_weights_kernel, "self_weights", 1, [codes], [],
        [mixed, da, h1, dqkv, gain1, gain2, gain3, dbias], "sffffffff",
        [((8, own_rows, 128), F32, False)] * 4,
        [(w_out.shape, F32), ((width, 3 * INNER), F32), ((BLOCKS * 8, 128), F32)], 8.0,
    )
    own = Chunk(fence(own, late, cross), own_shapes, codes, True)
    late.take_fourth()
    cross.take()
    fence((), own, late, cross)
    own.send_cores()
    late.send_back_fourth()
    cross.send_third()
    fence((), own)
    own.take_cores(weights)
    dfeat = fence(dfeat, own)
    own.send_first()
    patch_shapes = [w_patch.shape]
    patch_rows = block_rows(w_patch.shape)
    patch = run(
        patch_weight_kernel, "patch_weight", steps, [codes], [flat, dfeat], [], "srr",
        [((8, patch_rows, 128), F32, False)] * 4,
        [((width, patch_dim), F32), ((patch_dim, width), F32)], 12.0,
    )
    patch = Chunk(fence(patch, own, cross, late), patch_shapes, codes)
    late.take_back()
    cross.take()
    own.take_first()
    fence((), patch, own, cross, late)
    patch.send_cores()
    late.send_back_third()
    cross.send_fourth()
    own.send_second()
    fence((), patch)
    patch.take_cores(weights)
    dfeat = fence(dfeat, patch)
    patch.send_first()
    (grad_patches,) = run(
        patch_input_kernel, "patch_input", 2 * steps, [weights], [dfeat], [w_patch], "srf",
        [((image_rows, patch_dim), F32, True)], [], 12.0,
    )
    grad_patches = fence(grad_patches, patch, own, cross, late)
    late.take_back()
    cross.take_fourth()
    own.take()
    patch.take_first()
    fence((), patch, own, cross, late)
    late.send_back_second()
    cross.send_back_fourth()
    own.send_third()
    patch.send_second()
    late.take_back()
    late.send_back_first()
    cross.take_back()
    cross.send_back_third()
    own.take()
    own.send_fourth()
    own.take_fourth()
    patch.take()
    patch.send_third()
    cross.take_back()
    cross.send_back_second()
    own.send_back_fourth()
    patch.take()
    patch.send_fourth()
    patch.take_fourth()
    late.send_back_cores()
    cross.take_back()
    cross.send_back_first()
    own.take_back()
    own.send_back_third()
    patch.send_back_fourth()
    patch.take_back()
    patch.send_back_third()
    own.take_back()
    own.send_back_second()
    cross.send_back_cores()
    patch.take_back()
    patch.send_back_second()
    own.take_back()
    own.send_back_first()
    patch.take_back()
    late = fence(late.unpack(), patch)
    patch.send_back_first()
    own.send_back_cores()
    cross = cross.unpack()
    own = own.unpack()
    cross, own, late = fence((cross, own, late), patch)
    patch.send_back_cores()
    patch = patch.unpack()
    gains = [g.reshape(width) for g in own[5:]]
    return (
        result,
        grad_tokens,
        grad_patches.reshape(seqs, images, patch_dim),
        gains[0],
        own[1],
        own[2],
        own[3],
        own[0],
        gains[1],
        patch[0],
        gains[3],
        cross[1],
        cross[2],
        cross[3],
        cross[0],
        gains[2],
        late[1],
        late[2],
        late[0],
    )


def solution(mesh):
    split = P("dp", None)
    images = P("dp", None, None)
    return jax.shard_map(
        local,
        mesh=mesh,
        in_specs=(split, split, images, P("dp")) + (P(),) * 18,
        out_specs=(split, split, images) + (P(),) * 16,
        check_vma=False,
    )
```

```python
import functools

import jax
import jax.numpy as jnp
from jax import lax
from jax.experimental import pallas as pl
from jax.experimental.pallas import tpu as pltpu
from jax.sharding import PartitionSpec as P

HEADS = 6
HEAD_DIM = 64
PAIRS = HEADS // 2
PAIR = 2 * HEAD_DIM
INNER = HEADS * HEAD_DIM
BLOCKS = 32
HALF = 16
EPSILON = 1e-06
F32 = jnp.float32
BF16 = jnp.bfloat16
VMEM = pltpu.VMEM
SMEM = pltpu.SMEM


def dot_plain(left_op, right_op):
    return jnp.dot(left_op, right_op, preferred_element_type=F32)


def dot_rows(left_op, right_op):
    return lax.dot_general(left_op, right_op, (((0,), (0,)), ((), ())), preferred_element_type=F32)


def dot_back(left_op, right_op):
    return lax.dot_general(left_op, right_op, (((1,), (1,)), ((), ())), preferred_element_type=F32)


def inverse_rms(values):
    return lax.rsqrt(jnp.mean(values * values, axis=-1, keepdims=True) + EPSILON)


def norm_backward(values, gain, grad):
    inverse = inverse_rms(values)
    unit = values * inverse
    scaled = grad * gain
    along = jnp.mean(scaled * unit, axis=-1, keepdims=True)
    return inverse * (scaled - unit * along), jnp.sum(grad * unit, axis=0, keepdims=True)


def lane_masks():
    lane = lax.broadcasted_iota(jnp.int32, (1, PAIR), 1)
    first = jnp.where(lane < HEAD_DIM, 1.0, 0.0)
    return first.astype(BF16), (1.0 - first).astype(BF16)


def stack_heads(values):
    first, second = lane_masks()
    return jnp.concatenate([values * first, values * second], axis=0)


def fold_heads(values):
    half = values.shape[0] // 2
    lane = lax.broadcasted_iota(jnp.int32, (half, PAIR), 1)
    return jnp.where(lane < HEAD_DIM, values[:half], values[half:])


def pair_forward(queries, key_rows, value_rows, allowed):
    keys = key_rows.shape[0]
    scores = dot_back(stack_heads(key_rows), queries).reshape(2, keys, queries.shape[0])
    if allowed is not None:
        scores = jnp.where(allowed, scores, -1000000000.0)
    expo = jnp.exp(scores - jnp.max(scores, axis=1, keepdims=True))
    chances = expo * (1.0 / jnp.sum(expo, axis=1, keepdims=True))
    chances = chances.reshape(2 * keys, queries.shape[0]).astype(BF16)
    return chances, dot_rows(chances, stack_heads(value_rows)).astype(BF16)


def pair_backward(queries, key_rows, value_rows, chances, grad_mixed):
    keys, count = key_rows.shape[0], queries.shape[0]
    wide = chances.astype(F32)
    grad_chances = dot_back(stack_heads(value_rows), grad_mixed)
    product = wide * grad_chances
    inner = jnp.sum(product.reshape(2, keys, count), axis=1, keepdims=True)
    spread = (wide.reshape(2, keys, count) * inner).reshape(2 * keys, count)
    grad_scores = (product - spread).astype(BF16)
    grad_values = fold_heads(dot_plain(chances, grad_mixed))
    grad_keys = fold_heads(dot_plain(grad_scores, queries))
    grad_queries = dot_rows(grad_scores, stack_heads(key_rows)) * 0.125
    return grad_queries.astype(BF16), grad_keys.astype(BF16), grad_values.astype(BF16)


def pair_lanes(index, offset=0):
    return pl.ds(offset + index * PAIR, PAIR)


def count_kernel(me_ref, len_ref, member_ref, count_ref, code_ref):
    me = me_ref[0]
    count = sum(len_ref[s] for s in range(len_ref.shape[0])).astype(F32)
    in_first = member_ref[me] == 1
    count_ref[0] = jnp.where(in_first, count, 0.0)
    count_ref[1] = jnp.where(in_first, 0.0, count)
    code_ref[0], code_ref[1] = code_pair(me)


def weigh_kernel(me_ref, member_ref, mix_ref, *refs):
    me = me_ref[0]
    parts, (weight_ref, own_ref, other_ref) = refs[:-3], refs[-3:]
    count_one = sum(part[0] for part in parts)
    count_two = sum(part[1] for part in parts)
    total = count_one + count_two
    first = mix_ref[0] * total / count_one
    second = mix_ref[1] * total / count_two
    own = jnp.where(member_ref[me] == 1, first, second)
    other = jnp.where(member_ref[me ^ 1] == 1, first, second)
    weight_ref[0], weight_ref[1] = own, other
    own_ref[...] = jnp.full(own_ref.shape, own)
    other_ref[...] = jnp.full(other_ref.shape, other)


def add_to(ref, first, value):
    @pl.when(first)
    def fresh():
        ref[...] = value

    @pl.when(jnp.logical_not(first))
    def more():
        ref[...] += value


def gelu_parts(gate):
    slant = 0.7978845608028654
    square = gate * gate
    tanh = jnp.tanh(gate * (slant + (slant * 0.044715) * square))
    half = 0.5 + 0.5 * tanh
    slope = half + (0.5 * gate) * (1.0 - tanh * tanh) * (slant + (3.0 * slant * 0.044715) * square)
    return gate * half, slope


def forward_kernel(
    len_ref, code_ref,
    patch_ref, tok_ref, cot_ref,
    wp_ref, bias_ref, wck_ref, wcv_ref,
    g1_ref, wq_ref, wk_ref, wv_ref, wo_ref, g2_ref, wcq_ref, wco_ref, g3_ref, wg_ref, wu_ref, wd_ref,
    feat_ref, kv_ref, qkv_ref, pt_ref, o_ref, x1_ref, cq_ref, pc_ref, oc_ref,
    out_ref, dx2_ref, gain_ref, keep_low, keep_high, send_low, send_high,
    join_kv, join_qkv, wcq, h3_all, de_all, hid_all, dgate_all, dup_all, acc_down, acc_gate, acc_up,
):
    step, steps = pl.program_id(0), pl.num_programs(0)

    @pl.when(step == 0)
    def join():
        join_kv[:, :INNER] = wck_ref[...]
        join_kv[:, INNER:] = wcv_ref[...]
        join_qkv[:, :INNER] = wq_ref[...] * 0.125
        join_qkv[:, INNER : 2 * INNER] = wk_ref[...]
        join_qkv[:, 2 * INNER :] = wv_ref[...]
        wcq[...] = wcq_ref[...] * 0.125

    seqs, _, _, maxlen = pt_ref.shape
    patches = pc_ref.shape[2] // 2
    feat = (dot_plain(patch_ref[...], wp_ref[...]) + bias_ref[...]).astype(BF16)
    feat_ref[...] = feat
    kv_ref[...] = dot_plain(feat, join_kv[...]).astype(BF16)
    x = tok_ref[...].astype(F32)
    h1 = (x * inverse_rms(x) * g1_ref[...]).astype(BF16)
    qkv_ref[...] = dot_plain(h1, join_qkv[...]).astype(BF16)
    key_at = lax.broadcasted_iota(jnp.int32, (1, maxlen, maxlen), 1)
    query_at = lax.broadcasted_iota(jnp.int32, (1, maxlen, maxlen), 2)
    for s in range(seqs):
        rows = pl.ds(s * maxlen, maxlen)
        allowed = (key_at <= query_at) & (key_at < len_ref[step * seqs + s])
        for p in range(PAIRS):
            pt_ref[s, p], o_ref[rows, pair_lanes(p)] = pair_forward(
                qkv_ref[rows, pair_lanes(p)],
                qkv_ref[rows, pair_lanes(p, INNER)],
                qkv_ref[rows, pair_lanes(p, 2 * INNER)],
                allowed,
            )
    x1 = x + dot_plain(o_ref[...], wo_ref[...])
    x1_ref[...] = x1
    h2 = (x1 * inverse_rms(x1) * g2_ref[...]).astype(BF16)
    cq_ref[...] = dot_plain(h2, wcq[...]).astype(BF16)
    for s in range(seqs):
        rows, wide = pl.ds(s * maxlen, maxlen), pl.ds(s * patches, patches)
        for p in range(PAIRS):
            pc_ref[s, p], oc_ref[rows, pair_lanes(p)] = pair_forward(
                cq_ref[rows, pair_lanes(p)],
                kv_ref[wide, pair_lanes(p)],
                kv_ref[wide, pair_lanes(p, INNER)],
                None,
            )
    x2 = x1_ref[...] + dot_plain(oc_ref[...], wco_ref[...])
    h3 = (x2 * inverse_rms(x2) * g3_ref[...]).astype(BF16)
    at = lax.broadcasted_iota(jnp.int32, (maxlen, 1), 0)
    keep = jnp.concatenate(
        [jnp.where(at < len_ref[step * seqs + s], 1.0, 0.0) for s in range(seqs)], axis=0
    )
    e = cot_ref[...].astype(F32) * keep
    de = e.astype(BF16)
    count = x2.shape[0]
    here = pl.ds(pl.multiple_of(step * count, count), count)
    h3_all[here, :] = h3
    de_all[here, :] = de
    span = wg_ref.shape[1]
    chunk = 256
    for c in range(span // chunk):
        cols = pl.ds(c * chunk, chunk)
        gate = dot_plain(h3, wg_ref[:, cols])
        up = dot_plain(h3, wu_ref[:, cols])
        grad = dot_back(de, wd_ref[cols, :])
        gelu, slope = gelu_parts(gate)
        hid = (gelu * up).astype(BF16)
        dgate = (grad * up * slope).astype(BF16)
        dup = (grad * gelu).astype(BF16)
        hid_all[here, cols] = hid
        dgate_all[here, cols] = dgate
        dup_all[here, cols] = dup

    out_ref[...] = (x2 + dot_plain(hid_all[here, :], wd_ref[...])).astype(BF16)
    dh3 = dot_back(dgate_all[here, :], wg_ref[...]) + dot_back(dup_all[here, :], wu_ref[...])
    dx, gain = norm_backward(x2, g3_ref[...], dh3)
    dx2_ref[...] = e + dx
    add_to(gain_ref, step == 0, gain)

    @pl.when(step == steps - 1)
    def finish():
        for c in range(span // chunk):
            cols = pl.ds(c * chunk, chunk)
            acc_down[cols, :] = dot_rows(hid_all[:, cols], de_all[...])
            acc_gate[:, cols] = dot_rows(h3_all[...], dgate_all[:, cols])
            acc_up[:, cols] = dot_rows(h3_all[...], dup_all[:, cols])
        items = [(acc_down, acc_down.shape, 0), (acc_gate, acc_gate.shape, 0), (acc_up, acc_up.shape, 0)]
        pack(items, code_ref, keep_low, keep_high, send_low, send_high)


def cross_backward_kernel(
    code_ref, dx2_ref, cq_ref, pt_ref, kv_ref, x1_ref, oc_ref, feat_ref,
    g2_ref, wco_ref, wcq_ref, wck_ref, wcv_ref,
    dfeat_ref, dx1_ref, gain_ref, bias_ref, keep_low, keep_high, send_low, send_high,
    joined, dcq_all, dkv_all, dc_all, h2_all, oc_all, feat_all, acc_out, acc_query, acc_kv,
):
    step, steps = pl.program_id(0), pl.num_programs(0)

    @pl.when(step == 0)
    def join():
        joined[:, :INNER] = wck_ref[...]
        joined[:, INNER:] = wcv_ref[...]

    seqs, _, both, maxlen = pt_ref.shape
    patches = both // 2
    count, wide_count = seqs * maxlen, seqs * patches
    here = pl.ds(pl.multiple_of(step * count, count), count)
    wide_here = pl.ds(pl.multiple_of(step * wide_count, wide_count), wide_count)
    dx2 = dx2_ref[...]
    dc = dx2.astype(BF16)
    dc_all[here, :] = dc
    oc_all[here, :] = oc_ref[...]
    feat_all[wide_here, :] = feat_ref[...]
    doc = dot_back(dc, wco_ref[...]).astype(BF16)
    for s in range(seqs):
        rows, wide = pl.ds(s * maxlen, maxlen), pl.ds(s * patches, patches)
        at = pl.ds(pl.multiple_of(step * count + s * maxlen, maxlen), maxlen)
        wide_at = pl.ds(pl.multiple_of(step * wide_count + s * patches, patches), patches)
        for p in range(PAIRS):
            keys, values = pair_lanes(p), pair_lanes(p, INNER)
            dcq_all[at, keys], dkv_all[wide_at, keys], dkv_all[wide_at, values] = pair_backward(
                cq_ref[rows, keys],
                kv_ref[wide, keys],
                kv_ref[wide, values],
                pt_ref[s, p],
                doc[s * maxlen : (s + 1) * maxlen, p * PAIR : (p + 1) * PAIR],
            )
    dfeat = dot_back(dkv_all[wide_here, :], joined[...]).astype(BF16)
    dfeat_ref[...] = dfeat
    dh2 = dot_back(dcq_all[here, :], wcq_ref[...])
    x1 = x1_ref[...]
    h2_all[here, :] = (x1 * inverse_rms(x1) * g2_ref[...]).astype(BF16)
    dx, gain = norm_backward(x1, g2_ref[...], dh2)
    dx1_ref[...] = dx2 + dx
    add_to(gain_ref, step == 0, gain)
    add_to(bias_ref, step == 0, jnp.sum(dfeat.astype(F32), axis=0, keepdims=True))

    @pl.when(step == steps - 1)
    def finish():
        acc_out[...] = dot_rows(oc_all[...], dc_all[...])
        acc_query[...] = dot_rows(h2_all[...], dcq_all[...])
        acc_kv[...] = dot_rows(feat_all[...], dkv_all[...])
        small = acc_query.shape
        items = [(acc_out, acc_out.shape, 0), (acc_query, small, 0)]
        items += [(acc_kv, small, 0), (acc_kv, small, INNER)]
        pack(items, code_ref, keep_low, keep_high, send_low, send_high)


def patch_weight_kernel(code_ref, patch_ref, dfeat_ref, keep_low, keep_high, send_low, send_high, acc, turned):
    step, steps = pl.program_id(0), pl.num_programs(0)
    add_to(acc, step == 0, dot_rows(dfeat_ref[...], patch_ref[...]))

    @pl.when(step == steps - 1)
    def finish():
        turned[...] = acc[...].T
        pack([(turned, turned.shape, 0)], code_ref, keep_low, keep_high, send_low, send_high)


def patch_input_kernel(weight_ref, dfeat_ref, w_ref, *refs):
    refs[-1][...] = dot_back(dfeat_ref[...], w_ref[...]) * weight_ref[0]


def self_backward_kernel(
    code_ref, weight_ref, dx1_ref, qkv_ref, pt_ref, tok_ref, o_ref,
    g1_ref, wo_ref, wq_ref, wk_ref, wv_ref, gain_two_ref, gain_three_ref, bias_ref,
    dtok_ref, keep_low, keep_high, send_low, send_high,
    joined, dqkv_all, da_all, h1_all, o_all, acc_out, acc_qkv, gain_one, gain_block,
):
    step, steps = pl.program_id(0), pl.num_programs(0)

    @pl.when(step == 0)
    def join():
        joined[:, :INNER] = wq_ref[...]
        joined[:, INNER : 2 * INNER] = wk_ref[...]
        joined[:, 2 * INNER :] = wv_ref[...]

    seqs, _, _, maxlen = pt_ref.shape
    count = seqs * maxlen
    here = pl.ds(pl.multiple_of(step * count, count), count)
    dx1 = dx1_ref[...]
    da = dx1.astype(BF16)
    da_all[here, :] = da
    o_all[here, :] = o_ref[...]
    do = dot_back(da, wo_ref[...]).astype(BF16)
    for s in range(seqs):
        rows = pl.ds(s * maxlen, maxlen)
        at = pl.ds(pl.multiple_of(step * count + s * maxlen, maxlen), maxlen)
        for p in range(PAIRS):
            lanes = [pair_lanes(p, k * INNER) for k in range(3)]
            dqkv_all[at, lanes[0]], dqkv_all[at, lanes[1]], dqkv_all[at, lanes[2]] = pair_backward(
                qkv_ref[rows, lanes[0]],
                qkv_ref[rows, lanes[1]],
                qkv_ref[rows, lanes[2]],
                pt_ref[s, p],
                do[s * maxlen : (s + 1) * maxlen, p * PAIR : (p + 1) * PAIR],
            )
    dh1 = dot_back(dqkv_all[here, :], joined[...])
    x = tok_ref[...].astype(F32)
    h1_all[here, :] = (x * inverse_rms(x) * g1_ref[...]).astype(BF16)
    dx, gain = norm_backward(x, g1_ref[...], dh1)
    dtok_ref[...] = (dx1 + dx) * weight_ref[0]
    add_to(gain_one, step == 0, gain)

    @pl.when(step == steps - 1)
    def finish():
        acc_out[...] = dot_rows(o_all[...], da_all[...])
        acc_qkv[...] = dot_rows(h1_all[...], dqkv_all[...])
        gain_block[...] = jnp.zeros_like(gain_block)
        for k, ref in enumerate((gain_one, gain_two_ref, gain_three_ref, bias_ref)):
            for t in range(4):
                gain_block[pl.ds((4 * k + t) * 8, 1), :] = ref[:, pl.ds(t * 128, 128)]
        small = (acc_qkv.shape[0], INNER)
        items = [(acc_out, acc_out.shape, 0)]
        items += [(acc_qkv, small, k * INNER) for k in range(3)]
        items += [(gain_block, gain_block.shape, 0)]
        pack(items, code_ref, keep_low, keep_high, send_low, send_high)


def flips(count, first, second):
    return [(i, i ^ (first if i % 2 == 0 else second)) for i in range(count)]


def code_pair(me):
    core, ex, why = me & 1, (me >> 1) & 1, (me >> 2) & 1
    near, far = (me >> 3) & 1, (me >> 4) & 1
    even = ex * 8 + why * 4 + near * 2 + far
    odd = why * 8 + ex * 4 + far * 2 + near
    own = core * 16 + jnp.where(core == 0, even, odd)
    other = (1 - core) * 16 + jnp.where(core == 0, odd, even)
    return own, other


def exchange(values, first, second=None):
    count = lax.axis_size("dp")
    return lax.ppermute(values, "dp", flips(count, first, first if second is None else second))


def block_rows(shape):
    return shape[0] * shape[1] // (BLOCKS * 128)


def block_parts(shape, index, offset):
    rows, lanes = shape
    tiles = lanes // 128
    if BLOCKS % tiles:
        height = rows // BLOCKS
        return [
            (pl.ds(pl.multiple_of(index * height, 8), height), pl.ds(offset + t * 128, 128))
            for t in range(tiles)
        ]
    height = rows * tiles // BLOCKS
    row, lane = index // tiles, index % tiles
    return [
        (
            pl.ds(pl.multiple_of(row * height, 8), height),
            pl.ds(pl.multiple_of(offset + lane * 128, 128), 128),
        )
    ]


def pack(items, code_ref, *out_refs):
    def step(p, carry):
        for k, out_ref in enumerate(out_refs):
            start = 0
            index = (p + 8 * (k % 2)) ^ code_ref[k // 2]
            for ref, shape, offset in items:
                for rows, lanes in block_parts(shape, index, offset):
                    out_ref[p, pl.ds(start, rows.size), :] = ref[rows, lanes]
                    start += rows.size
        return carry

    lax.fori_loop(0, 8, step, 0)


def unpack_kernel(shapes, with_gains, code_ref, *refs):
    ins, outs = refs[:4], refs[4:]
    for k, piece in enumerate(ins):

        def step(p, carry, piece=piece, k=k):
            index = (p + 8 * (k % 2)) ^ code_ref[k // 2]
            start = 0
            for shape, out_ref in zip(shapes, outs):
                for rows, lanes in block_parts(shape, index, 0):
                    out_ref[rows, lanes] = piece[p, pl.ds(start, rows.size), :]
                    start += rows.size
            return carry

        lax.fori_loop(0, 8, step, 0)
    if with_gains:
        count = len(shapes)
        block = outs[count - 1]
        for k, out_ref in enumerate(outs[count:]):
            for t in range(4):
                out_ref[:, pl.ds(t * 128, 128)] = block[pl.ds((4 * k + t) * 8, 1), :]


def vmem(count):
    return [pl.BlockSpec(memory_space=VMEM)] * count


def unpack(pieces, shapes, codes, with_gains=False):
    outs = [jax.ShapeDtypeStruct(s, F32) for s in shapes]
    if with_gains:
        outs += [jax.ShapeDtypeStruct((1, 512), F32)] * 4
    return pl.pallas_call(
        functools.partial(unpack_kernel, shapes, with_gains),
        out_shape=outs,
        in_specs=[pl.BlockSpec(memory_space=SMEM)] + vmem(4),
        out_specs=vmem(len(outs)),
        compiler_params=pltpu.CompilerParams(vmem_limit_bytes=40 * 2**20),
        name="unpack",
    )(codes, *pieces)


class Chunk:
    def __init__(self, packed, shapes, codes, weights=None, with_gains=False):
        self.held, self.got, self.stage = tuple(packed), (), 0
        self.shapes, self.codes, self.weights, self.with_gains = shapes, codes, weights, with_gains

    def advance(self, token):
        (self.held, self.got), token = lax.optimization_barrier(((self.held, self.got), token))
        take, send = STAGES[self.stage]
        self.stage += 1
        if take is not None:
            take(self)
        send(self)
        return self.held[0]

    def send_cores(self):
        _, _, low, high = self.held
        self.got = (exchange(high, 1), exchange(low, 1))

    def take_cores(self):
        keep_low, keep_high, _, _ = self.held
        high, low = self.got
        self.held = (keep_high * self.weights[0] + high * self.weights[1], keep_low)
        self.got = (low,)

    def send_first(self):
        self.got += (exchange(self.held[0], 2, 4),)

    def take_first(self):
        (_, keep), (low, got) = self.held, self.got
        keep = keep * self.weights[0] + low * self.weights[1]
        self.held = (keep[4:] + got[4:], keep[:4] + got[:4])

    def take_half(self):
        (_, keep), (got,) = self.held, self.got
        half = keep.shape[0] // 2
        self.held = (keep[half:] + got[half:], keep[:half] + got[:half])

    def take_last(self):
        total = self.held[1] + self.got[0]
        extra = BLOCKS
        while extra < lax.axis_size("dp"):
            total = total + exchange(total, extra)
            extra *= 2
        self.held = (total,)

    def take_back(self):
        self.held = (jnp.concatenate([*self.held, *self.got]),)

    def send_second(self):
        self.got = (exchange(self.held[0], 4, 2),)

    def send_third(self):
        self.got = (exchange(self.held[0], 8, 16),)

    def send_fourth(self):
        self.got = (exchange(self.held[0], 16, 8),)

    def send_back_first(self):
        self.got = (exchange(self.held[0], 2, 4), exchange(self.held[0], 1))

    def send_back_cores(self):
        self.held = (self.held[0], *self.got)
        self.got = (exchange(self.held[1], 1),)

    def unpack(self, token):
        (held, got), token = lax.optimization_barrier(((self.held, self.got), token))
        return unpack(held + got, self.shapes, self.codes, self.with_gains)


STAGES = (
    (None, Chunk.send_cores),
    (Chunk.take_cores, Chunk.send_first),
    (Chunk.take_first, Chunk.send_second),
    (Chunk.take_half, Chunk.send_third),
    (Chunk.take_half, Chunk.send_fourth),
    (Chunk.take_last, Chunk.send_fourth),
    (Chunk.take_back, Chunk.send_third),
    (Chunk.take_back, Chunk.send_second),
    (Chunk.take_back, Chunk.send_back_first),
    (None, Chunk.send_back_cores),
)


def by_step(array_shape, steps):
    block = (array_shape[0] // steps,) + tuple(array_shape[1:])
    return pl.BlockSpec(block, lambda i: (i,) + (0,) * (len(block) - 1))


def whole(array_shape):
    return pl.BlockSpec(tuple(array_shape), lambda i: (0,) * len(array_shape))


SCALARS = pl.BlockSpec(memory_space=SMEM)


def run_small(kernel, name, operands, outs, ins=None):
    return pl.pallas_call(
        kernel,
        out_shape=[jax.ShapeDtypeStruct(s, d) for s, d, _ in outs],
        in_specs=ins or [SCALARS] * len(operands),
        out_specs=[spec for _, _, spec in outs],
        name=name,
    )(*operands)


def run(kernel, name, steps, scalars, stepped, fixed, order, outs, scratch, cost):
    lists = {"s": iter(scalars), "r": iter(stepped), "f": iter(fixed)}
    operands = [next(lists[c]) for c in order]
    in_specs = [
        SCALARS if c == "s" else by_step(v.shape, steps) if c == "r" else whole(v.shape)
        for c, v in zip(order, operands)
    ]
    return pl.pallas_call(
        kernel,
        grid=(steps,),
        out_shape=[jax.ShapeDtypeStruct(s, d) for s, d, _ in outs],
        in_specs=in_specs,
        out_specs=[
            SCALARS if moves is None else by_step(s, steps) if moves else whole(s)
            for s, _, moves in outs
        ],
        scratch_shapes=[VMEM(s, d) for s, d in scratch],
        compiler_params=pltpu.CompilerParams(vmem_limit_bytes=56 * 2**20),
        cost_estimate=pl.CostEstimate(flops=int(cost * 1e9), bytes_accessed=2**20, transcendentals=0),
        name=name,
    )(*operands)


def local(
    tokens,
    cotangent,
    patches,
    lengths,
    group_member,
    mix,
    gain_one,
    w_query,
    w_key,
    w_value,
    w_out,
    gain_two,
    w_patch,
    bias_patch,
    w_cross_query,
    w_cross_key,
    w_cross_value,
    w_cross_out,
    gain_three,
    w_gate,
    w_up,
    w_down,
):
    seqs = lengths.shape[0]
    rows, width = tokens.shape
    maxlen = rows // seqs
    images, patch_dim = patches.shape[1], patches.shape[2]
    image_rows = seqs * images
    wide = w_gate.shape[1]
    steps = seqs // 2
    part = rows // steps
    flat = patches.reshape(image_rows, patch_dim)
    gain_one, gain_two, gain_three, bias_patch = (
        g.reshape(1, width) for g in (gain_one, gain_two, gain_three, bias_patch)
    )

    me_ref = lax.axis_index("dp")[None].astype(jnp.int32)
    in_vmem = pl.BlockSpec(memory_space=VMEM)
    counts, codes = run_small(
        count_kernel, "count", [me_ref, lengths, group_member],
        [((2,), F32, SCALARS), ((2,), jnp.int32, SCALARS)],
    )
    devices = lax.axis_size("dp")
    counts = counts + exchange(counts, 1)
    flat, counts = lax.optimization_barrier((flat, counts))
    column = [counts] + [exchange(counts, bit) for bit in (8, 16, 24)]
    late_shapes = [w_down.shape, w_gate.shape, w_up.shape]
    late_rows = sum(block_rows(s) for s in late_shapes)
    (
        feat, cross_kv, qkv, chances, mixed, x1, cross_q, cross_chances, cross_mixed, result, dx2, gain3, *late
    ) = run(
        forward_kernel, "forward", steps, [lengths, codes], [flat, tokens, cotangent],
        [
            w_patch, bias_patch, w_cross_key, w_cross_value,
            gain_one, w_query, w_key, w_value, w_out, gain_two, w_cross_query, w_cross_out,
            gain_three, w_gate, w_up, w_down,
        ],
        "ssrrr" + "f" * 16,
        [
            ((image_rows, width), BF16, True),
            ((image_rows, 2 * INNER), BF16, True),
            ((rows, 3 * INNER), BF16, True),
            ((seqs, PAIRS, 2 * maxlen, maxlen), BF16, True),
            ((rows, INNER), BF16, True),
            ((rows, width), F32, True),
            ((rows, INNER), BF16, True),
            ((seqs, PAIRS, 2 * images, maxlen), BF16, True),
            ((rows, INNER), BF16, True),
            ((rows, width), BF16, True),
            ((rows, width), F32, True),
            ((1, width), F32, False),
        ] + [((8, late_rows, 128), F32, False)] * 4,
        [
            ((width, 2 * INNER), BF16),
            ((width, 3 * INNER), BF16),
            ((width, INNER), BF16),
            ((rows, width), BF16),
            ((rows, width), BF16),
            ((rows, wide), BF16),
            ((rows, wide), BF16),
            ((rows, wide), BF16),
            (w_down.shape, F32),
            (w_gate.shape, F32),
            (w_up.shape, F32),
        ],
        40.0,
    )
    late, column = lax.optimization_barrier((late, column))
    late = Chunk(late, late_shapes, codes)
    token = late.advance(dx2)
    column, token = lax.optimization_barrier((column, token))
    counts = sum(column)
    bit = BLOCKS
    while bit < devices:
        counts = counts + exchange(counts, bit)
        bit *= 2
    counts = counts + exchange(counts, 2)
    parts = [counts, exchange(counts, 4)]
    row = (1, 1, 128)
    weights, *rows_of_weights = run_small(
        weigh_kernel, "weigh", [me_ref, group_member, mix, *parts],
        [((2,), F32, SCALARS), (row, F32, in_vmem), (row, F32, in_vmem)],
    )
    late.weights = rows_of_weights
    token = weights

    def cross_backward(token):
        tied, token = lax.optimization_barrier((dx2, token))
        cross_shapes = [w_cross_out.shape, w_cross_query.shape, w_cross_key.shape, w_cross_value.shape]
        cross_rows = sum(block_rows(s) for s in cross_shapes)
        dfeat, dx1, gain2, dbias, *cross = run(
            cross_backward_kernel, "cross_backward", steps, [codes],
            [tied, cross_q, cross_chances, cross_kv, x1, cross_mixed, feat],
            [gain_two, w_cross_out, w_cross_query, w_cross_key, w_cross_value], "srrrrrrrfffff",
            [
                ((image_rows, width), BF16, True),
                ((rows, width), F32, True),
                ((1, width), F32, False),
                ((1, width), F32, False),
            ] + [((8, cross_rows, 128), F32, False)] * 4,
            [
                ((width, 2 * INNER), BF16),
                ((rows, INNER), BF16),
                ((image_rows, 2 * INNER), BF16),
                ((rows, width), BF16),
                ((rows, width), BF16),
                ((rows, INNER), BF16),
                ((image_rows, width), BF16),
                (w_cross_out.shape, F32),
                (w_cross_query.shape, F32),
                ((width, 2 * INNER), F32),
            ],
            20.0,
        )
        return (dfeat, dx1, gain2, dbias), Chunk(cross, cross_shapes, codes, late.weights)

    def self_backward(token, dx1, gain2, dbias):
        tied, token = lax.optimization_barrier((dx1, token))
        own_shapes = [w_out.shape, w_query.shape, w_key.shape, w_value.shape, (BLOCKS * 8, 128)]
        own_rows = sum(block_rows(s) for s in own_shapes)
        grad_tokens, *own = run(
            self_backward_kernel, "self_backward", steps, [codes, weights],
            [tied, qkv, chances, tokens, mixed],
            [gain_one, w_out, w_query, w_key, w_value, gain2, gain3, dbias], "ssrrrrr" + "f" * 8,
            [((rows, width), F32, True)] + [((8, own_rows, 128), F32, False)] * 4,
            [
                ((width, 3 * INNER), BF16),
                ((rows, 3 * INNER), BF16),
                ((rows, width), BF16),
                ((rows, width), BF16),
                ((rows, INNER), BF16),
                (w_out.shape, F32),
                ((width, 3 * INNER), F32),
                ((1, width), F32),
                ((BLOCKS * 8, 128), F32),
            ],
            16.0,
        )
        return grad_tokens, Chunk(own, own_shapes, codes, late.weights, True)

    def patch_weight(token, dfeat):
        tied, token = lax.optimization_barrier((dfeat, token))
        patch_shapes = [w_patch.shape]
        patch_rows = block_rows(w_patch.shape)
        patch = run(
            patch_weight_kernel, "patch_weight", steps, [codes], [flat, tied], [], "srr",
            [((8, patch_rows, 128), F32, False)] * 4,
            [((width, patch_dim), F32), ((patch_dim, width), F32)], 12.0,
        )
        return Chunk(patch, patch_shapes, codes, late.weights)

    def patch_input(token, dfeat, half, out):
        tied, token = lax.optimization_barrier((dfeat, token))
        return pl.pallas_call(
            patch_input_kernel,
            grid=(steps,),
            out_shape=jax.ShapeDtypeStruct((image_rows, patch_dim), F32),
            in_specs=[
                SCALARS,
                pl.BlockSpec((image_rows // (2 * steps), width), lambda i: (i + half * steps, 0)),
                whole(w_patch.shape),
            ]
            + [pl.BlockSpec(memory_space=pl.ANY)] * len(out),
            out_specs=pl.BlockSpec((image_rows // (2 * steps), patch_dim), lambda i: (i + half * steps, 0)),
            input_output_aliases={3: 0} if out else {},
            compiler_params=pltpu.CompilerParams(vmem_limit_bytes=32 * 2**20),
            cost_estimate=pl.CostEstimate(flops=6 * 10**9, bytes_accessed=2**20, transcendentals=0),
            name="patch_input",
        )(weights, tied, w_patch, *out)

    chunks, done, grad_patches = {"late": late}, {}, ()
    for name in (
        "late", "cross kernel", "late", "cross", "self kernel", "cross", "own", "late",
        "patch kernel", "late", "own", "patch", "cross", "patch", "late", "input kernel",
        "cross", "own", "late", "input kernel", "cross", "patch", "own", "late", "cross",
        "patch", "own", "cross", "late", "patch", "own", "cross", "patch", "own", "cross",
        "late", "patch", "own", "late", "cross", "patch", "own", "cross", "patch", "own", "own",
        "patch", "patch",
    ):
        if name == "cross kernel":
            (dfeat, dx1, gain2, dbias), chunks["cross"] = cross_backward(token)
            token = dx1
        elif name == "self kernel":
            grad_tokens, chunks["own"] = self_backward(token, dx1, gain2, dbias)
            token = grad_tokens
        elif name == "patch kernel":
            chunks["patch"] = patch_weight(token, dfeat)
            token = chunks["patch"].held
        elif name == "input kernel":
            half = len(grad_patches)
            grad_patches = (patch_input(token, dfeat, half, grad_patches),)
            token = grad_patches
        elif chunks[name].stage < len(STAGES):
            token = chunks[name].advance(token)
        else:
            done[name] = chunks[name].unpack(token)
            token = done[name]
    (grad_patches,) = grad_patches
    late, cross, own, patch = (done[name] for name in ("late", "cross", "own", "patch"))
    gains = [g.reshape(width) for g in own[5:]]
    return (
        result,
        grad_tokens,
        grad_patches.reshape(seqs, images, patch_dim),
        gains[0],
        own[1],
        own[2],
        own[3],
        own[0],
        gains[1],
        patch[0],
        gains[3],
        cross[1],
        cross[2],
        cross[3],
        cross[0],
        gains[2],
        late[1],
        late[2],
        late[0],
    )


def solution(mesh):
    split = P("dp", None)
    images = P("dp", None, None)
    return jax.shard_map(
        local,
        mesh=mesh,
        in_specs=(split, split, images, P("dp")) + (P(),) * 18,
        out_specs=(split, split, images) + (P(),) * 16,
        check_vma=False,
    )
```

```python
import functools

import jax
import jax.numpy as jnp
from jax import lax
from jax.experimental import pallas as pl
from jax.experimental.pallas import tpu as pltpu
from jax.sharding import PartitionSpec as P

HEADS = 6
HEAD_DIM = 64
PAIRS = HEADS // 2
PAIR = 2 * HEAD_DIM
INNER = HEADS * HEAD_DIM
BLOCKS = 32
HALF = 16
EPSILON = 1e-06
F32 = jnp.float32
BF16 = jnp.bfloat16
PLACES = {"late": 0, "cross": 2, "own": 4, "patch": 6}
AXES = {
    "late": ((1, 2, 3, 4), (2, 1, 4, 3)),
    "cross": ((1, 2, 3, 4), (2, 1, 4, 3)),
    "own": ((1, 2, 3, 4), (2, 1, 4, 3)),
    "patch": ((1, 2, 3, 4), (2, 1, 4, 3)),
}
EARLY = ("late", "patch",)
VMEM = pltpu.VMEM
SMEM = pltpu.SMEM


def dot_plain(left_op, right_op):
    return jnp.dot(left_op, right_op, preferred_element_type=F32)


def dot_rows(left_op, right_op):
    return lax.dot_general(left_op, right_op, (((0,), (0,)), ((), ())), preferred_element_type=F32)


def dot_back(left_op, right_op):
    return lax.dot_general(left_op, right_op, (((1,), (1,)), ((), ())), preferred_element_type=F32)


def inverse_rms(values):
    return lax.rsqrt(jnp.mean(values * values, axis=-1, keepdims=True) + EPSILON)


def norm_backward(values, gain, grad):
    inverse = inverse_rms(values)
    unit = values * inverse
    scaled = grad * gain
    along = jnp.mean(scaled * unit, axis=-1, keepdims=True)
    return inverse * (scaled - unit * along), jnp.sum(grad * unit, axis=0, keepdims=True)


def lane_masks():
    lane = lax.broadcasted_iota(jnp.int32, (1, PAIR), 1)
    first = jnp.where(lane < HEAD_DIM, 1.0, 0.0)
    return first.astype(BF16), (1.0 - first).astype(BF16)


def stack_heads(values):
    first, second = lane_masks()
    return jnp.concatenate([values * first, values * second], axis=0)


def fold_heads(values):
    half = values.shape[0] // 2
    lane = lax.broadcasted_iota(jnp.int32, (half, PAIR), 1)
    return jnp.where(lane < HEAD_DIM, values[:half], values[half:])


def pair_forward(queries, key_rows, value_rows, allowed):
    keys = key_rows.shape[0]
    scores = dot_back(stack_heads(key_rows), queries).reshape(2, keys, queries.shape[0])
    if allowed is not None:
        scores = jnp.where(allowed, scores, -1000000000.0)
    expo = jnp.exp(scores - jnp.max(scores, axis=1, keepdims=True))
    chances = expo * (1.0 / jnp.sum(expo, axis=1, keepdims=True))
    chances = chances.reshape(2 * keys, queries.shape[0]).astype(BF16)
    return chances, dot_rows(chances, stack_heads(value_rows)).astype(BF16)


def pair_backward(queries, key_rows, value_rows, chances, grad_mixed):
    keys, count = key_rows.shape[0], queries.shape[0]
    wide = chances.astype(F32)
    grad_chances = dot_back(stack_heads(value_rows), grad_mixed)
    product = wide * grad_chances
    inner = jnp.sum(product.reshape(2, keys, count), axis=1, keepdims=True)
    spread = (wide.reshape(2, keys, count) * inner).reshape(2 * keys, count)
    grad_scores = (product - spread).astype(BF16)
    grad_values = fold_heads(dot_plain(chances, grad_mixed))
    grad_keys = fold_heads(dot_plain(grad_scores, queries))
    grad_queries = dot_rows(grad_scores, stack_heads(key_rows)) * 0.125
    return grad_queries.astype(BF16), grad_keys.astype(BF16), grad_values.astype(BF16)


def pair_lanes(index, offset=0):
    return pl.ds(offset + index * PAIR, PAIR)


def count_kernel(me_ref, len_ref, member_ref, count_ref, code_ref):
    me = me_ref[0]
    count = sum(len_ref[s] for s in range(len_ref.shape[0])).astype(F32)
    in_first = member_ref[me] == 1
    count_ref[0] = jnp.where(in_first, count, 0.0)
    count_ref[1] = jnp.where(in_first, 0.0, count)
    for name, place in PLACES.items():
        code_ref[place], code_ref[place + 1] = code_pair(me, AXES[name])


def weigh_kernel(me_ref, member_ref, mix_ref, *refs):
    me = me_ref[0]
    parts, (weight_ref, own_ref, other_ref) = refs[:-3], refs[-3:]
    count_one = sum(part[0] for part in parts)
    count_two = sum(part[1] for part in parts)
    total = count_one + count_two
    first = mix_ref[0] * total / count_one
    second = mix_ref[1] * total / count_two
    own = jnp.where(member_ref[me] == 1, first, second)
    other = jnp.where(member_ref[me ^ 1] == 1, first, second)
    weight_ref[0], weight_ref[1] = own, other
    own_ref[...] = jnp.full(own_ref.shape, own)
    other_ref[...] = jnp.full(other_ref.shape, other)


def add_to(ref, first, value):
    @pl.when(first)
    def fresh():
        ref[...] = value

    @pl.when(jnp.logical_not(first))
    def more():
        ref[...] += value


def gelu_parts(gate):
    slant = 0.7978845608028654
    square = gate * gate
    tanh = jnp.tanh(gate * (slant + (slant * 0.044715) * square))
    half = 0.5 + 0.5 * tanh
    slope = half + (0.5 * gate) * (1.0 - tanh * tanh) * (slant + (3.0 * slant * 0.044715) * square)
    return gate * half, slope


def forward_kernel(
    len_ref, code_ref,
    patch_ref, tok_ref, cot_ref,
    wp_ref, bias_ref, wck_ref, wcv_ref,
    g1_ref, wq_ref, wk_ref, wv_ref, wo_ref, g2_ref, wcq_ref, wco_ref, g3_ref, wg_ref, wu_ref, wd_ref,
    feat_ref, kv_ref, qkv_ref, pt_ref, o_ref, x1_ref, cq_ref, pc_ref, oc_ref,
    out_ref, dx2_ref, gain_ref, keep_ref, send_ref,
    join_kv, join_qkv, wcq, h3_all, de_all, hid_all, dgate_all, dup_all, acc_down, acc_gate, acc_up,
):
    step, steps = pl.program_id(0), pl.num_programs(0)

    @pl.when(step == 0)
    def join():
        join_kv[:, :INNER] = wck_ref[...]
        join_kv[:, INNER:] = wcv_ref[...]
        join_qkv[:, :INNER] = wq_ref[...] * 0.125
        join_qkv[:, INNER : 2 * INNER] = wk_ref[...]
        join_qkv[:, 2 * INNER :] = wv_ref[...]
        wcq[...] = wcq_ref[...] * 0.125

    seqs, _, _, maxlen = pt_ref.shape
    patches = pc_ref.shape[2] // 2
    feat = (dot_plain(patch_ref[...], wp_ref[...]) + bias_ref[...]).astype(BF16)
    feat_ref[...] = feat
    kv_ref[...] = dot_plain(feat, join_kv[...]).astype(BF16)
    x = tok_ref[...].astype(F32)
    h1 = (x * inverse_rms(x) * g1_ref[...]).astype(BF16)
    qkv_ref[...] = dot_plain(h1, join_qkv[...]).astype(BF16)
    key_at = lax.broadcasted_iota(jnp.int32, (1, maxlen, maxlen), 1)
    query_at = lax.broadcasted_iota(jnp.int32, (1, maxlen, maxlen), 2)
    for s in range(seqs):
        rows = pl.ds(s * maxlen, maxlen)
        allowed = (key_at <= query_at) & (key_at < len_ref[step * seqs + s])
        for p in range(PAIRS):
            pt_ref[s, p], o_ref[rows, pair_lanes(p)] = pair_forward(
                qkv_ref[rows, pair_lanes(p)],
                qkv_ref[rows, pair_lanes(p, INNER)],
                qkv_ref[rows, pair_lanes(p, 2 * INNER)],
                allowed,
            )
    x1 = x + dot_plain(o_ref[...], wo_ref[...])
    x1_ref[...] = x1
    h2 = (x1 * inverse_rms(x1) * g2_ref[...]).astype(BF16)
    cq_ref[...] = dot_plain(h2, wcq[...]).astype(BF16)
    for s in range(seqs):
        rows, wide = pl.ds(s * maxlen, maxlen), pl.ds(s * patches, patches)
        for p in range(PAIRS):
            pc_ref[s, p], oc_ref[rows, pair_lanes(p)] = pair_forward(
                cq_ref[rows, pair_lanes(p)],
                kv_ref[wide, pair_lanes(p)],
                kv_ref[wide, pair_lanes(p, INNER)],
                None,
            )
    x2 = x1_ref[...] + dot_plain(oc_ref[...], wco_ref[...])
    h3 = (x2 * inverse_rms(x2) * g3_ref[...]).astype(BF16)
    at = lax.broadcasted_iota(jnp.int32, (maxlen, 1), 0)
    keep = jnp.concatenate(
        [jnp.where(at < len_ref[step * seqs + s], 1.0, 0.0) for s in range(seqs)], axis=0
    )
    e = cot_ref[...].astype(F32) * keep
    de = e.astype(BF16)
    count = x2.shape[0]
    here = pl.ds(pl.multiple_of(step * count, count), count)
    h3_all[here, :] = h3
    de_all[here, :] = de
    span = wg_ref.shape[1]
    chunk = 256
    for c in range(span // chunk):
        cols = pl.ds(c * chunk, chunk)
        gate = dot_plain(h3, wg_ref[:, cols])
        up = dot_plain(h3, wu_ref[:, cols])
        grad = dot_back(de, wd_ref[cols, :])
        gelu, slope = gelu_parts(gate)
        hid = (gelu * up).astype(BF16)
        dgate = (grad * up * slope).astype(BF16)
        dup = (grad * gelu).astype(BF16)
        hid_all[here, cols] = hid
        dgate_all[here, cols] = dgate
        dup_all[here, cols] = dup

    out_ref[...] = (x2 + dot_plain(hid_all[here, :], wd_ref[...])).astype(BF16)
    dh3 = dot_back(dgate_all[here, :], wg_ref[...]) + dot_back(dup_all[here, :], wu_ref[...])
    dx, gain = norm_backward(x2, g3_ref[...], dh3)
    dx2_ref[...] = e + dx
    add_to(gain_ref, step == 0, gain)

    @pl.when(step == steps - 1)
    def finish():
        for c in range(span // chunk):
            cols = pl.ds(c * chunk, chunk)
            acc_down[cols, :] = dot_rows(hid_all[:, cols], de_all[...])
            acc_gate[:, cols] = dot_rows(h3_all[...], dgate_all[:, cols])
            acc_up[:, cols] = dot_rows(h3_all[...], dup_all[:, cols])
        items = [(acc_down, acc_down.shape, 0), (acc_gate, acc_gate.shape, 0), (acc_up, acc_up.shape, 0)]
        pack(items, code_ref, PLACES["late"], keep_ref, send_ref)


def cross_backward_kernel(
    code_ref, dx2_ref, cq_ref, pt_ref, kv_ref, x1_ref, oc_ref, feat_ref,
    g2_ref, wco_ref, wcq_ref, wck_ref, wcv_ref,
    dfeat_ref, dx1_ref, gain_ref, bias_ref, keep_ref, send_ref,
    joined, dcq_all, dkv_all, dc_all, h2_all, oc_all, feat_all, acc_out, acc_query, acc_kv,
):
    step, steps = pl.program_id(0), pl.num_programs(0)

    @pl.when(step == 0)
    def join():
        joined[:, :INNER] = wck_ref[...]
        joined[:, INNER:] = wcv_ref[...]

    seqs, _, both, maxlen = pt_ref.shape
    patches = both // 2
    count, wide_count = seqs * maxlen, seqs * patches
    here = pl.ds(pl.multiple_of(step * count, count), count)
    wide_here = pl.ds(pl.multiple_of(step * wide_count, wide_count), wide_count)
    dx2 = dx2_ref[...]
    dc = dx2.astype(BF16)
    dc_all[here, :] = dc
    oc_all[here, :] = oc_ref[...]
    feat_all[wide_here, :] = feat_ref[...]
    doc = dot_back(dc, wco_ref[...]).astype(BF16)
    for s in range(seqs):
        rows, wide = pl.ds(s * maxlen, maxlen), pl.ds(s * patches, patches)
        at = pl.ds(pl.multiple_of(step * count + s * maxlen, maxlen), maxlen)
        wide_at = pl.ds(pl.multiple_of(step * wide_count + s * patches, patches), patches)
        for p in range(PAIRS):
            keys, values = pair_lanes(p), pair_lanes(p, INNER)
            dcq_all[at, keys], dkv_all[wide_at, keys], dkv_all[wide_at, values] = pair_backward(
                cq_ref[rows, keys],
                kv_ref[wide, keys],
                kv_ref[wide, values],
                pt_ref[s, p],
                doc[s * maxlen : (s + 1) * maxlen, p * PAIR : (p + 1) * PAIR],
            )
    dfeat = dot_back(dkv_all[wide_here, :], joined[...]).astype(BF16)
    dfeat_ref[...] = dfeat
    dh2 = dot_back(dcq_all[here, :], wcq_ref[...])
    x1 = x1_ref[...]
    h2_all[here, :] = (x1 * inverse_rms(x1) * g2_ref[...]).astype(BF16)
    dx, gain = norm_backward(x1, g2_ref[...], dh2)
    dx1_ref[...] = dx2 + dx
    add_to(gain_ref, step == 0, gain)
    add_to(bias_ref, step == 0, jnp.sum(dfeat.astype(F32), axis=0, keepdims=True))

    @pl.when(step == steps - 1)
    def finish():
        acc_out[...] = dot_rows(oc_all[...], dc_all[...])
        acc_query[...] = dot_rows(h2_all[...], dcq_all[...])
        acc_kv[...] = dot_rows(feat_all[...], dkv_all[...])
        small = acc_query.shape
        items = [(acc_out, acc_out.shape, 0), (acc_query, small, 0)]
        items += [(acc_kv, small, 0), (acc_kv, small, INNER)]
        pack(items, code_ref, PLACES["cross"], keep_ref, send_ref)


def patch_weight_kernel(code_ref, patch_ref, dfeat_ref, keep_ref, send_ref, acc, turned):
    step, steps = pl.program_id(0), pl.num_programs(0)
    add_to(acc, step == 0, dot_rows(dfeat_ref[...], patch_ref[...]))

    @pl.when(step == steps - 1)
    def finish():
        turned[...] = acc[...].T
        pack([(turned, turned.shape, 0)], code_ref, PLACES["patch"], keep_ref, send_ref)


def patch_input_kernel(weight_ref, dfeat_ref, w_ref, *refs):
    refs[-1][...] = dot_back(dfeat_ref[...], w_ref[...]) * weight_ref[0]


def self_backward_kernel(
    code_ref, weight_ref, dx1_ref, qkv_ref, pt_ref, tok_ref, o_ref,
    g1_ref, wo_ref, wq_ref, wk_ref, wv_ref, gain_two_ref, gain_three_ref, bias_ref,
    dtok_ref, keep_ref, send_ref,
    joined, dqkv_all, da_all, h1_all, o_all, acc_out, acc_qkv, gain_one, gain_block,
):
    step, steps = pl.program_id(0), pl.num_programs(0)

    @pl.when(step == 0)
    def join():
        joined[:, :INNER] = wq_ref[...]
        joined[:, INNER : 2 * INNER] = wk_ref[...]
        joined[:, 2 * INNER :] = wv_ref[...]

    seqs, _, _, maxlen = pt_ref.shape
    count = seqs * maxlen
    here = pl.ds(pl.multiple_of(step * count, count), count)
    dx1 = dx1_ref[...]
    da = dx1.astype(BF16)
    da_all[here, :] = da
    o_all[here, :] = o_ref[...]
    do = dot_back(da, wo_ref[...]).astype(BF16)
    for s in range(seqs):
        rows = pl.ds(s * maxlen, maxlen)
        at = pl.ds(pl.multiple_of(step * count + s * maxlen, maxlen), maxlen)
        for p in range(PAIRS):
            lanes = [pair_lanes(p, k * INNER) for k in range(3)]
            dqkv_all[at, lanes[0]], dqkv_all[at, lanes[1]], dqkv_all[at, lanes[2]] = pair_backward(
                qkv_ref[rows, lanes[0]],
                qkv_ref[rows, lanes[1]],
                qkv_ref[rows, lanes[2]],
                pt_ref[s, p],
                do[s * maxlen : (s + 1) * maxlen, p * PAIR : (p + 1) * PAIR],
            )
    dh1 = dot_back(dqkv_all[here, :], joined[...])
    x = tok_ref[...].astype(F32)
    h1_all[here, :] = (x * inverse_rms(x) * g1_ref[...]).astype(BF16)
    dx, gain = norm_backward(x, g1_ref[...], dh1)
    dtok_ref[...] = (dx1 + dx) * weight_ref[0]
    add_to(gain_one, step == 0, gain)

    @pl.when(step == steps - 1)
    def finish():
        acc_out[...] = dot_rows(o_all[...], da_all[...])
        acc_qkv[...] = dot_rows(h1_all[...], dqkv_all[...])
        gain_block[...] = jnp.zeros_like(gain_block)
        for k, ref in enumerate((gain_one, gain_two_ref, gain_three_ref, bias_ref)):
            for t in range(4):
                gain_block[pl.ds((4 * k + t) * 8, 1), :] = ref[:, pl.ds(t * 128, 128)]
        small = (acc_qkv.shape[0], INNER)
        items = [(acc_out, acc_out.shape, 0)]
        items += [(acc_qkv, small, k * INNER) for k in range(3)]
        items += [(gain_block, gain_block.shape, 0)]
        pack(items, code_ref, PLACES["own"], keep_ref, send_ref)


def flips(count, first, second):
    return [(i, i ^ (first if i % 2 == 0 else second)) for i in range(count)]


def code_of(me, core, axes):
    code = core
    for axis in axes:
        code = code * 2 + ((me >> axis) & 1)
    return code


def code_pair(me, axes):
    core = me & 1
    even, odd = code_of(me, core, axes[0]), code_of(me, core, axes[1])
    own = jnp.where(core == 0, even, odd)
    other = jnp.where(core == 0, odd, even)
    return own, other ^ HALF


def exchange(values, first, second=None):
    count = lax.axis_size("dp")
    return lax.ppermute(values, "dp", flips(count, first, first if second is None else second))


def block_rows(shape):
    return shape[0] * shape[1] // (BLOCKS * 128)


def block_parts(shape, index, offset):
    rows, lanes = shape
    tiles = lanes // 128
    if BLOCKS % tiles:
        height = rows // BLOCKS
        return [
            (pl.ds(pl.multiple_of(index * height, 8), height), pl.ds(offset + t * 128, 128))
            for t in range(tiles)
        ]
    height = rows * tiles // BLOCKS
    row, lane = index // tiles, index % tiles
    return [
        (
            pl.ds(pl.multiple_of(row * height, 8), height),
            pl.ds(pl.multiple_of(offset + lane * 128, 128), 128),
        )
    ]


def pack(items, code_ref, place, keep_ref, send_ref):
    def step(p, carry):
        for code, out_ref in ((code_ref[place], keep_ref), (code_ref[place + 1], send_ref)):
            start = 0
            for ref, shape, offset in items:
                for rows, lanes in block_parts(shape, p ^ code, offset):
                    out_ref[p, pl.ds(start, rows.size), :] = ref[rows, lanes]
                    start += rows.size
        return carry

    lax.fori_loop(0, HALF, step, 0)


def unpack_kernel(shapes, with_gains, place, code_ref, *refs):
    ins, outs = refs[:4], refs[4:]
    for k, piece in enumerate(ins):

        def step(p, carry, piece=piece, k=k):
            index = (p + 8 * (k % 2)) ^ code_ref[place + k // 2]
            start = 0
            for shape, out_ref in zip(shapes, outs):
                for rows, lanes in block_parts(shape, index, 0):
                    out_ref[rows, lanes] = piece[p, pl.ds(start, rows.size), :]
                    start += rows.size
            return carry

        lax.fori_loop(0, 8, step, 0)
    if with_gains:
        count = len(shapes)
        block = outs[count - 1]
        for k, out_ref in enumerate(outs[count:]):
            for t in range(4):
                out_ref[:, pl.ds(t * 128, 128)] = block[pl.ds((4 * k + t) * 8, 1), :]


def vmem(count):
    return [pl.BlockSpec(memory_space=VMEM)] * count


def unpack(pieces, shapes, codes, place, with_gains=False):
    outs = [jax.ShapeDtypeStruct(s, F32) for s in shapes]
    if with_gains:
        outs += [jax.ShapeDtypeStruct((1, 512), F32)] * 4
    return pl.pallas_call(
        functools.partial(unpack_kernel, shapes, with_gains, place),
        out_shape=outs,
        in_specs=[pl.BlockSpec(memory_space=SMEM)] + vmem(4),
        out_specs=vmem(len(outs)),
        compiler_params=pltpu.CompilerParams(vmem_limit_bytes=40 * 2**20),
        name="unpack",
    )(codes, *pieces)


class Chunk:
    def __init__(self, name, packed, shapes, codes, weights=None, with_gains=False):
        self.held, self.got, self.stage = tuple(packed), (), 0
        self.name, self.shapes, self.codes = name, shapes, codes
        self.weights, self.with_gains = weights, with_gains

    def advance(self, token):
        (self.held, self.got), token = lax.optimization_barrier(((self.held, self.got), token))
        take, send, axis = STAGES[self.stage]
        self.stage += 1
        if take is not None:
            take(self)
        send(self, axis)
        return self.held[0]

    def land(self, token):
        self.got, token = lax.optimization_barrier((self.got, token))
        return token

    def over(self, values, axis):
        even, odd = AXES[self.name]
        return exchange(values, 1 << even[axis], 1 << odd[axis])

    def send_cores(self, axis):
        self.got = (exchange(self.held[1], 1),)

    def take_cores(self):
        (keep, _), (got,), (own, other) = self.held, self.got, self.weights
        self.held = (keep[8:] * own + got[8:] * other, keep)

    def send_first(self, axis):
        self.got += (self.over(self.held[0], axis),)

    def take_first(self):
        (_, keep), (low, got), (own, other) = self.held, self.got, self.weights
        keep = keep[:8] * own + low[:8] * other
        self.held = (keep[4:] + got[4:], keep[:4] + got[:4])

    def take_half(self):
        (_, keep), (got,) = self.held, self.got
        half = keep.shape[0] // 2
        self.held = (keep[half:] + got[half:], keep[:half] + got[:half])

    def take_last(self):
        total = self.held[1] + self.got[0]
        extra = BLOCKS
        while extra < lax.axis_size("dp"):
            total = total + exchange(total, extra)
            extra *= 2
        self.held = (total,)

    def take_back(self):
        self.held = (jnp.concatenate([*self.held, *self.got]),)

    def send(self, axis):
        self.got = (self.over(self.held[0], axis),)

    def send_back_first(self, axis):
        self.send(axis)
        if self.name in EARLY:
            self.got += (exchange(self.held[0], 1),)

    def send_back_cores(self, axis):
        rest = self.got[0]
        self.held += self.got
        self.got = (exchange(rest, 1),)
        if len(self.held) < 3:
            self.held += (exchange(self.held[0], 1),)

    def unpack(self, token):
        (held, got), token = lax.optimization_barrier(((self.held, self.got), token))
        return unpack(held + got, self.shapes, self.codes, PLACES[self.name], self.with_gains)


STAGES = (
    (None, Chunk.send_cores, 0),
    (Chunk.take_cores, Chunk.send_first, 0),
    (Chunk.take_first, Chunk.send, 1),
    (Chunk.take_half, Chunk.send, 2),
    (Chunk.take_half, Chunk.send, 3),
    (Chunk.take_last, Chunk.send, 3),
    (Chunk.take_back, Chunk.send, 2),
    (Chunk.take_back, Chunk.send, 1),
    (Chunk.take_back, Chunk.send_back_first, 0),
    (None, Chunk.send_back_cores, 0),
)


def by_step(array_shape, steps):
    block = (array_shape[0] // steps,) + tuple(array_shape[1:])
    return pl.BlockSpec(block, lambda i: (i,) + (0,) * (len(block) - 1))


def whole(array_shape):
    return pl.BlockSpec(tuple(array_shape), lambda i: (0,) * len(array_shape))


SCALARS = pl.BlockSpec(memory_space=SMEM)
IN_VMEM = pl.BlockSpec(memory_space=VMEM)


def run_small(kernel, name, operands, outs, ins=None):
    return pl.pallas_call(
        kernel,
        out_shape=[jax.ShapeDtypeStruct(s, d) for s, d, _ in outs],
        in_specs=ins or [SCALARS] * len(operands),
        out_specs=[spec for _, _, spec in outs],
        name=name,
    )(*operands)


def run(kernel, name, steps, scalars, stepped, fixed, order, outs, scratch, cost):
    lists = {"s": iter(scalars), "r": iter(stepped), "f": iter(fixed)}
    operands = [next(lists[c]) for c in order]
    in_specs = [
        SCALARS if c == "s" else by_step(v.shape, steps) if c == "r" else whole(v.shape)
        for c, v in zip(order, operands)
    ]
    return pl.pallas_call(
        kernel,
        grid=(steps,),
        out_shape=[jax.ShapeDtypeStruct(s, d) for s, d, _ in outs],
        in_specs=in_specs,
        out_specs=[
            SCALARS if moves is None else by_step(s, steps) if moves else IN_VMEM if name != "forward" else whole(s)
            for s, _, moves in outs
        ],
        scratch_shapes=[VMEM(s, d) for s, d in scratch],
        compiler_params=pltpu.CompilerParams(vmem_limit_bytes=(56 if name == "forward" else 44) * 2**20),
        cost_estimate=pl.CostEstimate(flops=int(cost * 1e9), bytes_accessed=2**20, transcendentals=0),
        name=name,
    )(*operands)


ORDER = (
    "late", "cross kernel", "late", "cross", "self kernel", "cross", "own", "late",
    "patch kernel", "own", "late", "patch", "cross", "input kernel", "late", "cross", "patch",
    "own", "late", "cross", "input kernel", "patch", "late", "own", "patch", "cross", "own",
    "cross", "late", "patch", "own", "cross", "patch", "own", "patch", "cross", "late", "own",
    "late", "patch", "cross", "own", "cross", "patch", "own", "own", "patch", "patch",
)


def local(
    tokens,
    cotangent,
    patches,
    lengths,
    group_member,
    mix,
    gain_one,
    w_query,
    w_key,
    w_value,
    w_out,
    gain_two,
    w_patch,
    bias_patch,
    w_cross_query,
    w_cross_key,
    w_cross_value,
    w_cross_out,
    gain_three,
    w_gate,
    w_up,
    w_down,
):
    seqs = lengths.shape[0]
    rows, width = tokens.shape
    maxlen = rows // seqs
    images, patch_dim = patches.shape[1], patches.shape[2]
    image_rows = seqs * images
    wide = w_gate.shape[1]
    steps = seqs // 2
    part = rows // steps
    flat = patches.reshape(image_rows, patch_dim)
    gain_one, gain_two, gain_three, bias_patch = (
        g.reshape(1, width) for g in (gain_one, gain_two, gain_three, bias_patch)
    )

    me_ref = lax.axis_index("dp")[None].astype(jnp.int32)
    in_vmem = pl.BlockSpec(memory_space=VMEM)
    counts, codes = run_small(
        count_kernel, "count", [me_ref, lengths, group_member],
        [((2,), F32, SCALARS), ((8,), jnp.int32, SCALARS)],
    )
    devices = lax.axis_size("dp")
    counts = counts + exchange(counts, 1)
    flat, counts = lax.optimization_barrier((flat, counts))
    column = [counts] + [exchange(counts, bit) for bit in (8, 16, 24)]
    late_shapes = [w_down.shape, w_gate.shape, w_up.shape]
    late_rows = sum(block_rows(s) for s in late_shapes)
    (
        feat, cross_kv, qkv, chances, mixed, x1, cross_q, cross_chances, cross_mixed, result, dx2, gain3, *late
    ) = run(
        forward_kernel, "forward", steps, [lengths, codes], [flat, tokens, cotangent],
        [
            w_patch, bias_patch, w_cross_key, w_cross_value,
            gain_one, w_query, w_key, w_value, w_out, gain_two, w_cross_query, w_cross_out,
            gain_three, w_gate, w_up, w_down,
        ],
        "ssrrr" + "f" * 16,
        [
            ((image_rows, width), BF16, True),
            ((image_rows, 2 * INNER), BF16, True),
            ((rows, 3 * INNER), BF16, True),
            ((seqs, PAIRS, 2 * maxlen, maxlen), BF16, True),
            ((rows, INNER), BF16, True),
            ((rows, width), F32, True),
            ((rows, INNER), BF16, True),
            ((seqs, PAIRS, 2 * images, maxlen), BF16, True),
            ((rows, INNER), BF16, True),
            ((rows, width), BF16, True),
            ((rows, width), F32, True),
            ((1, width), F32, False),
        ] + [((HALF, late_rows, 128), F32, False)] * 2,
        [
            ((width, 2 * INNER), BF16),
            ((width, 3 * INNER), BF16),
            ((width, INNER), BF16),
            ((rows, width), BF16),
            ((rows, width), BF16),
            ((rows, wide), BF16),
            ((rows, wide), BF16),
            ((rows, wide), BF16),
            (w_down.shape, F32),
            (w_gate.shape, F32),
            (w_up.shape, F32),
        ],
        40.0,
    )
    late, column = lax.optimization_barrier((late, column))
    late = Chunk("late", late, late_shapes, codes)
    token = late.advance(dx2)
    column, token = lax.optimization_barrier((column, token))
    counts = sum(column)
    bit = BLOCKS
    while bit < devices:
        counts = counts + exchange(counts, bit)
        bit *= 2
    parts = [counts] + [exchange(counts, bit) for bit in (2, 4, 6)]
    row = (1, 1, 128)
    weights, *rows_of_weights = run_small(
        weigh_kernel, "weigh", [me_ref, group_member, mix, *parts],
        [((2,), F32, SCALARS), (row, F32, in_vmem), (row, F32, in_vmem)],
    )
    late.weights = rows_of_weights
    token = weights

    def cross_backward(token):
        tied, token = lax.optimization_barrier((dx2, token))
        cross_shapes = [w_cross_out.shape, w_cross_query.shape, w_cross_key.shape, w_cross_value.shape]
        cross_rows = sum(block_rows(s) for s in cross_shapes)
        dfeat, dx1, gain2, dbias, *cross = run(
            cross_backward_kernel, "cross_backward", steps, [codes],
            [tied, cross_q, cross_chances, cross_kv, x1, cross_mixed, feat],
            [gain_two, w_cross_out, w_cross_query, w_cross_key, w_cross_value], "srrrrrrrfffff",
            [
                ((image_rows, width), BF16, True),
                ((rows, width), F32, True),
                ((1, width), F32, False),
                ((1, width), F32, False),
            ] + [((HALF, cross_rows, 128), F32, False)] * 2,
            [
                ((width, 2 * INNER), BF16),
                ((rows, INNER), BF16),
                ((image_rows, 2 * INNER), BF16),
                ((rows, width), BF16),
                ((rows, width), BF16),
                ((rows, INNER), BF16),
                ((image_rows, width), BF16),
                (w_cross_out.shape, F32),
                (w_cross_query.shape, F32),
                ((width, 2 * INNER), F32),
            ],
            20.0,
        )
        return (dfeat, dx1, gain2, dbias), Chunk("cross", cross, cross_shapes, codes, late.weights)

    def self_backward(token, dx1, gain2, dbias):
        tied, token = lax.optimization_barrier((dx1, token))
        own_shapes = [w_out.shape, w_query.shape, w_key.shape, w_value.shape, (BLOCKS * 8, 128)]
        own_rows = sum(block_rows(s) for s in own_shapes)
        grad_tokens, *own = run(
            self_backward_kernel, "self_backward", steps, [codes, weights],
            [tied, qkv, chances, tokens, mixed],
            [gain_one, w_out, w_query, w_key, w_value, gain2, gain3, dbias], "ssrrrrr" + "f" * 8,
            [((rows, width), F32, True)] + [((HALF, own_rows, 128), F32, False)] * 2,
            [
                ((width, 3 * INNER), BF16),
                ((rows, 3 * INNER), BF16),
                ((rows, width), BF16),
                ((rows, width), BF16),
                ((rows, INNER), BF16),
                (w_out.shape, F32),
                ((width, 3 * INNER), F32),
                ((1, width), F32),
                ((BLOCKS * 8, 128), F32),
            ],
            16.0,
        )
        return grad_tokens, Chunk("own", own, own_shapes, codes, late.weights, True)

    def patch_weight(token, dfeat):
        tied, token = lax.optimization_barrier((dfeat, token))
        patch_shapes = [w_patch.shape]
        patch_rows = block_rows(w_patch.shape)
        patch = run(
            patch_weight_kernel, "patch_weight", steps, [codes], [flat, tied], [], "srr",
            [((HALF, patch_rows, 128), F32, False)] * 2,
            [((width, patch_dim), F32), ((patch_dim, width), F32)], 12.0,
        )
        return Chunk("patch", patch, patch_shapes, codes, late.weights)

    def patch_input(token, dfeat, half, out):
        tied, token = lax.optimization_barrier((dfeat, token))
        return pl.pallas_call(
            patch_input_kernel,
            grid=(steps,),
            out_shape=jax.ShapeDtypeStruct((image_rows, patch_dim), F32),
            in_specs=[
                SCALARS,
                pl.BlockSpec((image_rows // (2 * steps), width), lambda i: (i + half * steps, 0)),
                whole(w_patch.shape),
            ]
            + [pl.BlockSpec(memory_space=pl.ANY)] * len(out),
            out_specs=pl.BlockSpec((image_rows // (2 * steps), patch_dim), lambda i: (i + half * steps, 0)),
            input_output_aliases={3: 0} if out else {},
            compiler_params=pltpu.CompilerParams(vmem_limit_bytes=32 * 2**20),
            cost_estimate=pl.CostEstimate(flops=6 * 10**9, bytes_accessed=2**20, transcendentals=0),
            name="patch_input",
        )(weights, tied, w_patch, *out)

    chunks, done, grad_patches = {"late": late}, {}, ()
    for name in ORDER:
        if name == "cross kernel":
            (dfeat, dx1, gain2, dbias), chunks["cross"] = cross_backward(token)
            token = dx1
        elif name == "self kernel":
            grad_tokens, chunks["own"] = self_backward(token, dx1, gain2, dbias)
            token = grad_tokens
        elif name == "patch kernel":
            chunks["patch"] = patch_weight(token, dfeat)
            token = chunks["patch"].held
        elif name == "input kernel":
            half = len(grad_patches)
            grad_patches = (patch_input(token, dfeat, half, grad_patches),)
            token = grad_patches
        elif name.endswith(" lands"):
            token = chunks[name[:-6]].land(token)
        elif chunks[name].stage < len(STAGES):
            token = chunks[name].advance(token)
        else:
            done[name] = chunks[name].unpack(token)
            token = done[name]
    (grad_patches,) = grad_patches
    late, cross, own, patch = (done[name] for name in ("late", "cross", "own", "patch"))
    gains = [g.reshape(width) for g in own[5:]]
    return (
        result,
        grad_tokens,
        grad_patches.reshape(seqs, images, patch_dim),
        gains[0],
        own[1],
        own[2],
        own[3],
        own[0],
        gains[1],
        patch[0],
        gains[3],
        cross[1],
        cross[2],
        cross[3],
        cross[0],
        gains[2],
        late[1],
        late[2],
        late[0],
    )


def solution(mesh):
    split = P("dp", None)
    images = P("dp", None, None)
    return jax.shard_map(
        local,
        mesh=mesh,
        in_specs=(split, split, images, P("dp")) + (P(),) * 18,
        out_specs=(split, split, images) + (P(),) * 16,
        check_vma=False,
    )
```

```python
import functools

import jax
import jax.numpy as jnp
from jax import lax
from jax.experimental import pallas as pl
from jax.experimental.pallas import tpu as pltpu
from jax.sharding import PartitionSpec as P

HEADS = 6
HEAD_DIM = 64
PAIRS = HEADS // 2
PAIR = 2 * HEAD_DIM
INNER = HEADS * HEAD_DIM
BLOCKS = 32
HALF = 16
EPSILON = 1e-06
F32 = jnp.float32
BF16 = jnp.bfloat16
PLACES = {"late": 0, "cross": 2, "own": 4, "patch": 6}
AXES = {
    "late": ((1, 2, 3, 4), (2, 1, 4, 3)),
    "cross": ((1, 2, 3, 4), (2, 1, 4, 3)),
    "own": ((1, 2, 3, 4), (2, 1, 4, 3)),
    "patch": ((1, 2, 3, 4), (2, 1, 4, 3)),
}
EARLY = ("late", "patch",)
VMEM = pltpu.VMEM
SMEM = pltpu.SMEM


def dot_plain(left_op, right_op):
    return jnp.dot(left_op, right_op, preferred_element_type=F32)


def dot_rows(left_op, right_op):
    return lax.dot_general(left_op, right_op, (((0,), (0,)), ((), ())), preferred_element_type=F32)


def dot_back(left_op, right_op):
    return lax.dot_general(left_op, right_op, (((1,), (1,)), ((), ())), preferred_element_type=F32)


def inverse_rms(values):
    return lax.rsqrt(jnp.mean(values * values, axis=-1, keepdims=True) + EPSILON)


def norm_backward(values, gain, grad):
    inverse = inverse_rms(values)
    unit = values * inverse
    scaled = grad * gain
    along = jnp.mean(scaled * unit, axis=-1, keepdims=True)
    return inverse * (scaled - unit * along), jnp.sum(grad * unit, axis=0, keepdims=True)


def lane_masks():
    lane = lax.broadcasted_iota(jnp.int32, (1, PAIR), 1)
    first = jnp.where(lane < HEAD_DIM, 1.0, 0.0)
    return first.astype(BF16), (1.0 - first).astype(BF16)


def stack_heads(values):
    first, second = lane_masks()
    return jnp.concatenate([values * first, values * second], axis=0)


def fold_heads(values):
    half = values.shape[0] // 2
    lane = lax.broadcasted_iota(jnp.int32, (half, PAIR), 1)
    return jnp.where(lane < HEAD_DIM, values[:half], values[half:])


def pair_forward(queries, key_rows, value_rows, allowed):
    keys = key_rows.shape[0]
    scores = dot_back(stack_heads(key_rows), queries).reshape(2, keys, queries.shape[0])
    if allowed is not None:
        scores = jnp.where(allowed, scores, -1000000000.0)
    expo = jnp.exp(scores - jnp.max(scores, axis=1, keepdims=True))
    chances = expo * (1.0 / jnp.sum(expo, axis=1, keepdims=True))
    chances = chances.reshape(2 * keys, queries.shape[0]).astype(BF16)
    return chances, dot_rows(chances, stack_heads(value_rows)).astype(BF16)


def pair_backward(queries, key_rows, value_rows, chances, grad_mixed):
    keys, count = key_rows.shape[0], queries.shape[0]
    wide = chances.astype(F32)
    grad_chances = dot_back(stack_heads(value_rows), grad_mixed)
    product = wide * grad_chances
    inner = jnp.sum(product.reshape(2, keys, count), axis=1, keepdims=True)
    spread = (wide.reshape(2, keys, count) * inner).reshape(2 * keys, count)
    grad_scores = (product - spread).astype(BF16)
    grad_values = fold_heads(dot_plain(chances, grad_mixed))
    grad_keys = fold_heads(dot_plain(grad_scores, queries))
    grad_queries = dot_rows(grad_scores, stack_heads(key_rows)) * 0.125
    return grad_queries.astype(BF16), grad_keys.astype(BF16), grad_values.astype(BF16)


def pair_lanes(index, offset=0):
    return pl.ds(offset + index * PAIR, PAIR)


def count_kernel(me_ref, len_ref, member_ref, count_ref, code_ref):
    me = me_ref[0]
    count = sum(len_ref[s] for s in range(len_ref.shape[0])).astype(F32)
    in_first = member_ref[me] == 1
    count_ref[0] = jnp.where(in_first, count, 0.0)
    count_ref[1] = jnp.where(in_first, 0.0, count)
    for name, place in PLACES.items():
        code_ref[place], code_ref[place + 1] = code_pair(me, AXES[name])


def weigh_kernel(me_ref, member_ref, mix_ref, *refs):
    me = me_ref[0]
    parts, (weight_ref, own_ref, other_ref) = refs[:-3], refs[-3:]
    count_one = sum(part[0] for part in parts)
    count_two = sum(part[1] for part in parts)
    total = count_one + count_two
    first = mix_ref[0] * total / count_one
    second = mix_ref[1] * total / count_two
    own = jnp.where(member_ref[me] == 1, first, second)
    other = jnp.where(member_ref[me ^ 1] == 1, first, second)
    weight_ref[0], weight_ref[1] = own, other
    own_ref[...] = jnp.full(own_ref.shape, own)
    other_ref[...] = jnp.full(other_ref.shape, other)


def add_to(ref, first, value):
    @pl.when(first)
    def fresh():
        ref[...] = value

    @pl.when(jnp.logical_not(first))
    def more():
        ref[...] += value


def gelu_parts(gate):
    slant = 0.7978845608028654
    square = gate * gate
    tanh = jnp.tanh(gate * (slant + (slant * 0.044715) * square))
    half = 0.5 + 0.5 * tanh
    slope = half + (0.5 * gate) * (1.0 - tanh * tanh) * (slant + (3.0 * slant * 0.044715) * square)
    return gate * half, slope


def forward_kernel(
    len_ref, code_ref,
    patch_ref, tok_ref, cot_ref,
    wp_ref, bias_ref, wck_ref, wcv_ref,
    g1_ref, wq_ref, wk_ref, wv_ref, wo_ref, g2_ref, wcq_ref, wco_ref, g3_ref, wg_ref, wu_ref, wd_ref,
    feat_ref, kv_ref, qkv_ref, pt_ref, o_ref, x1_ref, cq_ref, pc_ref, oc_ref,
    out_ref, dx2_ref, gain_ref, keep_ref, send_ref,
    join_kv, join_qkv, wcq, h3_all, de_all, hid_all, dgate_all, dup_all, acc_down, acc_gate, acc_up,
):
    step, steps = pl.program_id(0), pl.num_programs(0)

    @pl.when(step == 0)
    def join():
        join_kv[:, :INNER] = wck_ref[...]
        join_kv[:, INNER:] = wcv_ref[...]
        join_qkv[:, :INNER] = wq_ref[...] * 0.125
        join_qkv[:, INNER : 2 * INNER] = wk_ref[...]
        join_qkv[:, 2 * INNER :] = wv_ref[...]
        wcq[...] = wcq_ref[...] * 0.125

    seqs, _, _, maxlen = pt_ref.shape
    patches = pc_ref.shape[2] // 2
    feat = (dot_plain(patch_ref[...], wp_ref[...]) + bias_ref[...]).astype(BF16)
    feat_ref[...] = feat
    kv_ref[...] = dot_plain(feat, join_kv[...]).astype(BF16)
    x = tok_ref[...].astype(F32)
    h1 = (x * inverse_rms(x) * g1_ref[...]).astype(BF16)
    qkv_ref[...] = dot_plain(h1, join_qkv[...]).astype(BF16)
    key_at = lax.broadcasted_iota(jnp.int32, (1, maxlen, maxlen), 1)
    query_at = lax.broadcasted_iota(jnp.int32, (1, maxlen, maxlen), 2)
    for s in range(seqs):
        rows = pl.ds(s * maxlen, maxlen)
        allowed = (key_at <= query_at) & (key_at < len_ref[step * seqs + s])
        for p in range(PAIRS):
            pt_ref[s, p], o_ref[rows, pair_lanes(p)] = pair_forward(
                qkv_ref[rows, pair_lanes(p)],
                qkv_ref[rows, pair_lanes(p, INNER)],
                qkv_ref[rows, pair_lanes(p, 2 * INNER)],
                allowed,
            )
    x1 = x + dot_plain(o_ref[...], wo_ref[...])
    x1_ref[...] = x1
    h2 = (x1 * inverse_rms(x1) * g2_ref[...]).astype(BF16)
    cq_ref[...] = dot_plain(h2, wcq[...]).astype(BF16)
    for s in range(seqs):
        rows, wide = pl.ds(s * maxlen, maxlen), pl.ds(s * patches, patches)
        for p in range(PAIRS):
            pc_ref[s, p], oc_ref[rows, pair_lanes(p)] = pair_forward(
                cq_ref[rows, pair_lanes(p)],
                kv_ref[wide, pair_lanes(p)],
                kv_ref[wide, pair_lanes(p, INNER)],
                None,
            )
    x2 = x1_ref[...] + dot_plain(oc_ref[...], wco_ref[...])
    h3 = (x2 * inverse_rms(x2) * g3_ref[...]).astype(BF16)
    at = lax.broadcasted_iota(jnp.int32, (maxlen, 1), 0)
    keep = jnp.concatenate(
        [jnp.where(at < len_ref[step * seqs + s], 1.0, 0.0) for s in range(seqs)], axis=0
    )
    e = cot_ref[...].astype(F32) * keep
    de = e.astype(BF16)
    count = x2.shape[0]
    here = pl.ds(pl.multiple_of(step * count, count), count)
    h3_all[here, :] = h3
    de_all[here, :] = de
    span = wg_ref.shape[1]
    chunk = 256
    for c in range(span // chunk):
        cols = pl.ds(c * chunk, chunk)
        gate = dot_plain(h3, wg_ref[:, cols])
        up = dot_plain(h3, wu_ref[:, cols])
        grad = dot_back(de, wd_ref[cols, :])
        gelu, slope = gelu_parts(gate)
        hid = (gelu * up).astype(BF16)
        dgate = (grad * up * slope).astype(BF16)
        dup = (grad * gelu).astype(BF16)
        hid_all[here, cols] = hid
        dgate_all[here, cols] = dgate
        dup_all[here, cols] = dup

    out_ref[...] = (x2 + dot_plain(hid_all[here, :], wd_ref[...])).astype(BF16)
    dh3 = dot_back(dgate_all[here, :], wg_ref[...]) + dot_back(dup_all[here, :], wu_ref[...])
    dx, gain = norm_backward(x2, g3_ref[...], dh3)
    dx2_ref[...] = e + dx
    add_to(gain_ref, step == 0, gain)

    @pl.when(step == steps - 1)
    def finish():
        for c in range(span // chunk):
            cols = pl.ds(c * chunk, chunk)
            acc_down[cols, :] = dot_rows(hid_all[:, cols], de_all[...])
            acc_gate[:, cols] = dot_rows(h3_all[...], dgate_all[:, cols])
            acc_up[:, cols] = dot_rows(h3_all[...], dup_all[:, cols])
        items = [(acc_down, acc_down.shape, 0), (acc_gate, acc_gate.shape, 0), (acc_up, acc_up.shape, 0)]
        pack(items, code_ref, PLACES["late"], keep_ref, send_ref)


def cross_backward_kernel(
    code_ref, dx2_ref, cq_ref, pt_ref, kv_ref, x1_ref, oc_ref, feat_ref,
    g2_ref, wco_ref, wcq_ref, wck_ref, wcv_ref,
    dfeat_ref, dx1_ref, gain_ref, bias_ref, keep_ref, send_ref,
    joined, dcq_all, dkv_all, dc_all, h2_all, oc_all, feat_all, acc_out, acc_query, acc_kv,
):
    step, steps = pl.program_id(0), pl.num_programs(0)

    @pl.when(step == 0)
    def join():
        joined[:, :INNER] = wck_ref[...]
        joined[:, INNER:] = wcv_ref[...]

    seqs, _, both, maxlen = pt_ref.shape
    patches = both // 2
    count, wide_count = seqs * maxlen, seqs * patches
    here = pl.ds(pl.multiple_of(step * count, count), count)
    wide_here = pl.ds(pl.multiple_of(step * wide_count, wide_count), wide_count)
    dx2 = dx2_ref[...]
    dc = dx2.astype(BF16)
    dc_all[here, :] = dc
    oc_all[here, :] = oc_ref[...]
    feat_all[wide_here, :] = feat_ref[...]
    doc = dot_back(dc, wco_ref[...]).astype(BF16)
    for s in range(seqs):
        rows, wide = pl.ds(s * maxlen, maxlen), pl.ds(s * patches, patches)
        at = pl.ds(pl.multiple_of(step * count + s * maxlen, maxlen), maxlen)
        wide_at = pl.ds(pl.multiple_of(step * wide_count + s * patches, patches), patches)
        for p in range(PAIRS):
            keys, values = pair_lanes(p), pair_lanes(p, INNER)
            dcq_all[at, keys], dkv_all[wide_at, keys], dkv_all[wide_at, values] = pair_backward(
                cq_ref[rows, keys],
                kv_ref[wide, keys],
                kv_ref[wide, values],
                pt_ref[s, p],
                doc[s * maxlen : (s + 1) * maxlen, p * PAIR : (p + 1) * PAIR],
            )
    dfeat = dot_back(dkv_all[wide_here, :], joined[...]).astype(BF16)
    dfeat_ref[...] = dfeat
    dh2 = dot_back(dcq_all[here, :], wcq_ref[...])
    x1 = x1_ref[...]
    h2_all[here, :] = (x1 * inverse_rms(x1) * g2_ref[...]).astype(BF16)
    dx, gain = norm_backward(x1, g2_ref[...], dh2)
    dx1_ref[...] = dx2 + dx
    add_to(gain_ref, step == 0, gain)
    add_to(bias_ref, step == 0, jnp.sum(dfeat.astype(F32), axis=0, keepdims=True))

    @pl.when(step == steps - 1)
    def finish():
        acc_out[...] = dot_rows(oc_all[...], dc_all[...])
        acc_query[...] = dot_rows(h2_all[...], dcq_all[...])
        acc_kv[...] = dot_rows(feat_all[...], dkv_all[...])
        small = acc_query.shape
        items = [(acc_out, acc_out.shape, 0), (acc_query, small, 0)]
        items += [(acc_kv, small, 0), (acc_kv, small, INNER)]
        pack(items, code_ref, PLACES["cross"], keep_ref, send_ref)


def patch_weight_kernel(code_ref, patch_ref, dfeat_ref, keep_ref, send_ref, acc, turned):
    step, steps = pl.program_id(0), pl.num_programs(0)
    add_to(acc, step == 0, dot_rows(dfeat_ref[...], patch_ref[...]))

    @pl.when(step == steps - 1)
    def finish():
        turned[...] = acc[...].T
        pack([(turned, turned.shape, 0)], code_ref, PLACES["patch"], keep_ref, send_ref)


def patch_input_kernel(weight_ref, dfeat_ref, w_ref, *refs):
    refs[-1][...] = dot_back(dfeat_ref[...], w_ref[...]) * weight_ref[0]


def self_backward_kernel(
    code_ref, weight_ref, dx1_ref, qkv_ref, pt_ref, tok_ref, o_ref,
    g1_ref, wo_ref, wq_ref, wk_ref, wv_ref, gain_two_ref, gain_three_ref, bias_ref,
    dtok_ref, keep_ref, send_ref,
    joined, dqkv_all, da_all, h1_all, o_all, acc_out, acc_qkv, gain_one, gain_block,
):
    step, steps = pl.program_id(0), pl.num_programs(0)

    @pl.when(step == 0)
    def join():
        joined[:, :INNER] = wq_ref[...]
        joined[:, INNER : 2 * INNER] = wk_ref[...]
        joined[:, 2 * INNER :] = wv_ref[...]

    seqs, _, _, maxlen = pt_ref.shape
    count = seqs * maxlen
    here = pl.ds(pl.multiple_of(step * count, count), count)
    dx1 = dx1_ref[...]
    da = dx1.astype(BF16)
    da_all[here, :] = da
    o_all[here, :] = o_ref[...]
    do = dot_back(da, wo_ref[...]).astype(BF16)
    for s in range(seqs):
        rows = pl.ds(s * maxlen, maxlen)
        at = pl.ds(pl.multiple_of(step * count + s * maxlen, maxlen), maxlen)
        for p in range(PAIRS):
            lanes = [pair_lanes(p, k * INNER) for k in range(3)]
            dqkv_all[at, lanes[0]], dqkv_all[at, lanes[1]], dqkv_all[at, lanes[2]] = pair_backward(
                qkv_ref[rows, lanes[0]],
                qkv_ref[rows, lanes[1]],
                qkv_ref[rows, lanes[2]],
                pt_ref[s, p],
                do[s * maxlen : (s + 1) * maxlen, p * PAIR : (p + 1) * PAIR],
            )
    dh1 = dot_back(dqkv_all[here, :], joined[...])
    x = tok_ref[...].astype(F32)
    h1_all[here, :] = (x * inverse_rms(x) * g1_ref[...]).astype(BF16)
    dx, gain = norm_backward(x, g1_ref[...], dh1)
    dtok_ref[...] = (dx1 + dx) * weight_ref[0]
    add_to(gain_one, step == 0, gain)

    @pl.when(step == steps - 1)
    def finish():
        acc_out[...] = dot_rows(o_all[...], da_all[...])
        acc_qkv[...] = dot_rows(h1_all[...], dqkv_all[...])
        gain_block[...] = jnp.zeros_like(gain_block)
        for k, ref in enumerate((gain_one, gain_two_ref, gain_three_ref, bias_ref)):
            for t in range(4):
                gain_block[pl.ds((4 * k + t) * 8, 1), :] = ref[:, pl.ds(t * 128, 128)]
        small = (acc_qkv.shape[0], INNER)
        items = [(acc_out, acc_out.shape, 0)]
        items += [(acc_qkv, small, k * INNER) for k in range(3)]
        items += [(gain_block, gain_block.shape, 0)]
        pack(items, code_ref, PLACES["own"], keep_ref, send_ref)


def flips(count, first, second):
    return [(i, i ^ (first if i % 2 == 0 else second)) for i in range(count)]


def code_of(me, core, axes):
    code = core
    for axis in axes:
        code = code * 2 + ((me >> axis) & 1)
    return code


def code_pair(me, axes):
    core = me & 1
    even, odd = code_of(me, core, axes[0]), code_of(me, core, axes[1])
    own = jnp.where(core == 0, even, odd)
    other = jnp.where(core == 0, odd, even)
    return own, other ^ HALF


def exchange(values, first, second=None):
    count = lax.axis_size("dp")
    return lax.ppermute(values, "dp", flips(count, first, first if second is None else second))


def block_rows(shape):
    return shape[0] * shape[1] // (BLOCKS * 128)


def block_parts(shape, index, offset):
    rows, lanes = shape
    tiles = lanes // 128
    if BLOCKS % tiles:
        height = rows // BLOCKS
        return [
            (pl.ds(pl.multiple_of(index * height, 8), height), pl.ds(offset + t * 128, 128))
            for t in range(tiles)
        ]
    height = rows * tiles // BLOCKS
    row, lane = index // tiles, index % tiles
    return [
        (
            pl.ds(pl.multiple_of(row * height, 8), height),
            pl.ds(pl.multiple_of(offset + lane * 128, 128), 128),
        )
    ]


def pack(items, code_ref, place, keep_ref, send_ref):
    def step(p, carry):
        for code, out_ref in ((code_ref[place], keep_ref), (code_ref[place + 1], send_ref)):
            start = 0
            for ref, shape, offset in items:
                for rows, lanes in block_parts(shape, p ^ code, offset):
                    out_ref[p, pl.ds(start, rows.size), :] = ref[rows, lanes]
                    start += rows.size
        return carry

    lax.fori_loop(0, HALF, step, 0)


def unpack_kernel(shapes, with_gains, place, code_ref, *refs):
    ins, outs = refs[:4], refs[4:]
    for k, piece in enumerate(ins):

        def step(p, carry, piece=piece, k=k):
            index = (p + 8 * (k % 2)) ^ code_ref[place + k // 2]
            start = 0
            for shape, out_ref in zip(shapes, outs):
                for rows, lanes in block_parts(shape, index, 0):
                    out_ref[rows, lanes] = piece[p, pl.ds(start, rows.size), :]
                    start += rows.size
            return carry

        lax.fori_loop(0, 8, step, 0)
    if with_gains:
        count = len(shapes)
        block = outs[count - 1]
        for k, out_ref in enumerate(outs[count:]):
            for t in range(4):
                out_ref[:, pl.ds(t * 128, 128)] = block[pl.ds((4 * k + t) * 8, 1), :]


def vmem(count):
    return [pl.BlockSpec(memory_space=VMEM)] * count


def unpack(pieces, shapes, codes, place, with_gains=False):
    outs = [jax.ShapeDtypeStruct(s, F32) for s in shapes]
    if with_gains:
        outs += [jax.ShapeDtypeStruct((1, 512), F32)] * 4
    return pl.pallas_call(
        functools.partial(unpack_kernel, shapes, with_gains, place),
        out_shape=outs,
        in_specs=[pl.BlockSpec(memory_space=SMEM)] + vmem(4),
        out_specs=vmem(len(outs)),
        compiler_params=pltpu.CompilerParams(vmem_limit_bytes=40 * 2**20),
        name="unpack",
    )(codes, *pieces)


class Chunk:
    def __init__(self, name, packed, shapes, codes, weights=None, with_gains=False):
        self.held, self.got, self.stage = tuple(packed), (), 0
        self.name, self.shapes, self.codes = name, shapes, codes
        self.weights, self.with_gains = weights, with_gains

    def advance(self, token):
        (self.held, self.got), token = lax.optimization_barrier(((self.held, self.got), token))
        take, send, axis = STAGES[self.stage]
        self.stage += 1
        if take is not None:
            take(self)
        send(self, axis)
        return self.held[0]

    def land(self, token):
        self.got, token = lax.optimization_barrier((self.got, token))
        return token

    def over(self, values, axis):
        even, odd = AXES[self.name]
        return exchange(values, 1 << even[axis], 1 << odd[axis])

    def send_cores(self, axis):
        self.got = (exchange(self.held[1], 1),)

    def take_cores(self):
        (keep, _), (got,), (own, other) = self.held, self.got, self.weights
        self.held = (keep[8:] * own + got[8:] * other, keep)

    def send_first(self, axis):
        self.got += (self.over(self.held[0], axis),)

    def take_first(self):
        (_, keep), (low, got), (own, other) = self.held, self.got, self.weights
        keep = keep[:8] * own + low[:8] * other
        self.held = (keep[4:] + got[4:], keep[:4] + got[:4])

    def take_half(self):
        (_, keep), (got,) = self.held, self.got
        half = keep.shape[0] // 2
        self.held = (keep[half:] + got[half:], keep[:half] + got[:half])

    def take_last(self):
        total = self.held[1] + self.got[0]
        extra = BLOCKS
        while extra < lax.axis_size("dp"):
            total = total + exchange(total, extra)
            extra *= 2
        self.held = (total,)

    def take_back(self):
        self.held = (jnp.concatenate([*self.held, *self.got]),)

    def send(self, axis):
        self.got = (self.over(self.held[0], axis),)

    def send_back_first(self, axis):
        self.send(axis)
        if self.name in EARLY:
            self.got += (exchange(self.held[0], 1),)

    def send_back_cores(self, axis):
        rest = self.got[0]
        self.held += self.got
        self.got = (exchange(rest, 1),)
        if len(self.held) < 3:
            self.held += (exchange(self.held[0], 1),)

    def unpack(self, token):
        (held, got), token = lax.optimization_barrier(((self.held, self.got), token))
        return unpack(held + got, self.shapes, self.codes, PLACES[self.name], self.with_gains)


STAGES = (
    (None, Chunk.send_cores, 0),
    (Chunk.take_cores, Chunk.send_first, 0),
    (Chunk.take_first, Chunk.send, 1),
    (Chunk.take_half, Chunk.send, 2),
    (Chunk.take_half, Chunk.send, 3),
    (Chunk.take_last, Chunk.send, 3),
    (Chunk.take_back, Chunk.send, 2),
    (Chunk.take_back, Chunk.send, 1),
    (Chunk.take_back, Chunk.send_back_first, 0),
    (None, Chunk.send_back_cores, 0),
)


def by_step(array_shape, steps):
    block = (array_shape[0] // steps,) + tuple(array_shape[1:])
    return pl.BlockSpec(block, lambda i: (i,) + (0,) * (len(block) - 1))


def whole(array_shape):
    return pl.BlockSpec(tuple(array_shape), lambda i: (0,) * len(array_shape))


SCALARS = pl.BlockSpec(memory_space=SMEM)
IN_VMEM = pl.BlockSpec(memory_space=VMEM)


def run_small(kernel, name, operands, outs, ins=None):
    return pl.pallas_call(
        kernel,
        out_shape=[jax.ShapeDtypeStruct(s, d) for s, d, _ in outs],
        in_specs=ins or [SCALARS] * len(operands),
        out_specs=[spec for _, _, spec in outs],
        name=name,
    )(*operands)


def run(kernel, name, steps, scalars, stepped, fixed, order, outs, scratch, cost):
    lists = {"s": iter(scalars), "r": iter(stepped), "f": iter(fixed)}
    operands = [next(lists[c]) for c in order]
    in_specs = [
        SCALARS if c == "s" else by_step(v.shape, steps) if c == "r" else whole(v.shape)
        for c, v in zip(order, operands)
    ]
    return pl.pallas_call(
        kernel,
        grid=(steps,),
        out_shape=[jax.ShapeDtypeStruct(s, d) for s, d, _ in outs],
        in_specs=in_specs,
        out_specs=[
            SCALARS if moves is None else by_step(s, steps) if moves else IN_VMEM if name != "forward" else whole(s)
            for s, _, moves in outs
        ],
        scratch_shapes=[VMEM(s, d) for s, d in scratch],
        compiler_params=pltpu.CompilerParams(vmem_limit_bytes=(56 if name == "forward" else 44) * 2**20),
        cost_estimate=pl.CostEstimate(flops=int(cost * 1e9), bytes_accessed=2**20, transcendentals=0),
        name=name,
    )(*operands)


ORDER = (
    "late", "cross kernel", "late", "cross", "self kernel", "cross", "own", "late",
    "patch kernel", "own", "late", "patch", "cross", "input kernel", "late", "cross", "patch",
    "late", "cross", "own", "input kernel", "patch", "late", "own", "patch", "cross", "own",
    "late", "patch", "cross", "own", "cross", "patch", "own", "patch", "cross", "late", "own",
    "late", "patch", "cross", "own", "cross", "patch", "own", "own", "patch", "patch",
)


def local(
    tokens,
    cotangent,
    patches,
    lengths,
    group_member,
    mix,
    gain_one,
    w_query,
    w_key,
    w_value,
    w_out,
    gain_two,
    w_patch,
    bias_patch,
    w_cross_query,
    w_cross_key,
    w_cross_value,
    w_cross_out,
    gain_three,
    w_gate,
    w_up,
    w_down,
):
    seqs = lengths.shape[0]
    rows, width = tokens.shape
    maxlen = rows // seqs
    images, patch_dim = patches.shape[1], patches.shape[2]
    image_rows = seqs * images
    wide = w_gate.shape[1]
    steps = seqs // 2
    part = rows // steps
    flat = patches.reshape(image_rows, patch_dim)
    gain_one, gain_two, gain_three, bias_patch = (
        g.reshape(1, width) for g in (gain_one, gain_two, gain_three, bias_patch)
    )

    me_ref = lax.axis_index("dp")[None].astype(jnp.int32)
    in_vmem = pl.BlockSpec(memory_space=VMEM)
    counts, codes = run_small(
        count_kernel, "count", [me_ref, lengths, group_member],
        [((2,), F32, SCALARS), ((8,), jnp.int32, SCALARS)],
    )
    devices = lax.axis_size("dp")
    counts = counts + exchange(counts, 1)
    flat, counts = lax.optimization_barrier((flat, counts))
    column = [counts] + [exchange(counts, bit) for bit in (8, 16, 24)]
    late_shapes = [w_down.shape, w_gate.shape, w_up.shape]
    late_rows = sum(block_rows(s) for s in late_shapes)
    (
        feat, cross_kv, qkv, chances, mixed, x1, cross_q, cross_chances, cross_mixed, result, dx2, gain3, *late
    ) = run(
        forward_kernel, "forward", steps, [lengths, codes], [flat, tokens, cotangent],
        [
            w_patch, bias_patch, w_cross_key, w_cross_value,
            gain_one, w_query, w_key, w_value, w_out, gain_two, w_cross_query, w_cross_out,
            gain_three, w_gate, w_up, w_down,
        ],
        "ssrrr" + "f" * 16,
        [
            ((image_rows, width), BF16, True),
            ((image_rows, 2 * INNER), BF16, True),
            ((rows, 3 * INNER), BF16, True),
            ((seqs, PAIRS, 2 * maxlen, maxlen), BF16, True),
            ((rows, INNER), BF16, True),
            ((rows, width), F32, True),
            ((rows, INNER), BF16, True),
            ((seqs, PAIRS, 2 * images, maxlen), BF16, True),
            ((rows, INNER), BF16, True),
            ((rows, width), BF16, True),
            ((rows, width), F32, True),
            ((1, width), F32, False),
        ] + [((HALF, late_rows, 128), F32, False)] * 2,
        [
            ((width, 2 * INNER), BF16),
            ((width, 3 * INNER), BF16),
            ((width, INNER), BF16),
            ((rows, width), BF16),
            ((rows, width), BF16),
            ((rows, wide), BF16),
            ((rows, wide), BF16),
            ((rows, wide), BF16),
            (w_down.shape, F32),
            (w_gate.shape, F32),
            (w_up.shape, F32),
        ],
        40.0,
    )
    late, column = lax.optimization_barrier((late, column))
    late = Chunk("late", late, late_shapes, codes)
    token = late.advance(dx2)
    column, token = lax.optimization_barrier((column, token))
    counts = sum(column)
    bit = BLOCKS
    while bit < devices:
        counts = counts + exchange(counts, bit)
        bit *= 2
    parts = [counts] + [exchange(counts, bit) for bit in (2, 4, 6)]
    row = (1, 1, 128)
    weights, *rows_of_weights = run_small(
        weigh_kernel, "weigh", [me_ref, group_member, mix, *parts],
        [((2,), F32, SCALARS), (row, F32, in_vmem), (row, F32, in_vmem)],
    )
    late.weights = rows_of_weights
    token = weights

    def cross_backward(token):
        tied, token = lax.optimization_barrier((dx2, token))
        cross_shapes = [w_cross_out.shape, w_cross_query.shape, w_cross_key.shape, w_cross_value.shape]
        cross_rows = sum(block_rows(s) for s in cross_shapes)
        dfeat, dx1, gain2, dbias, *cross = run(
            cross_backward_kernel, "cross_backward", steps, [codes],
            [tied, cross_q, cross_chances, cross_kv, x1, cross_mixed, feat],
            [gain_two, w_cross_out, w_cross_query, w_cross_key, w_cross_value], "srrrrrrrfffff",
            [
                ((image_rows, width), BF16, True),
                ((rows, width), F32, True),
                ((1, width), F32, False),
                ((1, width), F32, False),
            ] + [((HALF, cross_rows, 128), F32, False)] * 2,
            [
                ((width, 2 * INNER), BF16),
                ((rows, INNER), BF16),
                ((image_rows, 2 * INNER), BF16),
                ((rows, width), BF16),
                ((rows, width), BF16),
                ((rows, INNER), BF16),
                ((image_rows, width), BF16),
                (w_cross_out.shape, F32),
                (w_cross_query.shape, F32),
                ((width, 2 * INNER), F32),
            ],
            20.0,
        )
        return (dfeat, dx1, gain2, dbias), Chunk("cross", cross, cross_shapes, codes, late.weights)

    def self_backward(token, dx1, gain2, dbias):
        tied, token = lax.optimization_barrier((dx1, token))
        own_shapes = [w_out.shape, w_query.shape, w_key.shape, w_value.shape, (BLOCKS * 8, 128)]
        own_rows = sum(block_rows(s) for s in own_shapes)
        grad_tokens, *own = run(
            self_backward_kernel, "self_backward", steps, [codes, weights],
            [tied, qkv, chances, tokens, mixed],
            [gain_one, w_out, w_query, w_key, w_value, gain2, gain3, dbias], "ssrrrrr" + "f" * 8,
            [((rows, width), F32, True)] + [((HALF, own_rows, 128), F32, False)] * 2,
            [
                ((width, 3 * INNER), BF16),
                ((rows, 3 * INNER), BF16),
                ((rows, width), BF16),
                ((rows, width), BF16),
                ((rows, INNER), BF16),
                (w_out.shape, F32),
                ((width, 3 * INNER), F32),
                ((1, width), F32),
                ((BLOCKS * 8, 128), F32),
            ],
            16.0,
        )
        return grad_tokens, Chunk("own", own, own_shapes, codes, late.weights, True)

    def patch_weight(token, dfeat):
        tied, token = lax.optimization_barrier((dfeat, token))
        patch_shapes = [w_patch.shape]
        patch_rows = block_rows(w_patch.shape)
        patch = run(
            patch_weight_kernel, "patch_weight", steps, [codes], [flat, tied], [], "srr",
            [((HALF, patch_rows, 128), F32, False)] * 2,
            [((width, patch_dim), F32), ((patch_dim, width), F32)], 12.0,
        )
        return Chunk("patch", patch, patch_shapes, codes, late.weights)

    def patch_input(token, dfeat, half, out):
        tied, token = lax.optimization_barrier((dfeat, token))
        return pl.pallas_call(
            patch_input_kernel,
            grid=(steps,),
            out_shape=jax.ShapeDtypeStruct((image_rows, patch_dim), F32),
            in_specs=[
                SCALARS,
                pl.BlockSpec((image_rows // (2 * steps), width), lambda i: (i + half * steps, 0)),
                whole(w_patch.shape),
            ]
            + [pl.BlockSpec(memory_space=pl.ANY)] * len(out),
            out_specs=pl.BlockSpec((image_rows // (2 * steps), patch_dim), lambda i: (i + half * steps, 0)),
            input_output_aliases={3: 0} if out else {},
            compiler_params=pltpu.CompilerParams(vmem_limit_bytes=32 * 2**20),
            cost_estimate=pl.CostEstimate(flops=6 * 10**9, bytes_accessed=2**20, transcendentals=0),
            name="patch_input",
        )(weights, tied, w_patch, *out)

    chunks, done, grad_patches = {"late": late}, {}, ()
    for name in ORDER:
        if name == "cross kernel":
            (dfeat, dx1, gain2, dbias), chunks["cross"] = cross_backward(token)
            token = dx1
        elif name == "self kernel":
            grad_tokens, chunks["own"] = self_backward(token, dx1, gain2, dbias)
            token = grad_tokens
        elif name == "patch kernel":
            chunks["patch"] = patch_weight(token, dfeat)
            token = chunks["patch"].held
        elif name == "input kernel":
            half = len(grad_patches)
            grad_patches = (patch_input(token, dfeat, half, grad_patches),)
            token = grad_patches
        elif name.endswith(" lands"):
            token = chunks[name[:-6]].land(token)
        elif chunks[name].stage < len(STAGES):
            token = chunks[name].advance(token)
        else:
            done[name] = chunks[name].unpack(token)
            token = done[name]
    (grad_patches,) = grad_patches
    late, cross, own, patch = (done[name] for name in ("late", "cross", "own", "patch"))
    gains = [g.reshape(width) for g in own[5:]]
    return (
        result,
        grad_tokens,
        grad_patches.reshape(seqs, images, patch_dim),
        gains[0],
        own[1],
        own[2],
        own[3],
        own[0],
        gains[1],
        patch[0],
        gains[3],
        cross[1],
        cross[2],
        cross[3],
        cross[0],
        gains[2],
        late[1],
        late[2],
        late[0],
    )


def solution(mesh):
    split = P("dp", None)
    images = P("dp", None, None)
    return jax.shard_map(
        local,
        mesh=mesh,
        in_specs=(split, split, images, P("dp")) + (P(),) * 18,
        out_specs=(split, split, images) + (P(),) * 16,
        check_vma=False,
    )
```

```python
import functools

import jax
import jax.numpy as jnp
from jax import lax
from jax.experimental import pallas as pl
from jax.experimental.pallas import tpu as pltpu
from jax.sharding import PartitionSpec as P

HEADS = 6
HEAD_DIM = 64
PAIRS = HEADS // 2
PAIR = 2 * HEAD_DIM
INNER = HEADS * HEAD_DIM
BLOCKS = 32
HALF = 16
EPSILON = 1e-06
F32 = jnp.float32
BF16 = jnp.bfloat16
PLACES = {"late": 0, "cross": 2, "own": 4, "patch": 6}
AXES = {
    "late": ((1, 2, 3, 4), (2, 1, 4, 3)),
    "cross": ((1, 2, 3, 4), (2, 1, 4, 3)),
    "own": ((1, 2, 3, 4), (2, 1, 4, 3)),
    "patch": ((1, 2, 3, 4), (2, 1, 4, 3)),
}
EARLY = ("late", "patch",)
VMEM = pltpu.VMEM
SMEM = pltpu.SMEM


def dot_plain(left_op, right_op):
    return jnp.dot(left_op, right_op, preferred_element_type=F32)


def dot_rows(left_op, right_op):
    return lax.dot_general(left_op, right_op, (((0,), (0,)), ((), ())), preferred_element_type=F32)


def dot_back(left_op, right_op):
    return lax.dot_general(left_op, right_op, (((1,), (1,)), ((), ())), preferred_element_type=F32)


def inverse_rms(values):
    return lax.rsqrt(jnp.mean(values * values, axis=-1, keepdims=True) + EPSILON)


def norm_backward(values, gain, grad):
    inverse = inverse_rms(values)
    unit = values * inverse
    scaled = grad * gain
    along = jnp.mean(scaled * unit, axis=-1, keepdims=True)
    return inverse * (scaled - unit * along), jnp.sum(grad * unit, axis=0, keepdims=True)


def lane_masks():
    lane = lax.broadcasted_iota(jnp.int32, (1, PAIR), 1)
    first = jnp.where(lane < HEAD_DIM, 1.0, 0.0)
    return first.astype(BF16), (1.0 - first).astype(BF16)


def stack_heads(values):
    first, second = lane_masks()
    return jnp.concatenate([values * first, values * second], axis=0)


def fold_heads(values):
    half = values.shape[0] // 2
    lane = lax.broadcasted_iota(jnp.int32, (half, PAIR), 1)
    return jnp.where(lane < HEAD_DIM, values[:half], values[half:])


def pair_forward(queries, key_rows, value_rows, allowed):
    keys = key_rows.shape[0]
    scores = dot_back(stack_heads(key_rows), queries).reshape(2, keys, queries.shape[0])
    if allowed is not None:
        scores = jnp.where(allowed, scores, -1000000000.0)
    expo = jnp.exp(scores - jnp.max(scores, axis=1, keepdims=True))
    chances = expo * (1.0 / jnp.sum(expo, axis=1, keepdims=True))
    chances = chances.reshape(2 * keys, queries.shape[0]).astype(BF16)
    return chances, dot_rows(chances, stack_heads(value_rows)).astype(BF16)


def pair_backward(queries, key_rows, value_rows, chances, grad_mixed):
    keys, count = key_rows.shape[0], queries.shape[0]
    wide = chances.astype(F32)
    grad_chances = dot_back(stack_heads(value_rows), grad_mixed)
    product = wide * grad_chances
    inner = jnp.sum(product.reshape(2, keys, count), axis=1, keepdims=True)
    spread = (wide.reshape(2, keys, count) * inner).reshape(2 * keys, count)
    grad_scores = (product - spread).astype(BF16)
    grad_values = fold_heads(dot_plain(chances, grad_mixed))
    grad_keys = fold_heads(dot_plain(grad_scores, queries))
    grad_queries = dot_rows(grad_scores, stack_heads(key_rows)) * 0.125
    return grad_queries.astype(BF16), grad_keys.astype(BF16), grad_values.astype(BF16)


def pair_lanes(index, offset=0):
    return pl.ds(offset + index * PAIR, PAIR)


def count_kernel(me_ref, len_ref, member_ref, count_ref, code_ref):
    me = me_ref[0]
    count = sum(len_ref[s] for s in range(len_ref.shape[0])).astype(F32)
    in_first = member_ref[me] == 1
    count_ref[0] = jnp.where(in_first, count, 0.0)
    count_ref[1] = jnp.where(in_first, 0.0, count)
    for name, place in PLACES.items():
        code_ref[place], code_ref[place + 1] = code_pair(me, AXES[name])


def weigh_kernel(me_ref, member_ref, mix_ref, *refs):
    me = me_ref[0]
    parts, (weight_ref, own_ref, other_ref) = refs[:-3], refs[-3:]
    count_one = sum(part[0] for part in parts)
    count_two = sum(part[1] for part in parts)
    total = count_one + count_two
    first = mix_ref[0] * total / count_one
    second = mix_ref[1] * total / count_two
    own = jnp.where(member_ref[me] == 1, first, second)
    other = jnp.where(member_ref[me ^ 1] == 1, first, second)
    weight_ref[0], weight_ref[1] = own, other
    own_ref[...] = jnp.full(own_ref.shape, own)
    other_ref[...] = jnp.full(other_ref.shape, other)


def add_to(ref, first, value):
    @pl.when(first)
    def fresh():
        ref[...] = value

    @pl.when(jnp.logical_not(first))
    def more():
        ref[...] += value


def gelu_parts(gate):
    slant = 0.7978845608028654
    square = gate * gate
    tanh = jnp.tanh(gate * (slant + (slant * 0.044715) * square))
    half = 0.5 + 0.5 * tanh
    slope = half + (0.5 * gate) * (1.0 - tanh * tanh) * (slant + (3.0 * slant * 0.044715) * square)
    return gate * half, slope


def forward_kernel(
    len_ref, code_ref,
    patch_ref, tok_ref, cot_ref,
    wp_ref, bias_ref, wck_ref, wcv_ref,
    g1_ref, wq_ref, wk_ref, wv_ref, wo_ref, g2_ref, wcq_ref, wco_ref, g3_ref, wg_ref, wu_ref, wd_ref,
    feat_ref, kv_ref, qkv_ref, pt_ref, o_ref, x1_ref, cq_ref, pc_ref, oc_ref,
    out_ref, dx2_ref, gain_ref, keep_ref, send_ref,
    join_kv, join_qkv, wcq, h3_all, de_all, hid_all, dgate_all, dup_all, acc_down, acc_gate, acc_up,
):
    step, steps = pl.program_id(0), pl.num_programs(0)

    @pl.when(step == 0)
    def join():
        join_kv[:, :INNER] = wck_ref[...]
        join_kv[:, INNER:] = wcv_ref[...]
        join_qkv[:, :INNER] = wq_ref[...] * 0.125
        join_qkv[:, INNER : 2 * INNER] = wk_ref[...]
        join_qkv[:, 2 * INNER :] = wv_ref[...]
        wcq[...] = wcq_ref[...] * 0.125

    seqs, _, _, maxlen = pt_ref.shape
    patches = pc_ref.shape[2] // 2
    feat = (dot_plain(patch_ref[...], wp_ref[...]) + bias_ref[...]).astype(BF16)
    feat_ref[...] = feat
    kv_ref[...] = dot_plain(feat, join_kv[...]).astype(BF16)
    x = tok_ref[...].astype(F32)
    h1 = (x * inverse_rms(x) * g1_ref[...]).astype(BF16)
    qkv_ref[...] = dot_plain(h1, join_qkv[...]).astype(BF16)
    key_at = lax.broadcasted_iota(jnp.int32, (1, maxlen, maxlen), 1)
    query_at = lax.broadcasted_iota(jnp.int32, (1, maxlen, maxlen), 2)
    for s in range(seqs):
        rows = pl.ds(s * maxlen, maxlen)
        allowed = (key_at <= query_at) & (key_at < len_ref[step * seqs + s])
        for p in range(PAIRS):
            pt_ref[s, p], o_ref[rows, pair_lanes(p)] = pair_forward(
                qkv_ref[rows, pair_lanes(p)],
                qkv_ref[rows, pair_lanes(p, INNER)],
                qkv_ref[rows, pair_lanes(p, 2 * INNER)],
                allowed,
            )
    x1 = x + dot_plain(o_ref[...], wo_ref[...])
    x1_ref[...] = x1
    h2 = (x1 * inverse_rms(x1) * g2_ref[...]).astype(BF16)
    cq_ref[...] = dot_plain(h2, wcq[...]).astype(BF16)
    for s in range(seqs):
        rows, wide = pl.ds(s * maxlen, maxlen), pl.ds(s * patches, patches)
        for p in range(PAIRS):
            pc_ref[s, p], oc_ref[rows, pair_lanes(p)] = pair_forward(
                cq_ref[rows, pair_lanes(p)],
                kv_ref[wide, pair_lanes(p)],
                kv_ref[wide, pair_lanes(p, INNER)],
                None,
            )
    x2 = x1_ref[...] + dot_plain(oc_ref[...], wco_ref[...])
    h3 = (x2 * inverse_rms(x2) * g3_ref[...]).astype(BF16)
    at = lax.broadcasted_iota(jnp.int32, (maxlen, 1), 0)
    keep = jnp.concatenate(
        [jnp.where(at < len_ref[step * seqs + s], 1.0, 0.0) for s in range(seqs)], axis=0
    )
    e = cot_ref[...].astype(F32) * keep
    de = e.astype(BF16)
    count = x2.shape[0]
    here = pl.ds(pl.multiple_of(step * count, count), count)
    h3_all[here, :] = h3
    de_all[here, :] = de
    span = wg_ref.shape[1]
    chunk = 256
    for c in range(span // chunk):
        cols = pl.ds(c * chunk, chunk)
        gate = dot_plain(h3, wg_ref[:, cols])
        up = dot_plain(h3, wu_ref[:, cols])
        grad = dot_back(de, wd_ref[cols, :])
        gelu, slope = gelu_parts(gate)
        hid = (gelu * up).astype(BF16)
        dgate = (grad * up * slope).astype(BF16)
        dup = (grad * gelu).astype(BF16)
        hid_all[here, cols] = hid
        dgate_all[here, cols] = dgate
        dup_all[here, cols] = dup

    out_ref[...] = (x2 + dot_plain(hid_all[here, :], wd_ref[...])).astype(BF16)
    dh3 = dot_back(dgate_all[here, :], wg_ref[...]) + dot_back(dup_all[here, :], wu_ref[...])
    dx, gain = norm_backward(x2, g3_ref[...], dh3)
    dx2_ref[...] = e + dx
    add_to(gain_ref, step == 0, gain)

    @pl.when(step == steps - 1)
    def finish():
        for c in range(span // chunk):
            cols = pl.ds(c * chunk, chunk)
            acc_down[cols, :] = dot_rows(hid_all[:, cols], de_all[...])
            acc_gate[:, cols] = dot_rows(h3_all[...], dgate_all[:, cols])
            acc_up[:, cols] = dot_rows(h3_all[...], dup_all[:, cols])
        items = [(acc_down, acc_down.shape, 0), (acc_gate, acc_gate.shape, 0), (acc_up, acc_up.shape, 0)]
        pack(items, code_ref, PLACES["late"], keep_ref, send_ref)


def cross_backward_kernel(
    code_ref, dx2_ref, cq_ref, pt_ref, kv_ref, x1_ref, oc_ref, feat_ref,
    g2_ref, wco_ref, wcq_ref, wck_ref, wcv_ref,
    dfeat_ref, dx1_ref, gain_ref, bias_ref, keep_ref, send_ref,
    joined, dcq_all, dkv_all, dc_all, h2_all, oc_all, feat_all, acc_out, acc_query, acc_kv,
):
    step, steps = pl.program_id(0), pl.num_programs(0)

    @pl.when(step == 0)
    def join():
        joined[:, :INNER] = wck_ref[...]
        joined[:, INNER:] = wcv_ref[...]

    seqs, _, both, maxlen = pt_ref.shape
    patches = both // 2
    count, wide_count = seqs * maxlen, seqs * patches
    here = pl.ds(pl.multiple_of(step * count, count), count)
    wide_here = pl.ds(pl.multiple_of(step * wide_count, wide_count), wide_count)
    dx2 = dx2_ref[...]
    dc = dx2.astype(BF16)
    dc_all[here, :] = dc
    oc_all[here, :] = oc_ref[...]
    feat_all[wide_here, :] = feat_ref[...]
    doc = dot_back(dc, wco_ref[...]).astype(BF16)
    for s in range(seqs):
        rows, wide = pl.ds(s * maxlen, maxlen), pl.ds(s * patches, patches)
        at = pl.ds(pl.multiple_of(step * count + s * maxlen, maxlen), maxlen)
        wide_at = pl.ds(pl.multiple_of(step * wide_count + s * patches, patches), patches)
        for p in range(PAIRS):
            keys, values = pair_lanes(p), pair_lanes(p, INNER)
            dcq_all[at, keys], dkv_all[wide_at, keys], dkv_all[wide_at, values] = pair_backward(
                cq_ref[rows, keys],
                kv_ref[wide, keys],
                kv_ref[wide, values],
                pt_ref[s, p],
                doc[s * maxlen : (s + 1) * maxlen, p * PAIR : (p + 1) * PAIR],
            )
    dfeat = dot_back(dkv_all[wide_here, :], joined[...]).astype(BF16)
    dfeat_ref[...] = dfeat
    dh2 = dot_back(dcq_all[here, :], wcq_ref[...])
    x1 = x1_ref[...]
    h2_all[here, :] = (x1 * inverse_rms(x1) * g2_ref[...]).astype(BF16)
    dx, gain = norm_backward(x1, g2_ref[...], dh2)
    dx1_ref[...] = dx2 + dx
    add_to(gain_ref, step == 0, gain)
    add_to(bias_ref, step == 0, jnp.sum(dfeat.astype(F32), axis=0, keepdims=True))

    @pl.when(step == steps - 1)
    def finish():
        acc_out[...] = dot_rows(oc_all[...], dc_all[...])
        acc_query[...] = dot_rows(h2_all[...], dcq_all[...])
        acc_kv[...] = dot_rows(feat_all[...], dkv_all[...])
        small = acc_query.shape
        items = [(acc_out, acc_out.shape, 0), (acc_query, small, 0)]
        items += [(acc_kv, small, 0), (acc_kv, small, INNER)]
        pack(items, code_ref, PLACES["cross"], keep_ref, send_ref)


def patch_weight_kernel(code_ref, patch_ref, dfeat_ref, keep_ref, send_ref, acc, turned):
    step, steps = pl.program_id(0), pl.num_programs(0)
    add_to(acc, step == 0, dot_rows(dfeat_ref[...], patch_ref[...]))

    @pl.when(step == steps - 1)
    def finish():
        turned[...] = acc[...].T
        pack([(turned, turned.shape, 0)], code_ref, PLACES["patch"], keep_ref, send_ref)


def patch_input_kernel(weight_ref, dfeat_ref, w_ref, *refs):
    refs[-1][...] = dot_back(dfeat_ref[...], w_ref[...]) * weight_ref[0]


def self_backward_kernel(
    code_ref, weight_ref, dx1_ref, qkv_ref, pt_ref, tok_ref, o_ref,
    g1_ref, wo_ref, wq_ref, wk_ref, wv_ref, gain_two_ref, gain_three_ref, bias_ref,
    dtok_ref, keep_ref, send_ref,
    joined, dqkv_all, da_all, h1_all, o_all, acc_out, acc_qkv, gain_one, gain_block,
):
    step, steps = pl.program_id(0), pl.num_programs(0)

    @pl.when(step == 0)
    def join():
        joined[:, :INNER] = wq_ref[...]
        joined[:, INNER : 2 * INNER] = wk_ref[...]
        joined[:, 2 * INNER :] = wv_ref[...]

    seqs, _, _, maxlen = pt_ref.shape
    count = seqs * maxlen
    here = pl.ds(pl.multiple_of(step * count, count), count)
    dx1 = dx1_ref[...]
    da = dx1.astype(BF16)
    da_all[here, :] = da
    o_all[here, :] = o_ref[...]
    do = dot_back(da, wo_ref[...]).astype(BF16)
    for s in range(seqs):
        rows = pl.ds(s * maxlen, maxlen)
        at = pl.ds(pl.multiple_of(step * count + s * maxlen, maxlen), maxlen)
        for p in range(PAIRS):
            lanes = [pair_lanes(p, k * INNER) for k in range(3)]
            dqkv_all[at, lanes[0]], dqkv_all[at, lanes[1]], dqkv_all[at, lanes[2]] = pair_backward(
                qkv_ref[rows, lanes[0]],
                qkv_ref[rows, lanes[1]],
                qkv_ref[rows, lanes[2]],
                pt_ref[s, p],
                do[s * maxlen : (s + 1) * maxlen, p * PAIR : (p + 1) * PAIR],
            )
    dh1 = dot_back(dqkv_all[here, :], joined[...])
    x = tok_ref[...].astype(F32)
    h1_all[here, :] = (x * inverse_rms(x) * g1_ref[...]).astype(BF16)
    dx, gain = norm_backward(x, g1_ref[...], dh1)
    dtok_ref[...] = (dx1 + dx) * weight_ref[0]
    add_to(gain_one, step == 0, gain)

    @pl.when(step == steps - 1)
    def finish():
        acc_out[...] = dot_rows(o_all[...], da_all[...])
        acc_qkv[...] = dot_rows(h1_all[...], dqkv_all[...])
        gain_block[...] = jnp.zeros_like(gain_block)
        for k, ref in enumerate((gain_one, gain_two_ref, gain_three_ref, bias_ref)):
            for t in range(4):
                gain_block[pl.ds((4 * k + t) * 8, 1), :] = ref[:, pl.ds(t * 128, 128)]
        small = (acc_qkv.shape[0], INNER)
        items = [(acc_out, acc_out.shape, 0)]
        items += [(acc_qkv, small, k * INNER) for k in range(3)]
        items += [(gain_block, gain_block.shape, 0)]
        pack(items, code_ref, PLACES["own"], keep_ref, send_ref)


def flips(count, first, second):
    return [(i, i ^ (first if i % 2 == 0 else second)) for i in range(count)]


def code_of(me, core, axes):
    code = core
    for axis in axes:
        code = code * 2 + ((me >> axis) & 1)
    return code


def code_pair(me, axes):
    core = me & 1
    even, odd = code_of(me, core, axes[0]), code_of(me, core, axes[1])
    own = jnp.where(core == 0, even, odd)
    other = jnp.where(core == 0, odd, even)
    return own, other ^ HALF


def exchange(values, first, second=None):
    count = lax.axis_size("dp")
    return lax.ppermute(values, "dp", flips(count, first, first if second is None else second))


def block_rows(shape):
    return shape[0] * shape[1] // (BLOCKS * 128)


def block_parts(shape, index, offset):
    rows, lanes = shape
    tiles = lanes // 128
    if BLOCKS % tiles:
        height = rows // BLOCKS
        return [
            (pl.ds(pl.multiple_of(index * height, 8), height), pl.ds(offset + t * 128, 128))
            for t in range(tiles)
        ]
    height = rows * tiles // BLOCKS
    row, lane = index // tiles, index % tiles
    return [
        (
            pl.ds(pl.multiple_of(row * height, 8), height),
            pl.ds(pl.multiple_of(offset + lane * 128, 128), 128),
        )
    ]


def pack(items, code_ref, place, keep_ref, send_ref):
    def step(p, carry):
        for code, out_ref in ((code_ref[place], keep_ref), (code_ref[place + 1], send_ref)):
            start = 0
            for ref, shape, offset in items:
                for rows, lanes in block_parts(shape, p ^ code, offset):
                    out_ref[p, pl.ds(start, rows.size), :] = ref[rows, lanes]
                    start += rows.size
        return carry

    lax.fori_loop(0, HALF, step, 0)


def unpack_kernel(shapes, with_gains, place, code_ref, *refs):
    ins, outs = refs[:4], refs[4:]
    for k, piece in enumerate(ins):

        def step(p, carry, piece=piece, k=k):
            index = (p + 8 * (k % 2)) ^ code_ref[place + k // 2]
            start = 0
            for shape, out_ref in zip(shapes, outs):
                for rows, lanes in block_parts(shape, index, 0):
                    out_ref[rows, lanes] = piece[p, pl.ds(start, rows.size), :]
                    start += rows.size
            return carry

        lax.fori_loop(0, 8, step, 0)
    if with_gains:
        count = len(shapes)
        block = outs[count - 1]
        for k, out_ref in enumerate(outs[count:]):
            for t in range(4):
                out_ref[:, pl.ds(t * 128, 128)] = block[pl.ds((4 * k + t) * 8, 1), :]


def vmem(count):
    return [pl.BlockSpec(memory_space=VMEM)] * count


def unpack(pieces, shapes, codes, place, with_gains=False):
    outs = [jax.ShapeDtypeStruct(s, F32) for s in shapes]
    if with_gains:
        outs += [jax.ShapeDtypeStruct((1, 512), F32)] * 4
    return pl.pallas_call(
        functools.partial(unpack_kernel, shapes, with_gains, place),
        out_shape=outs,
        in_specs=[pl.BlockSpec(memory_space=SMEM)] + vmem(4),
        out_specs=vmem(len(outs)),
        compiler_params=pltpu.CompilerParams(vmem_limit_bytes=40 * 2**20),
        name="unpack",
    )(codes, *pieces)


class Chunk:
    def __init__(self, name, packed, shapes, codes, weights=None, with_gains=False):
        self.held, self.got, self.stage = tuple(packed), (), 0
        self.name, self.shapes, self.codes = name, shapes, codes
        self.weights, self.with_gains = weights, with_gains

    def advance(self, token):
        (self.held, self.got), token = lax.optimization_barrier(((self.held, self.got), token))
        take, send, axis = STAGES[self.stage]
        self.stage += 1
        if take is not None:
            take(self)
        send(self, axis)
        return self.held[0]

    def land(self, token):
        self.got, token = lax.optimization_barrier((self.got, token))
        return token

    def over(self, values, axis):
        even, odd = AXES[self.name]
        return exchange(values, 1 << even[axis], 1 << odd[axis])

    def send_cores(self, axis):
        self.got = (exchange(self.held[1], 1),)

    def take_cores(self):
        (keep, _), (got,), (own, other) = self.held, self.got, self.weights
        self.held = (keep[8:] * own + got[8:] * other, keep)

    def send_first(self, axis):
        self.got += (self.over(self.held[0], axis),)

    def take_first(self):
        (_, keep), (low, got), (own, other) = self.held, self.got, self.weights
        keep = keep[:8] * own + low[:8] * other
        self.held = (keep[4:] + got[4:], keep[:4] + got[:4])

    def take_half(self):
        (_, keep), (got,) = self.held, self.got
        half = keep.shape[0] // 2
        self.held = (keep[half:] + got[half:], keep[:half] + got[:half])

    def take_last(self):
        total = self.held[1] + self.got[0]
        extra = BLOCKS
        while extra < lax.axis_size("dp"):
            total = total + exchange(total, extra)
            extra *= 2
        self.held = (total,)

    def take_back(self):
        self.held = (jnp.concatenate([*self.held, *self.got]),)

    def send(self, axis):
        self.got = (self.over(self.held[0], axis),)

    def send_back_first(self, axis):
        self.send(axis)
        if self.name in EARLY:
            self.got += (exchange(self.held[0], 1),)

    def send_back_cores(self, axis):
        rest = self.got[0]
        self.held += self.got
        self.got = (exchange(rest, 1),)
        if len(self.held) < 3:
            self.held += (exchange(self.held[0], 1),)

    def unpack(self, token):
        (held, got), token = lax.optimization_barrier(((self.held, self.got), token))
        return unpack(held + got, self.shapes, self.codes, PLACES[self.name], self.with_gains)


STAGES = (
    (None, Chunk.send_cores, 0),
    (Chunk.take_cores, Chunk.send_first, 0),
    (Chunk.take_first, Chunk.send, 1),
    (Chunk.take_half, Chunk.send, 2),
    (Chunk.take_half, Chunk.send, 3),
    (Chunk.take_last, Chunk.send, 3),
    (Chunk.take_back, Chunk.send, 2),
    (Chunk.take_back, Chunk.send, 1),
    (Chunk.take_back, Chunk.send_back_first, 0),
    (None, Chunk.send_back_cores, 0),
)


def by_step(array_shape, steps):
    block = (array_shape[0] // steps,) + tuple(array_shape[1:])
    return pl.BlockSpec(block, lambda i: (i,) + (0,) * (len(block) - 1))


def whole(array_shape):
    return pl.BlockSpec(tuple(array_shape), lambda i: (0,) * len(array_shape))


SCALARS = pl.BlockSpec(memory_space=SMEM)
IN_VMEM = pl.BlockSpec(memory_space=VMEM)


def run_small(kernel, name, operands, outs, ins=None):
    return pl.pallas_call(
        kernel,
        out_shape=[jax.ShapeDtypeStruct(s, d) for s, d, _ in outs],
        in_specs=ins or [SCALARS] * len(operands),
        out_specs=[spec for _, _, spec in outs],
        name=name,
    )(*operands)


def run(kernel, name, steps, scalars, stepped, fixed, order, outs, scratch, cost):
    lists = {"s": iter(scalars), "r": iter(stepped), "f": iter(fixed)}
    operands = [next(lists[c]) for c in order]
    in_specs = [
        SCALARS if c == "s" else by_step(v.shape, steps) if c == "r" else whole(v.shape)
        for c, v in zip(order, operands)
    ]
    return pl.pallas_call(
        kernel,
        grid=(steps,),
        out_shape=[jax.ShapeDtypeStruct(s, d) for s, d, _ in outs],
        in_specs=in_specs,
        out_specs=[
            SCALARS if moves is None else by_step(s, steps) if moves else IN_VMEM if name != "forward" else whole(s)
            for s, _, moves in outs
        ],
        scratch_shapes=[VMEM(s, d) for s, d in scratch],
        compiler_params=pltpu.CompilerParams(vmem_limit_bytes=(56 if name == "forward" else 44) * 2**20),
        cost_estimate=pl.CostEstimate(flops=int(cost * 1e9), bytes_accessed=2**20, transcendentals=0),
        name=name,
    )(*operands)


ORDER = (
    "late", "cross kernel", "late", "cross", "self kernel", "cross", "own", "late",
    "patch kernel", "own", "late", "patch", "cross", "input kernel", "late", "patch", "cross",
    "late", "cross", "own", "input kernel", "patch", "late", "own", "patch", "cross", "own",
    "late", "patch", "cross", "own", "cross", "patch", "own", "patch", "cross", "late", "own",
    "late", "patch", "cross", "own", "cross", "patch", "own", "own", "patch", "patch",
)


def local(
    tokens,
    cotangent,
    patches,
    lengths,
    group_member,
    mix,
    gain_one,
    w_query,
    w_key,
    w_value,
    w_out,
    gain_two,
    w_patch,
    bias_patch,
    w_cross_query,
    w_cross_key,
    w_cross_value,
    w_cross_out,
    gain_three,
    w_gate,
    w_up,
    w_down,
):
    seqs = lengths.shape[0]
    rows, width = tokens.shape
    maxlen = rows // seqs
    images, patch_dim = patches.shape[1], patches.shape[2]
    image_rows = seqs * images
    wide = w_gate.shape[1]
    steps = seqs // 2
    part = rows // steps
    flat = patches.reshape(image_rows, patch_dim)
    gain_one, gain_two, gain_three, bias_patch = (
        g.reshape(1, width) for g in (gain_one, gain_two, gain_three, bias_patch)
    )

    me_ref = lax.axis_index("dp")[None].astype(jnp.int32)
    in_vmem = pl.BlockSpec(memory_space=VMEM)
    counts, codes = run_small(
        count_kernel, "count", [me_ref, lengths, group_member],
        [((2,), F32, SCALARS), ((8,), jnp.int32, SCALARS)],
    )
    devices = lax.axis_size("dp")
    counts = counts + exchange(counts, 1)
    flat, counts = lax.optimization_barrier((flat, counts))
    column = [counts] + [exchange(counts, bit) for bit in (8, 16, 24)]
    late_shapes = [w_down.shape, w_gate.shape, w_up.shape]
    late_rows = sum(block_rows(s) for s in late_shapes)
    (
        feat, cross_kv, qkv, chances, mixed, x1, cross_q, cross_chances, cross_mixed, result, dx2, gain3, *late
    ) = run(
        forward_kernel, "forward", steps, [lengths, codes], [flat, tokens, cotangent],
        [
            w_patch, bias_patch, w_cross_key, w_cross_value,
            gain_one, w_query, w_key, w_value, w_out, gain_two, w_cross_query, w_cross_out,
            gain_three, w_gate, w_up, w_down,
        ],
        "ssrrr" + "f" * 16,
        [
            ((image_rows, width), BF16, True),
            ((image_rows, 2 * INNER), BF16, True),
            ((rows, 3 * INNER), BF16, True),
            ((seqs, PAIRS, 2 * maxlen, maxlen), BF16, True),
            ((rows, INNER), BF16, True),
            ((rows, width), F32, True),
            ((rows, INNER), BF16, True),
            ((seqs, PAIRS, 2 * images, maxlen), BF16, True),
            ((rows, INNER), BF16, True),
            ((rows, width), BF16, True),
            ((rows, width), F32, True),
            ((1, width), F32, False),
        ] + [((HALF, late_rows, 128), F32, False)] * 2,
        [
            ((width, 2 * INNER), BF16),
            ((width, 3 * INNER), BF16),
            ((width, INNER), BF16),
            ((rows, width), BF16),
            ((rows, width), BF16),
            ((rows, wide), BF16),
            ((rows, wide), BF16),
            ((rows, wide), BF16),
            (w_down.shape, F32),
            (w_gate.shape, F32),
            (w_up.shape, F32),
        ],
        40.0,
    )
    late, column = lax.optimization_barrier((late, column))
    late = Chunk("late", late, late_shapes, codes)
    token = late.advance(dx2)
    column, token = lax.optimization_barrier((column, token))
    counts = sum(column)
    bit = BLOCKS
    while bit < devices:
        counts = counts + exchange(counts, bit)
        bit *= 2
    parts = [counts] + [exchange(counts, bit) for bit in (2, 4, 6)]
    row = (1, 1, 128)
    weights, *rows_of_weights = run_small(
        weigh_kernel, "weigh", [me_ref, group_member, mix, *parts],
        [((2,), F32, SCALARS), (row, F32, in_vmem), (row, F32, in_vmem)],
    )
    late.weights = rows_of_weights
    token = weights

    def cross_backward(token):
        tied, token = lax.optimization_barrier((dx2, token))
        cross_shapes = [w_cross_out.shape, w_cross_query.shape, w_cross_key.shape, w_cross_value.shape]
        cross_rows = sum(block_rows(s) for s in cross_shapes)
        dfeat, dx1, gain2, dbias, *cross = run(
            cross_backward_kernel, "cross_backward", steps, [codes],
            [tied, cross_q, cross_chances, cross_kv, x1, cross_mixed, feat],
            [gain_two, w_cross_out, w_cross_query, w_cross_key, w_cross_value], "srrrrrrrfffff",
            [
                ((image_rows, width), BF16, True),
                ((rows, width), F32, True),
                ((1, width), F32, False),
                ((1, width), F32, False),
            ] + [((HALF, cross_rows, 128), F32, False)] * 2,
            [
                ((width, 2 * INNER), BF16),
                ((rows, INNER), BF16),
                ((image_rows, 2 * INNER), BF16),
                ((rows, width), BF16),
                ((rows, width), BF16),
                ((rows, INNER), BF16),
                ((image_rows, width), BF16),
                (w_cross_out.shape, F32),
                (w_cross_query.shape, F32),
                ((width, 2 * INNER), F32),
            ],
            20.0,
        )
        return (dfeat, dx1, gain2, dbias), Chunk("cross", cross, cross_shapes, codes, late.weights)

    def self_backward(token, dx1, gain2, dbias):
        tied, token = lax.optimization_barrier((dx1, token))
        own_shapes = [w_out.shape, w_query.shape, w_key.shape, w_value.shape, (BLOCKS * 8, 128)]
        own_rows = sum(block_rows(s) for s in own_shapes)
        grad_tokens, *own = run(
            self_backward_kernel, "self_backward", steps, [codes, weights],
            [tied, qkv, chances, tokens, mixed],
            [gain_one, w_out, w_query, w_key, w_value, gain2, gain3, dbias], "ssrrrrr" + "f" * 8,
            [((rows, width), F32, True)] + [((HALF, own_rows, 128), F32, False)] * 2,
            [
                ((width, 3 * INNER), BF16),
                ((rows, 3 * INNER), BF16),
                ((rows, width), BF16),
                ((rows, width), BF16),
                ((rows, INNER), BF16),
                (w_out.shape, F32),
                ((width, 3 * INNER), F32),
                ((1, width), F32),
                ((BLOCKS * 8, 128), F32),
            ],
            16.0,
        )
        return grad_tokens, Chunk("own", own, own_shapes, codes, late.weights, True)

    def patch_weight(token, dfeat):
        tied, token = lax.optimization_barrier((dfeat, token))
        patch_shapes = [w_patch.shape]
        patch_rows = block_rows(w_patch.shape)
        patch = run(
            patch_weight_kernel, "patch_weight", steps, [codes], [flat, tied], [], "srr",
            [((HALF, patch_rows, 128), F32, False)] * 2,
            [((width, patch_dim), F32), ((patch_dim, width), F32)], 12.0,
        )
        return Chunk("patch", patch, patch_shapes, codes, late.weights)

    def patch_input(token, dfeat, half, out):
        tied, token = lax.optimization_barrier((dfeat, token))
        return pl.pallas_call(
            patch_input_kernel,
            grid=(steps,),
            out_shape=jax.ShapeDtypeStruct((image_rows, patch_dim), F32),
            in_specs=[
                SCALARS,
                pl.BlockSpec((image_rows // (2 * steps), width), lambda i: (i + half * steps, 0)),
                whole(w_patch.shape),
            ]
            + [pl.BlockSpec(memory_space=pl.ANY)] * len(out),
            out_specs=pl.BlockSpec((image_rows // (2 * steps), patch_dim), lambda i: (i + half * steps, 0)),
            input_output_aliases={3: 0} if out else {},
            compiler_params=pltpu.CompilerParams(vmem_limit_bytes=32 * 2**20),
            cost_estimate=pl.CostEstimate(flops=6 * 10**9, bytes_accessed=2**20, transcendentals=0),
            name="patch_input",
        )(weights, tied, w_patch, *out)

    chunks, done, grad_patches = {"late": late}, {}, ()
    for name in ORDER:
        if name == "cross kernel":
            (dfeat, dx1, gain2, dbias), chunks["cross"] = cross_backward(token)
            token = dx1
        elif name == "self kernel":
            grad_tokens, chunks["own"] = self_backward(token, dx1, gain2, dbias)
            token = grad_tokens
        elif name == "patch kernel":
            chunks["patch"] = patch_weight(token, dfeat)
            token = chunks["patch"].held
        elif name == "input kernel":
            half = len(grad_patches)
            grad_patches = (patch_input(token, dfeat, half, grad_patches),)
            token = grad_patches
        elif name.endswith(" lands"):
            token = chunks[name[:-6]].land(token)
        elif chunks[name].stage < len(STAGES):
            token = chunks[name].advance(token)
        else:
            done[name] = chunks[name].unpack(token)
            token = done[name]
    (grad_patches,) = grad_patches
    late, cross, own, patch = (done[name] for name in ("late", "cross", "own", "patch"))
    gains = [g.reshape(width) for g in own[5:]]
    return (
        result,
        grad_tokens,
        grad_patches.reshape(seqs, images, patch_dim),
        gains[0],
        own[1],
        own[2],
        own[3],
        own[0],
        gains[1],
        patch[0],
        gains[3],
        cross[1],
        cross[2],
        cross[3],
        cross[0],
        gains[2],
        late[1],
        late[2],
        late[0],
    )


def solution(mesh):
    split = P("dp", None)
    images = P("dp", None, None)
    return jax.shard_map(
        local,
        mesh=mesh,
        in_specs=(split, split, images, P("dp")) + (P(),) * 18,
        out_specs=(split, split, images) + (P(),) * 16,
        check_vma=False,
    )
```
